32 devices in a mesh: pool: 8 (over z, y), blk: 4 (over x, core).
Axes of the slice: x: 2, y: 2, z: 4, core: 2. Of those that a mesh axis runs over, the one named last changes fastest.
Arguments:
- queries: bfloat16 [4096, 4096], P(('pool', 'blk')), may hold values from -7.5 to 7.5
- span_kv: bfloat16 [4096, 1024], P(('pool', 'blk')), may hold values from -6 to 6
- kv_store: bfloat16 [128, 64, 1024], P('pool'), may hold values from -6 to 6
- page_ids: int32 [8, 8], P('pool'), may hold values from 0 to 15
- page_owner: int32 [8, 8], P('pool'), may hold values from 0 to 7, as said below
- prefix_len: int32 [8], P('pool'), may hold values from 320 to 512, as said below
Outputs:
- attended: bfloat16 [4096, 4096], P(('pool', 'blk'))
The draws below stay inside these ranges and needn't reach their ends.
Inputs may be any that keep to these rules, and one draw needn't show every extreme that they name: `page_owner`: each request's list names 4 owners, each exactly 2 times; one owner is named by every request. `prefix_len`: some request has a prefix of exactly 512 tokens.
All inputs are finite; a program needn't handle non-finite values.
Results may differ from the reference program's by a relative error of at most 0.005.
Values may be sent and summed in bfloat16 or wider, within the bound.
No kernel may reach another device: no remote copies, remote signals or barrier semaphores. Data moves between devices by JAX's collectives and lax.ppermute only.
A program may use at most 128 MiB of HBM per device.

```python
import math
import jax
import jax.numpy as jnp
from jax import lax

QH = 32
KVH = 4
DH = 128
PAGE = 64
CAP = 2
QB = 128
PAGES_DEV = 16
GROUP = 8
F = 1024
PAGES_REQ = 8
PREFIX = 512
SPAN = 512
TOKENS = 4096
N_POOL = 8
N_BLK = 4


def draw_span_kv(key, part):
    key = jax.random.fold_in(key, 11)
    first = jax.random.fold_in(key, 0)
    pairs = jnp.clip(jax.random.normal(first, (TOKENS, 2, KVH, DH), jnp.float32), -6.0, 6.0)
    return pairs.reshape(TOKENS, 2 * KVH * DH).astype(jnp.bfloat16)


def draw_queries(key, part):
    key = jax.random.fold_in(key, 12)
    base = jnp.clip(2.5 * jax.random.normal(key, (TOKENS, KVH, GROUP, DH), jnp.float32), -7.5, 7.5)
    return base.reshape(TOKENS, QH * DH).astype(jnp.bfloat16)


def draw_page_owner(key, part):
    key = jax.random.fold_in(key, 13)
    hot_key, rest = jax.random.split(key)
    hottest = jax.random.randint(hot_key, (), 0, N_POOL)
    request_keys = jax.random.split(rest, N_POOL)
    half = N_POOL // 2

    def one_list(inner):
        pick_key, order_key = jax.random.split(inner)
        others = 1 + jax.random.permutation(pick_key, N_POOL - 1)[:half - 1]
        chosen = (hottest + jnp.concatenate([jnp.zeros((1,), jnp.int32), others.astype(jnp.int32)])) % N_POOL
        listed = jnp.tile(chosen, CAP)
        return listed[jax.random.permutation(order_key, PAGES_REQ)]
    return jax.vmap(one_list)(request_keys).astype(jnp.int32)


def draw_prefix_len(key, part):
    key = jax.random.fold_in(key, 14)
    first, second = jax.random.split(key)
    lengths = jax.random.randint(first, (N_POOL,), 5 * PREFIX // 8, PREFIX + 1)
    longest = jax.random.randint(second, (), 0, N_POOL)
    return jnp.where(jnp.arange(N_POOL) == longest, PREFIX, lengths).astype(jnp.int32)


def set_ends(entries, stream_key, low, largest):
    shape = entries.shape
    index_at = [jax.random.randint(jax.random.fold_in(stream_key, axis), (), 0, shape[axis]) for axis in range(len(shape))]
    entries = entries.at[tuple(index_at)].set(low)
    longest = shape.index(max(shape))
    index_at[longest] = (index_at[longest] + 1) % shape[longest]
    return entries.at[tuple(index_at)].set(largest)


def block_levels(key, extent, shards, low, top_value):
    level, own = 1.0, jax.random.fold_in(key, 6)
    for position, shards_of in shards:
        heights = jnp.exp(jax.random.uniform(jax.random.fold_in(own, position), (shards_of,), jnp.float32, low / len(shards), top_value / len(shards)))
        level = level * jnp.repeat(heights, extent[position] // shards_of).reshape([-1 if axis == position else 1 for axis in range(len(extent))])
    return level


def centred(stream_key, extent, deviation, most, cuts=(), kind=jnp.bfloat16):
    level = block_levels(stream_key, extent, cuts, -0.22, 0.18) if cuts else 1.0
    values = jax.random.normal(stream_key, extent, jnp.float32) * deviation * level
    return jnp.minimum(jnp.maximum(values, -most), most).astype(kind)


def setup_inputs(seed: int = 0) -> dict:
    seeds = jax.random.split(jax.random.key(seed), 7)
    return {
        "queries": draw_queries(jax.random.fold_in(seeds[6], 71), 0),
        "span_kv": draw_span_kv(jax.random.fold_in(seeds[6], 71), 0),
        "kv_store": centred(seeds[2], (N_POOL * PAGES_DEV, PAGE, F), 1.0, 6.0, ((0, 8),)),
        "page_ids": set_ends(jax.random.randint(seeds[3], (N_POOL, PAGES_REQ), 0, PAGES_DEV), jax.random.fold_in(seeds[3], 1), 0, PAGES_DEV - 1).astype(jnp.int32),
        "page_owner": draw_page_owner(jax.random.fold_in(seeds[6], 71), 0),
        "prefix_len": draw_prefix_len(jax.random.fold_in(seeds[6], 71), 0),
    }


def reference(queries, span_kv, kv_store, page_ids, page_owner, prefix_len):
    scale = 1.0 / math.sqrt(DH)

    def one_request(packed):
        req_q, req_kv, ident, owners, limit = packed
        rows_at = (owners * PAGES_DEV + ident).astype(jnp.int32)
        prefix = kv_store[rows_at].reshape(PREFIX, F)
        prefix_ok = jnp.arange(PREFIX) < limit
        every = jnp.concatenate([prefix, req_kv], 0)
        pairs = every.reshape(-1, 2, KVH, DH).astype(jnp.float32)
        key_rows = pairs[:, 0]
        val_rows = pairs[:, 1]

        def one_block(block):
            block_q, base = block
            q_four = block_q.reshape(QB, KVH, GROUP, DH).astype(jnp.float32)
            scores = jnp.einsum('qgjd,ngd->qgjn', q_four, key_rows, precision=lax.Precision.HIGHEST) * scale
            query_pos = base + jnp.arange(QB)
            span_ok = jnp.arange(SPAN)[None, :] <= query_pos[:, None]
            allowed = jnp.concatenate([jnp.broadcast_to(prefix_ok[None, :], (QB, PREFIX)), span_ok], 1)[:, None, None, :]
            row_top = lax.optimization_barrier(jnp.max(jnp.where(allowed, scores, -1e+30), axis=-1))
            weights = jnp.where(allowed, jnp.exp(scores - row_top[..., None]), 0.0)
            denom = lax.optimization_barrier(jnp.sum(weights, axis=-1))
            rounded = lax.optimization_barrier(weights.astype(jnp.bfloat16))
            numer = jnp.einsum('qgjn,ngd->qgjd', rounded.astype(jnp.float32), val_rows, precision=lax.Precision.HIGHEST)
            return (numer / denom[..., None]).astype(jnp.bfloat16).reshape(QB, QH * DH)
        starts = (jnp.arange(N_BLK) * QB).astype(jnp.int32)
        outputs = lax.map(one_block, (req_q.reshape(N_BLK, QB, QH * DH), starts))
        return outputs.reshape(SPAN, QH * DH)
    result = lax.map(one_request, (queries.reshape(N_POOL, SPAN, QH * DH), span_kv.reshape(N_POOL, SPAN, F), page_ids, page_owner, prefix_len))
    return result.reshape(TOKENS, QH * DH)
```

```python
import functools
import math

import jax
import jax.numpy as jnp
from jax import lax
from jax.experimental import pallas as pl
from jax.experimental.pallas import tpu as pltpu
from jax.sharding import PartitionSpec as P

KVH = 4
DH = 128
GROUP = 8
CAP = 2
COEF = math.log2(math.e) / math.sqrt(DH)
LOW = -1e30
ROWS = 256


def pick_kernel(pools, listed, place_ref, *refs):
    tables = refs[:pools]
    keys_ref, values_ref, out_ref = refs[pools:]
    own = place_ref[0]
    stored = keys_ref.shape[0]
    for shift in range(pools):
        table = tables[shift]
        request = lax.rem(own + shift, pools)

        def visit(entry, rank):
            code = table[entry]
            hit = lax.div(code, stored) == own

            @pl.when(hit)
            def _():
                page = lax.rem(code, stored)
                slot = jnp.minimum(rank, CAP - 1)
                out_ref[request, slot, :, :DH] = keys_ref[page]
                out_ref[request, slot, :, DH:] = values_ref[page]

            return rank + hit.astype(jnp.int32)

        lax.fori_loop(0, listed, visit, jnp.int32(0))


def pick_pages(place, tables, kv_store, pools, rows):
    stored = kv_store.shape[0]
    listed = tables[0].shape[0]
    block = (stored, rows, DH)
    spec = pltpu.PrefetchScalarGridSpec(
        num_scalar_prefetch=1 + pools,
        grid=(1,),
        in_specs=[
            pl.BlockSpec(block, lambda i, place, *_: (0, place[3], place[2])),
            pl.BlockSpec(block, lambda i, place, *_: (0, place[3], KVH + place[2])),
        ],
        out_specs=pl.BlockSpec((pools, CAP, rows, 2 * DH), lambda i, *_: (0, 0, 0, 0)),
    )
    return pl.pallas_call(
        functools.partial(pick_kernel, pools, listed),
        grid_spec=spec,
        out_shape=jax.ShapeDtypeStruct((pools, CAP, rows, 2 * DH), kv_store.dtype),
        name="pick_pages",
    )(place, *tables, kv_store, kv_store)


def order_kernel(listed, stored, table_ref, fetched_ref, out_ref, sems):
    copies = []
    for entry in range(listed):
        owner = lax.div(table_ref[entry], stored)
        rank = jnp.int32(0)
        for earlier in range(entry):
            rank += (lax.div(table_ref[earlier], stored) == owner).astype(jnp.int32)
        rank = jnp.minimum(rank, CAP - 1)
        copies.append(
            pltpu.make_async_copy(fetched_ref.at[owner, rank], out_ref.at[entry], sems.at[entry])
        )
        copies[-1].start()
    for copy in copies:
        copy.wait()


def order_pages(table, fetched, stored):
    listed = table.shape[0]
    rows = fetched.shape[2]
    return pl.pallas_call(
        functools.partial(order_kernel, listed, stored),
        in_specs=[pl.BlockSpec(memory_space=pltpu.SMEM), pl.BlockSpec(memory_space=pl.ANY)],
        out_specs=pl.BlockSpec(memory_space=pl.ANY),
        scratch_shapes=[pltpu.SemaphoreType.DMA((listed,))],
        out_shape=jax.ShapeDtypeStruct((listed, rows, 2 * DH), fetched.dtype),
        name="order_pages",
    )(table, fetched)


def scores_of(query_ref, first, count, keys):
    heads = [query_ref[:, (first + j) * DH : (first + j + 1) * DH] for j in range(count)]
    stacked = jnp.concatenate(heads, axis=0)
    return lax.dot_general(
        stacked, keys, (((1,), (1,)), ((), ())), preferred_element_type=jnp.float32
    )


def span_kernel(place_ref, query_ref, keys_ref, values_ref, numer_ref, stats_ref):
    q_rows = query_ref.shape[0]
    count = ROWS // q_rows
    length = keys_ref.shape[0]
    keys = keys_ref[...]
    values = jnp.concatenate([values_ref[...], jnp.ones((length, DH), jnp.bfloat16)], axis=1)
    query_pos = place_ref[1] * q_rows + lax.broadcasted_iota(jnp.int32, (q_rows, length), 0)
    allowed = lax.broadcasted_iota(jnp.int32, (q_rows, length), 1) <= query_pos
    bias = jnp.where(allowed, 0.0, LOW)
    bias = jnp.concatenate([bias] * count, axis=0)
    lanes = lax.broadcasted_iota(jnp.int32, (q_rows, DH), 1)
    stats = jnp.zeros((q_rows, DH), jnp.float32)
    for first in range(0, GROUP, count):
        scores = scores_of(query_ref, first, count, keys) + bias
        top = jnp.max(scores, axis=1, keepdims=True)
        weights = jnp.exp2((scores - top) * COEF)
        summed = jnp.dot(
            weights.astype(jnp.bfloat16), values, preferred_element_type=jnp.float32
        )
        for j in range(count):
            at = slice(j * q_rows, (j + 1) * q_rows)
            head = first + j
            numer_ref[:, head * DH : (head + 1) * DH] = summed[at, :DH]
            stats = jnp.where(lanes == head, top[at], stats)
            stats = jnp.where(lanes == GROUP + head, summed[at, DH:], stats)
    stats_ref[0] = stats


def attend_span(place, queries, span):
    q_rows = queries.shape[0]
    length = span.shape[0]
    wide = GROUP * DH
    spec = pltpu.PrefetchScalarGridSpec(
        num_scalar_prefetch=1,
        grid=(KVH,),
        in_specs=[
            pl.BlockSpec((q_rows, wide), lambda g, place: (0, g)),
            pl.BlockSpec((length, DH), lambda g, place: (0, g)),
            pl.BlockSpec((length, DH), lambda g, place: (0, KVH + g)),
        ],
        out_specs=[
            pl.BlockSpec((q_rows, wide), lambda g, place: (0, g)),
            pl.BlockSpec((1, q_rows, DH), lambda g, place: (g, 0, 0)),
        ],
    )
    return pl.pallas_call(
        span_kernel,
        grid_spec=spec,
        out_shape=[
            jax.ShapeDtypeStruct((q_rows, KVH * wide), jnp.float32),
            jax.ShapeDtypeStruct((KVH, q_rows, DH), jnp.float32),
        ],
        cost_estimate=pl.CostEstimate(
            flops=4 * q_rows * KVH * wide * length, bytes_accessed=8 * 2**20, transcendentals=0
        ),
        compiler_params=pltpu.CompilerParams(vmem_limit_bytes=48 * 2**20),
        name="attend_span",
    )(place, queries, span, span)


def prefix_kernel(parts, mask, place_ref, limit_ref, query_ref, *refs):
    pieces = refs[:parts]
    numer_ref, stats_ref, *_, out_ref = refs[parts:]
    q_rows = query_ref.shape[0]
    count = ROWS // q_rows
    listed, rows, _ = pieces[0].shape
    page = parts * rows
    length = listed * rows
    both = [piece[...].reshape(length, 2 * DH) for piece in pieces]
    both = both[0] if parts == 1 else jnp.concatenate(both, axis=0)
    keys = both[:, :DH]
    values = jnp.concatenate([both[:, DH:], jnp.ones((parts * length, DH), jnp.bfloat16)], axis=1)
    index = lax.broadcasted_iota(jnp.int32, (1, length), 1)
    at_page = lax.div(index, rows) * page + lax.rem(index, rows)
    positions = []
    for step in range(parts):
        part = lax.rem(place_ref[3] + step, parts)
        positions.append(at_page + part * rows)
    position = positions[0] if parts == 1 else jnp.concatenate(positions, axis=1)
    bias = jnp.where(position < limit_ref[0], 0.0, LOW)
    for first in range(0, GROUP, count):
        scores = scores_of(query_ref, first, count, keys) + bias
        top = jnp.max(scores, axis=1, keepdims=True)
        old_top = jnp.concatenate(
            [stats_ref[0, :, first + j : first + j + 1] for j in range(count)], axis=0
        )
        old_sum = jnp.concatenate(
            [stats_ref[0, :, GROUP + first + j : GROUP + first + j + 1] for j in range(count)],
            axis=0,
        )
        new_top = jnp.maximum(top, old_top)
        weights = jnp.exp2((scores - new_top) * COEF)
        factor = jnp.exp2((old_top - new_top) * COEF)
        summed = jnp.dot(
            weights.astype(jnp.bfloat16), values, preferred_element_type=jnp.float32
        )
        scale = 1.0 / (summed[:, DH : DH + 1] + old_sum * factor)
        for j in range(count):
            at = slice(j * q_rows, (j + 1) * q_rows)
            cols = slice((first + j) * DH, (first + j + 1) * DH)
            total = summed[at, :DH] + numer_ref[:, cols] * factor[at]
            out_ref[:, cols] = (total * scale[at]).astype(jnp.bfloat16)


def attend_prefix(place, limit, queries, pieces, numer, stats, partial, mask):
    q_rows = queries.shape[0]
    parts = len(pieces)
    wide = GROUP * DH
    head = lambda place: lax.rem(jnp.bitwise_xor(place[2], mask % KVH), KVH)
    column = pl.BlockSpec((q_rows, wide), lambda i, place, limit: (0, head(place)))
    spec = pltpu.PrefetchScalarGridSpec(
        num_scalar_prefetch=2,
        grid=(1,),
        in_specs=[column]
        + [pl.BlockSpec(pieces[0].shape, lambda i, place, limit: (0, 0, 0))] * parts
        + [
            column,
            pl.BlockSpec((1, q_rows, DH), lambda i, place, limit: (head(place), 0, 0)),
        ]
        + [pl.BlockSpec(memory_space=pl.ANY)] * len(partial),
        out_specs=column,
    )
    length = parts * pieces[0].shape[0] * pieces[0].shape[1]
    return pl.pallas_call(
        functools.partial(prefix_kernel, parts, mask),
        grid_spec=spec,
        out_shape=jax.ShapeDtypeStruct(queries.shape, jnp.bfloat16),
        input_output_aliases={2 + 1 + parts + 2: 0} if partial else {},
        cost_estimate=pl.CostEstimate(
            flops=4 * q_rows * wide * length, bytes_accessed=2 * 2**20, transcendentals=0
        ),
        compiler_params=pltpu.CompilerParams(vmem_limit_bytes=48 * 2**20),
        name="attend_prefix",
    )(place, limit, queries, *pieces, numer, stats, *partial)


def swap(array, blks, mask):
    return lax.ppermute(array, "blk", [(i, i ^ mask) for i in range(blks)])


def per_device(queries, span_kv, kv_store, page_ids, page_owner, prefix_len):
    pools = lax.axis_size("pool")
    blks = lax.axis_size("blk")
    pool_at = lax.axis_index("pool")
    blk_at = lax.axis_index("blk")
    stored, page, _ = kv_store.shape
    parts = blks // KVH
    rows = page // parts
    place = jnp.stack([pool_at, blk_at, blk_at % KVH, blk_at // KVH]).astype(jnp.int32)

    table = page_owner[0] * stored + page_ids[0]
    tables = [table]
    for shift in range(1, pools):
        tables.append(
            lax.ppermute(table, "pool", [((i + shift) % pools, i) for i in range(pools)])
        )
    span = lax.all_gather(span_kv, "blk", axis=0, tiled=True)
    picked = pick_pages(place, tables, kv_store, pools, rows)
    fetched = lax.all_to_all(picked, "pool", split_axis=0, concat_axis=0, tiled=True)
    numer, stats = attend_span(place, queries, span)
    held = {0: order_pages(table, fetched, stored)}
    bit = blks // 2
    while bit:
        held.update({mask ^ bit: swap(piece, blks, bit) for mask, piece in list(held.items())})
        bit //= 2
    partial = []
    for mask in range(KVH):
        pieces = [held[mask + step * KVH] for step in range(parts)]
        out = attend_prefix(place, prefix_len, queries, pieces, numer, stats, partial, mask)
        partial = [out]
    return out


def solution(mesh):
    in_specs = (
        P(("pool", "blk"), None),
        P(("pool", "blk"), None),
        P("pool", None, None),
        P("pool", None),
        P("pool", None),
        P("pool"),
    )
    out_specs = P(("pool", "blk"), None)
    return jax.shard_map(
        per_device, mesh=mesh, in_specs=in_specs, out_specs=out_specs, check_vma=False
    )
```

```python
import functools
import math

import jax
import jax.numpy as jnp
from jax import lax
from jax.experimental import pallas as pl
from jax.experimental.pallas import tpu as pltpu
from jax.sharding import PartitionSpec as P

KVH = 4
DH = 128
GROUP = 8
CAP = 2
COEF = math.log2(math.e) / math.sqrt(DH)
LOW = -1e30
ROWS = 256
STEPS = 2


def pick_kernel(place_ref, tables_ref, keys_ref, values_ref, out_ref):
    pools, listed = tables_ref.shape
    own = place_ref[0]
    stored = keys_ref.shape[0]

    def serve(request, carry):
        def visit(entry, rank):
            code = tables_ref[request, entry]
            hit = lax.div(code, stored) == own

            @pl.when(hit)
            def _():
                page = lax.rem(code, stored)
                slot = jnp.minimum(rank, CAP - 1)
                out_ref[request, slot, :, :DH] = keys_ref[page]
                out_ref[request, slot, :, DH:] = values_ref[page]

            return rank + hit.astype(jnp.int32)

        lax.fori_loop(0, listed, visit, jnp.int32(0))
        return carry

    lax.fori_loop(0, pools, serve, 0)


def pick_pages(place, tables, kv_store, rows):
    pools = tables.shape[0]
    block = (kv_store.shape[0], rows, DH)
    spec = pltpu.PrefetchScalarGridSpec(
        num_scalar_prefetch=2,
        grid=(1,),
        in_specs=[
            pl.BlockSpec(block, lambda i, place, tables: (0, place[3], place[2])),
            pl.BlockSpec(block, lambda i, place, tables: (0, place[3], KVH + place[2])),
        ],
        out_specs=pl.BlockSpec((pools, CAP, rows, 2 * DH), lambda i, *_: (0, 0, 0, 0)),
    )
    return pl.pallas_call(
        pick_kernel,
        grid_spec=spec,
        out_shape=jax.ShapeDtypeStruct((pools, CAP, rows, 2 * DH), kv_store.dtype),
        name="pick_pages",
    )(place, tables, kv_store, kv_store)


def order_kernel(stored, table_ref, fetched_ref, out_ref):
    listed = out_ref.shape[0]
    for entry in range(listed):
        owner = lax.div(table_ref[entry], stored)
        rank = jnp.int32(0)
        for earlier in range(entry):
            rank += (lax.div(table_ref[earlier], stored) == owner).astype(jnp.int32)
        out_ref[entry] = fetched_ref[owner, jnp.minimum(rank, CAP - 1)]


def order_pages(table, fetched, stored):
    listed = table.shape[0]
    rows = fetched.shape[2]
    spec = pltpu.PrefetchScalarGridSpec(
        num_scalar_prefetch=1,
        grid=(1,),
        in_specs=[pl.BlockSpec(fetched.shape, lambda i, table: (0, 0, 0, 0))],
        out_specs=pl.BlockSpec((listed, rows, 2 * DH), lambda i, table: (0, 0, 0)),
    )
    return pl.pallas_call(
        functools.partial(order_kernel, stored),
        grid_spec=spec,
        out_shape=jax.ShapeDtypeStruct((listed, rows, 2 * DH), fetched.dtype),
        name="order_pages",
    )(table, fetched)


def scores_of(query_ref, first, count, keys):
    heads = [query_ref[:, (first + j) * DH : (first + j + 1) * DH] for j in range(count)]
    stacked = jnp.concatenate(heads, axis=0)
    return lax.dot_general(
        stacked, keys, (((1,), (1,)), ((), ())), preferred_element_type=jnp.float32
    )


def span_kernel(place_ref, query_ref, keys_ref, values_ref, numer_ref, stats_ref):
    q_rows = query_ref.shape[0]
    count = ROWS // q_rows
    length = keys_ref.shape[0]
    keys = keys_ref[...]
    values = jnp.concatenate([values_ref[...], jnp.ones((length, DH), jnp.bfloat16)], axis=1)
    query_pos = place_ref[1] * q_rows + lax.broadcasted_iota(jnp.int32, (q_rows, length), 0)
    allowed = lax.broadcasted_iota(jnp.int32, (q_rows, length), 1) <= query_pos
    bias = jnp.where(allowed, 0.0, LOW)
    bias = jnp.concatenate([bias] * count, axis=0)
    lanes = lax.broadcasted_iota(jnp.int32, (q_rows, DH), 1)
    stats = jnp.zeros((q_rows, DH), jnp.float32)
    for first in range(0, GROUP, count):
        scores = scores_of(query_ref, first, count, keys) + bias
        top = jnp.max(scores, axis=1, keepdims=True)
        weights = jnp.exp2((scores - top) * COEF)
        summed = jnp.dot(
            weights.astype(jnp.bfloat16), values, preferred_element_type=jnp.float32
        )
        for j in range(count):
            at = slice(j * q_rows, (j + 1) * q_rows)
            head = first + j
            numer_ref[:, head * DH : (head + 1) * DH] = summed[at, :DH]
            stats = jnp.where(lanes == head, top[at], stats)
            stats = jnp.where(lanes == GROUP + head, summed[at, DH:], stats)
    stats_ref[0] = stats


def attend_span(place, queries, span):
    q_rows = queries.shape[0]
    length = span.shape[0]
    wide = GROUP * DH
    spec = pltpu.PrefetchScalarGridSpec(
        num_scalar_prefetch=1,
        grid=(KVH,),
        in_specs=[
            pl.BlockSpec((q_rows, wide), lambda g, place: (0, g)),
            pl.BlockSpec((length, DH), lambda g, place: (0, g)),
            pl.BlockSpec((length, DH), lambda g, place: (0, KVH + g)),
        ],
        out_specs=[
            pl.BlockSpec((q_rows, wide), lambda g, place: (0, g)),
            pl.BlockSpec((1, q_rows, DH), lambda g, place: (g, 0, 0)),
        ],
    )
    return pl.pallas_call(
        span_kernel,
        grid_spec=spec,
        out_shape=[
            jax.ShapeDtypeStruct((q_rows, KVH * wide), jnp.float32),
            jax.ShapeDtypeStruct((KVH, q_rows, DH), jnp.float32),
        ],
        cost_estimate=pl.CostEstimate(
            flops=4 * q_rows * KVH * wide * length, bytes_accessed=8 * 2**20, transcendentals=0
        ),
        compiler_params=pltpu.CompilerParams(vmem_limit_bytes=48 * 2**20),
        name="attend_span",
    )(place, queries, span, span)


def prefix_kernel(parts, mask, place_ref, limit_ref, query_ref, *refs):
    pieces = refs[:parts]
    numer_ref, stats_ref, *_, out_ref = refs[parts:]
    q_rows = query_ref.shape[0]
    count = ROWS // q_rows
    listed, rows, _ = pieces[0].shape
    page = parts * rows
    length = listed * rows
    both = [piece[...].reshape(length, 2 * DH) for piece in pieces]
    both = both[0] if parts == 1 else jnp.concatenate(both, axis=0)
    keys = both[:, :DH]
    values = jnp.concatenate([both[:, DH:], jnp.ones((parts * length, DH), jnp.bfloat16)], axis=1)
    index = lax.broadcasted_iota(jnp.int32, (1, length), 1)
    at_page = lax.div(index, rows) * page + lax.rem(index, rows)
    positions = []
    for step in range(parts):
        part = lax.rem(place_ref[3] + step, parts)
        positions.append(at_page + part * rows)
    position = positions[0] if parts == 1 else jnp.concatenate(positions, axis=1)
    bias = jnp.where(position < limit_ref[0], 0.0, LOW)
    base = pl.program_id(0) * (GROUP // STEPS)
    lanes = lax.broadcasted_iota(jnp.int32, (q_rows, DH), 1)
    stats = stats_ref[0]

    def column(lane):
        return jnp.sum(jnp.where(lanes == lane, stats, 0.0), axis=1, keepdims=True)

    for first in range(0, GROUP // STEPS, count):
        scores = scores_of(query_ref, first, count, keys) + bias
        top = jnp.max(scores, axis=1, keepdims=True)
        old_top = jnp.concatenate([column(base + first + j) for j in range(count)], axis=0)
        old_sum = jnp.concatenate(
            [column(base + GROUP + first + j) for j in range(count)], axis=0
        )
        new_top = jnp.maximum(top, old_top)
        weights = jnp.exp2((scores - new_top) * COEF)
        factor = jnp.exp2((old_top - new_top) * COEF)
        summed = jnp.dot(
            weights.astype(jnp.bfloat16), values, preferred_element_type=jnp.float32
        )
        scale = 1.0 / (summed[:, DH : DH + 1] + old_sum * factor)
        for j in range(count):
            at = slice(j * q_rows, (j + 1) * q_rows)
            cols = slice((first + j) * DH, (first + j + 1) * DH)
            total = summed[at, :DH] + numer_ref[:, cols] * factor[at]
            out_ref[:, cols] = (total * scale[at]).astype(jnp.bfloat16)


def attend_prefix(place, limit, queries, pieces, numer, stats, partial, mask):
    q_rows = queries.shape[0]
    parts = len(pieces)
    wide = GROUP * DH // STEPS
    head = lambda place: lax.rem(jnp.bitwise_xor(place[2], mask % KVH), KVH)
    column = pl.BlockSpec((q_rows, wide), lambda i, place, limit: (0, head(place) * STEPS + i))
    spec = pltpu.PrefetchScalarGridSpec(
        num_scalar_prefetch=2,
        grid=(STEPS,),
        in_specs=[column]
        + [pl.BlockSpec(pieces[0].shape, lambda i, place, limit: (0, 0, 0))] * parts
        + [
            column,
            pl.BlockSpec((1, q_rows, DH), lambda i, place, limit: (head(place), 0, 0)),
        ]
        + [pl.BlockSpec(memory_space=pl.ANY)] * len(partial),
        out_specs=column,
    )
    length = parts * pieces[0].shape[0] * pieces[0].shape[1]
    return pl.pallas_call(
        functools.partial(prefix_kernel, parts, mask),
        grid_spec=spec,
        out_shape=jax.ShapeDtypeStruct(queries.shape, jnp.bfloat16),
        input_output_aliases={2 + 1 + parts + 2: 0} if partial else {},
        cost_estimate=pl.CostEstimate(
            flops=4 * q_rows * GROUP * DH * length, bytes_accessed=2 * 2**20, transcendentals=0
        ),
        compiler_params=pltpu.CompilerParams(vmem_limit_bytes=48 * 2**20),
        name="attend_prefix",
    )(place, limit, queries, *pieces, numer, stats, *partial)


def swap(array, blks, mask):
    return lax.ppermute(array, "blk", [(i, i ^ mask) for i in range(blks)])


def per_device(queries, span_kv, kv_store, page_ids, page_owner, prefix_len):
    pools = lax.axis_size("pool")
    blks = lax.axis_size("blk")
    pool_at = lax.axis_index("pool")
    blk_at = lax.axis_index("blk")
    stored, page, _ = kv_store.shape
    parts = blks // KVH
    rows = page // parts
    place = jnp.stack([pool_at, blk_at, blk_at % KVH, blk_at // KVH]).astype(jnp.int32)

    table = page_owner[0] * stored + page_ids[0]
    tables = lax.all_to_all(
        jnp.broadcast_to(table[None, :], (pools, table.shape[0])),
        "pool",
        split_axis=0,
        concat_axis=0,
        tiled=True,
    )
    span = lax.all_gather(span_kv, "blk", axis=0, tiled=True)
    picked = pick_pages(place, tables, kv_store, rows)
    fetched = lax.all_to_all(picked, "pool", split_axis=0, concat_axis=0, tiled=True)
    fetched, span = lax.optimization_barrier((fetched, span))
    numer, stats = attend_span(place, queries, span)
    held = {0: order_pages(table, fetched, stored)}
    bit = blks // 2
    while bit:
        if bit == 1:
            far = {mask: piece for mask, piece in held.items() if mask}
            far, numer, stats = lax.optimization_barrier((far, numer, stats))
            held.update(far)
        held.update({mask ^ bit: swap(piece, blks, bit) for mask, piece in list(held.items())})
        bit //= 2
    partial = []
    for mask in range(KVH):
        pieces = [held[mask + step * KVH] for step in range(parts)]
        out = attend_prefix(place, prefix_len, queries, pieces, numer, stats, partial, mask)
        partial = [out]
    return out


def solution(mesh):
    in_specs = (
        P(("pool", "blk"), None),
        P(("pool", "blk"), None),
        P("pool", None, None),
        P("pool", None),
        P("pool", None),
        P("pool"),
    )
    out_specs = P(("pool", "blk"), None)
    return jax.shard_map(
        per_device, mesh=mesh, in_specs=in_specs, out_specs=out_specs, check_vma=False
    )
```

```python
import functools
import math

import jax
import jax.numpy as jnp
from jax import lax
from jax.experimental import pallas as pl
from jax.experimental.pallas import tpu as pltpu
from jax.sharding import PartitionSpec as P

KVH = 4
DH = 128
GROUP = 8
CAP = 2
COEF = math.log2(math.e) / math.sqrt(DH)
LOW = -1e30
ROWS = 256
STEPS = 2


def pick_kernel(place_ref, tables_ref, keys_ref, values_ref, out_ref):
    pools, listed = tables_ref.shape
    own = place_ref[0]
    stored = keys_ref.shape[0]

    def serve(request, carry):
        def visit(entry, rank):
            code = tables_ref[request, entry]
            hit = lax.div(code, stored) == own

            @pl.when(hit)
            def _():
                page = lax.rem(code, stored)
                slot = jnp.minimum(rank, CAP - 1)
                out_ref[request, slot, :, :DH] = keys_ref[page]
                out_ref[request, slot, :, DH:] = values_ref[page]

            return rank + hit.astype(jnp.int32)

        lax.fori_loop(0, listed, visit, jnp.int32(0))
        return carry

    lax.fori_loop(0, pools, serve, 0)


def pick_pages(place, tables, kv_store, rows):
    pools = tables.shape[0]
    block = (kv_store.shape[0], rows, DH)
    spec = pltpu.PrefetchScalarGridSpec(
        num_scalar_prefetch=2,
        grid=(1,),
        in_specs=[
            pl.BlockSpec(block, lambda i, place, tables: (0, place[3], place[2])),
            pl.BlockSpec(block, lambda i, place, tables: (0, place[3], KVH + place[2])),
        ],
        out_specs=pl.BlockSpec((pools, CAP, rows, 2 * DH), lambda i, *_: (0, 0, 0, 0)),
    )
    return pl.pallas_call(
        pick_kernel,
        grid_spec=spec,
        out_shape=jax.ShapeDtypeStruct((pools, CAP, rows, 2 * DH), kv_store.dtype),
        name="pick_pages",
    )(place, tables, kv_store, kv_store)


def order_kernel(stored, table_ref, fetched_ref, out_ref):
    listed = out_ref.shape[0]
    for entry in range(listed):
        owner = lax.div(table_ref[entry], stored)
        rank = jnp.int32(0)
        for earlier in range(entry):
            rank += (lax.div(table_ref[earlier], stored) == owner).astype(jnp.int32)
        out_ref[entry] = fetched_ref[owner, jnp.minimum(rank, CAP - 1)]


def order_pages(table, fetched, stored):
    listed = table.shape[0]
    rows = fetched.shape[2]
    spec = pltpu.PrefetchScalarGridSpec(
        num_scalar_prefetch=1,
        grid=(1,),
        in_specs=[pl.BlockSpec(fetched.shape, lambda i, table: (0, 0, 0, 0))],
        out_specs=pl.BlockSpec((listed, rows, 2 * DH), lambda i, table: (0, 0, 0)),
    )
    return pl.pallas_call(
        functools.partial(order_kernel, stored),
        grid_spec=spec,
        out_shape=jax.ShapeDtypeStruct((listed, rows, 2 * DH), fetched.dtype),
        name="order_pages",
    )(table, fetched)


def scores_of(query_ref, first, count, keys):
    heads = [query_ref[:, (first + j) * DH : (first + j + 1) * DH] for j in range(count)]
    stacked = jnp.concatenate(heads, axis=0)
    return lax.dot_general(
        stacked, keys, (((1,), (1,)), ((), ())), preferred_element_type=jnp.float32
    )


def span_kernel(place_ref, query_ref, keys_ref, values_ref, numer_ref, stats_ref):
    q_rows = query_ref.shape[0]
    count = ROWS // q_rows
    length = keys_ref.shape[0]
    keys = keys_ref[...]
    values = jnp.concatenate([values_ref[...], jnp.ones((length, DH), jnp.bfloat16)], axis=1)
    query_pos = place_ref[1] * q_rows + lax.broadcasted_iota(jnp.int32, (q_rows, length), 0)
    allowed = lax.broadcasted_iota(jnp.int32, (q_rows, length), 1) <= query_pos
    bias = jnp.where(allowed, 0.0, LOW)
    bias = jnp.concatenate([bias] * count, axis=0)
    lanes = lax.broadcasted_iota(jnp.int32, (q_rows, DH), 1)
    stats = jnp.zeros((q_rows, DH), jnp.float32)
    for first in range(0, GROUP, count):
        scores = scores_of(query_ref, first, count, keys) + bias
        top = jnp.max(scores, axis=1, keepdims=True)
        weights = jnp.exp2((scores - top) * COEF)
        summed = jnp.dot(
            weights.astype(jnp.bfloat16), values, preferred_element_type=jnp.float32
        )
        for j in range(count):
            at = slice(j * q_rows, (j + 1) * q_rows)
            head = first + j
            numer_ref[:, head * DH : (head + 1) * DH] = summed[at, :DH]
            stats = jnp.where(lanes == head, top[at], stats)
            stats = jnp.where(lanes == GROUP + head, summed[at, DH:], stats)
    stats_ref[0] = stats


def attend_span(place, queries, span):
    q_rows = queries.shape[0]
    length = span.shape[0]
    wide = GROUP * DH
    spec = pltpu.PrefetchScalarGridSpec(
        num_scalar_prefetch=1,
        grid=(KVH,),
        in_specs=[
            pl.BlockSpec((q_rows, wide), lambda g, place: (0, g)),
            pl.BlockSpec((length, DH), lambda g, place: (0, g)),
            pl.BlockSpec((length, DH), lambda g, place: (0, KVH + g)),
        ],
        out_specs=[
            pl.BlockSpec((q_rows, wide), lambda g, place: (0, g)),
            pl.BlockSpec((1, q_rows, DH), lambda g, place: (g, 0, 0)),
        ],
    )
    return pl.pallas_call(
        span_kernel,
        grid_spec=spec,
        out_shape=[
            jax.ShapeDtypeStruct((q_rows, KVH * wide), jnp.float32),
            jax.ShapeDtypeStruct((KVH, q_rows, DH), jnp.float32),
        ],
        cost_estimate=pl.CostEstimate(
            flops=4 * q_rows * KVH * wide * length, bytes_accessed=8 * 2**20, transcendentals=0
        ),
        compiler_params=pltpu.CompilerParams(vmem_limit_bytes=48 * 2**20),
        name="attend_span",
    )(place, queries, span, span)


def prefix_kernel(masks, parts, place_ref, limit_ref, query_ref, *refs):
    numer_ref, stats_ref, *_, out_ref = refs[masks * parts :]
    for at in range(masks):
        pieces = refs[at * parts : (at + 1) * parts]

        @pl.when(pl.program_id(0) == at)
        def _():
            finish_head(place_ref, limit_ref, query_ref, pieces, numer_ref, stats_ref, out_ref)


def finish_head(place_ref, limit_ref, query_ref, pieces, numer_ref, stats_ref, out_ref):
    parts = len(pieces)
    q_rows = query_ref.shape[0]
    count = ROWS // q_rows
    listed, rows, _ = pieces[0].shape
    page = parts * rows
    length = listed * rows
    both = [piece[...].reshape(length, 2 * DH) for piece in pieces]
    both = both[0] if parts == 1 else jnp.concatenate(both, axis=0)
    keys = both[:, :DH]
    values = jnp.concatenate([both[:, DH:], jnp.ones((parts * length, DH), jnp.bfloat16)], axis=1)
    index = lax.broadcasted_iota(jnp.int32, (1, length), 1)
    at_page = lax.div(index, rows) * page + lax.rem(index, rows)
    positions = []
    for step in range(parts):
        part = lax.rem(place_ref[3] + step, parts)
        positions.append(at_page + part * rows)
    position = positions[0] if parts == 1 else jnp.concatenate(positions, axis=1)
    bias = jnp.where(position < limit_ref[0], 0.0, LOW)
    base = pl.program_id(1) * (GROUP // STEPS)
    lanes = lax.broadcasted_iota(jnp.int32, (q_rows, DH), 1)
    stats = stats_ref[0]

    def column(lane):
        return jnp.sum(jnp.where(lanes == lane, stats, 0.0), axis=1, keepdims=True)

    for first in range(0, GROUP // STEPS, count):
        scores = scores_of(query_ref, first, count, keys) + bias
        top = jnp.max(scores, axis=1, keepdims=True)
        old_top = jnp.concatenate([column(base + first + j) for j in range(count)], axis=0)
        old_sum = jnp.concatenate(
            [column(base + GROUP + first + j) for j in range(count)], axis=0
        )
        new_top = jnp.maximum(top, old_top)
        weights = jnp.exp2((scores - new_top) * COEF)
        factor = jnp.exp2((old_top - new_top) * COEF)
        summed = jnp.dot(
            weights.astype(jnp.bfloat16), values, preferred_element_type=jnp.float32
        )
        scale = 1.0 / (summed[:, DH : DH + 1] + old_sum * factor)
        for j in range(count):
            at = slice(j * q_rows, (j + 1) * q_rows)
            cols = slice((first + j) * DH, (first + j + 1) * DH)
            total = summed[at, :DH] + numer_ref[:, cols] * factor[at]
            out_ref[:, cols] = (total * scale[at]).astype(jnp.bfloat16)


def attend_prefix(place, limit, queries, held, numer, stats, partial, masks):
    q_rows = queries.shape[0]
    parts = len(held) // KVH
    pieces = [held[mask + step * KVH] for mask in masks for step in range(parts)]
    wide = GROUP * DH // STEPS

    def head(h, place):
        mask = masks[0]
        for at in range(1, len(masks)):
            mask = jnp.where(h == at, masks[at], mask)
        return jnp.bitwise_xor(place[2], mask)

    column = pl.BlockSpec(
        (q_rows, wide), lambda h, i, place, limit: (0, head(h, place) * STEPS + i)
    )
    spec = pltpu.PrefetchScalarGridSpec(
        num_scalar_prefetch=2,
        grid=(len(masks), STEPS),
        in_specs=[column]
        + [pl.BlockSpec(pieces[0].shape, lambda h, i, place, limit: (0, 0, 0))] * len(pieces)
        + [
            column,
            pl.BlockSpec((1, q_rows, DH), lambda h, i, place, limit: (head(h, place), 0, 0)),
        ]
        + [pl.BlockSpec(memory_space=pl.ANY)] * len(partial),
        out_specs=column,
    )
    length = parts * pieces[0].shape[0] * pieces[0].shape[1]
    return pl.pallas_call(
        functools.partial(prefix_kernel, len(masks), parts),
        grid_spec=spec,
        out_shape=jax.ShapeDtypeStruct(queries.shape, jnp.bfloat16),
        input_output_aliases={2 + 1 + len(pieces) + 2: 0} if partial else {},
        cost_estimate=pl.CostEstimate(
            flops=len(masks) * 4 * q_rows * GROUP * DH * length,
            bytes_accessed=len(masks) * 2 * 2**20,
            transcendentals=0,
        ),
        compiler_params=pltpu.CompilerParams(vmem_limit_bytes=48 * 2**20),
        name="attend_prefix",
    )(place, limit, queries, *pieces, numer, stats, *partial)


def swap(array, blks, mask):
    return lax.ppermute(array, "blk", [(i, i ^ mask) for i in range(blks)])


def per_device(queries, span_kv, kv_store, page_ids, page_owner, prefix_len):
    pools = lax.axis_size("pool")
    blks = lax.axis_size("blk")
    pool_at = lax.axis_index("pool")
    blk_at = lax.axis_index("blk")
    stored, page, _ = kv_store.shape
    parts = blks // KVH
    rows = page // parts
    place = jnp.stack([pool_at, blk_at, blk_at % KVH, blk_at // KVH]).astype(jnp.int32)

    table = page_owner[0] * stored + page_ids[0]
    tables = lax.all_to_all(
        jnp.broadcast_to(table[None, :], (pools, table.shape[0])),
        "pool",
        split_axis=0,
        concat_axis=0,
        tiled=True,
    )
    span = lax.all_gather(span_kv, "blk", axis=0, tiled=True)
    picked = pick_pages(place, tables, kv_store, rows)
    fetched = lax.all_to_all(picked, "pool", split_axis=0, concat_axis=0, tiled=True)
    numer, stats = attend_span(place, queries, span)
    fetched, numer, stats = lax.optimization_barrier((fetched, numer, stats))
    held = {0: order_pages(table, fetched, stored)}
    bit = blks // 2
    while bit:
        held.update({mask ^ bit: swap(piece, blks, bit) for mask, piece in list(held.items())})
        bit //= 2
    partial = []
    for masks in ((0,), (1, 2), (3,)):
        partial = [
            attend_prefix(place, prefix_len, queries, held, numer, stats, partial, masks)
        ]
    return partial[0]


def solution(mesh):
    in_specs = (
        P(("pool", "blk"), None),
        P(("pool", "blk"), None),
        P("pool", None, None),
        P("pool", None),
        P("pool", None),
        P("pool"),
    )
    out_specs = P(("pool", "blk"), None)
    return jax.shard_map(
        per_device, mesh=mesh, in_specs=in_specs, out_specs=out_specs, check_vma=False
    )
```

```python
import functools
import math

import jax
import jax.numpy as jnp
from jax import lax
from jax.experimental import pallas as pl
from jax.experimental.pallas import tpu as pltpu
from jax.sharding import PartitionSpec as P

KVH = 4
DH = 128
GROUP = 8
CAP = 2
COEF = math.log2(math.e) / math.sqrt(DH)
LOW = -1e30
ROWS = 256


SMEM = pl.BlockSpec(memory_space=pltpu.SMEM)
VMEM = pl.BlockSpec(memory_space=pltpu.VMEM)
ANY = pl.BlockSpec(memory_space=pl.ANY)


def pick_kernel(place_ref, tables_ref, keys_ref, values_ref, out_ref):
    pools, listed = tables_ref.shape
    own = place_ref[0]
    stored = keys_ref.shape[0]

    def serve(request, carry):
        def visit(entry, rank):
            code = tables_ref[request, entry]
            hit = lax.div(code, stored) == own

            @pl.when(hit)
            def _():
                page = lax.rem(code, stored)
                slot = jnp.minimum(rank, CAP - 1)
                out_ref[request, slot, :, :DH] = keys_ref[page]
                out_ref[request, slot, :, DH:] = values_ref[page]

            return rank + hit.astype(jnp.int32)

        lax.fori_loop(0, listed, visit, jnp.int32(0))
        return carry

    lax.fori_loop(0, pools, serve, 0)


def pick_pages(place, tables, kv_store, rows):
    pools = tables.shape[0]
    shape = (kv_store.shape[0], rows, DH)
    keys = lax.dynamic_slice(kv_store, (0, place[3] * rows, place[2] * DH), shape)
    values = lax.dynamic_slice(kv_store, (0, place[3] * rows, (KVH + place[2]) * DH), shape)
    return pl.pallas_call(
        pick_kernel,
        in_specs=[SMEM, SMEM, VMEM, VMEM],
        out_specs=VMEM,
        out_shape=jax.ShapeDtypeStruct((pools, CAP, rows, 2 * DH), kv_store.dtype),
        name="pick_pages",
    )(place, tables, keys, values)


def order_kernel(stored, table_ref, fetched_ref, out_ref):
    listed = out_ref.shape[0]
    for entry in range(listed):
        owner = lax.div(table_ref[entry], stored)
        rank = jnp.int32(0)
        for earlier in range(entry):
            rank += (lax.div(table_ref[earlier], stored) == owner).astype(jnp.int32)
        out_ref[entry] = fetched_ref[owner, jnp.minimum(rank, CAP - 1)]


def order_pages(table, fetched, stored):
    listed = table.shape[0]
    rows = fetched.shape[2]
    return pl.pallas_call(
        functools.partial(order_kernel, stored),
        in_specs=[SMEM, VMEM],
        out_specs=VMEM,
        out_shape=jax.ShapeDtypeStruct((listed, rows, 2 * DH), fetched.dtype),
        name="order_pages",
    )(table, fetched)


def scores_of(query_ref, first, count, keys):
    heads = [query_ref[:, (first + j) * DH : (first + j + 1) * DH] for j in range(count)]
    stacked = heads[0] if count == 1 else jnp.concatenate(heads, axis=0)
    return lax.dot_general(
        stacked, keys, (((1,), (1,)), ((), ())), preferred_element_type=jnp.float32
    )


def with_ones(values):
    return jnp.concatenate([values, jnp.ones((values.shape[0], DH), values.dtype)], axis=1)


def span_kernel(place_ref, query_ref, keys_ref, values_ref, numer_ref, stats_ref, copy_ref):
    q_rows = query_ref.shape[0]
    count = ROWS // q_rows
    length = keys_ref.shape[0]
    copy_ref[0] = query_ref[...]
    keys = keys_ref[...]
    values = with_ones(values_ref[...])
    query_pos = place_ref[1] * q_rows + lax.broadcasted_iota(jnp.int32, (q_rows, length), 0)
    allowed = lax.broadcasted_iota(jnp.int32, (q_rows, length), 1) <= query_pos
    bias = jnp.where(allowed, 0.0, LOW)
    bias = jnp.concatenate([bias] * count, axis=0)
    lanes = lax.broadcasted_iota(jnp.int32, (q_rows, DH), 1)
    stats = jnp.zeros((q_rows, DH), jnp.float32)
    for first in range(0, GROUP, count):
        scores = scores_of(query_ref, first, count, keys) + bias
        top = jnp.max(scores, axis=1, keepdims=True)
        weights = jnp.exp2((scores - top) * COEF)
        summed = jnp.dot(
            weights.astype(jnp.bfloat16), values, preferred_element_type=jnp.float32
        )
        for j in range(count):
            at = slice(j * q_rows, (j + 1) * q_rows)
            head = first + j
            numer_ref[0, :, head * DH : (head + 1) * DH] = summed[at, :DH]
            stats = jnp.where(lanes == head, top[at], stats)
            stats = jnp.where(lanes == GROUP + head, summed[at, DH:], stats)
    stats_ref[0] = stats


def attend_span(place, queries, span):
    q_rows = queries.shape[0]
    length = span.shape[0]
    wide = GROUP * DH
    spec = pltpu.PrefetchScalarGridSpec(
        num_scalar_prefetch=1,
        grid=(KVH,),
        in_specs=[
            pl.BlockSpec((q_rows, wide), lambda m, place: (0, place[2] ^ m)),
            pl.BlockSpec((length, DH), lambda m, place: (0, place[2] ^ m)),
            pl.BlockSpec((length, DH), lambda m, place: (0, KVH + (place[2] ^ m))),
        ],
        out_specs=[
            pl.BlockSpec((1, q_rows, wide), lambda m, place: (m, 0, 0)),
            pl.BlockSpec((1, q_rows, DH), lambda m, place: (m, 0, 0)),
            pl.BlockSpec((1, q_rows, wide), lambda m, place: (m, 0, 0)),
        ],
    )
    return pl.pallas_call(
        span_kernel,
        grid_spec=spec,
        out_shape=[
            jax.ShapeDtypeStruct((KVH, q_rows, wide), jnp.float32),
            jax.ShapeDtypeStruct((KVH, q_rows, DH), jnp.float32),
            jax.ShapeDtypeStruct((KVH, q_rows, wide), jnp.bfloat16),
        ],
        cost_estimate=pl.CostEstimate(
            flops=4 * q_rows * KVH * wide * length, bytes_accessed=8 * 2**20, transcendentals=0
        ),
        compiler_params=pltpu.CompilerParams(vmem_limit_bytes=48 * 2**20),
        name="attend_span",
    )(place, queries, span, span)


def prefix_kernel(mask, parts, place_ref, limit_ref, *refs):
    pieces = refs[:parts]
    query_ref, numer_ref, stats_ref, *_, out_ref, done_ref, sem = refs[parts:]
    q_rows = query_ref.shape[1]
    count = ROWS // q_rows
    wide = GROUP * DH
    listed, rows, _ = pieces[0].shape
    length = listed * rows
    both = [piece[...].reshape(length, 2 * DH) for piece in pieces]
    both = both[0] if parts == 1 else jnp.concatenate(both, axis=0)
    keys = both[:, :DH]
    values = with_ones(both[:, DH:])
    index = lax.broadcasted_iota(jnp.int32, (1, length), 1)
    at_page = lax.div(index, rows) * (parts * rows) + lax.rem(index, rows)
    positions = [at_page + lax.rem(place_ref[3] + step, parts) * rows for step in range(parts)]
    position = positions[0] if parts == 1 else jnp.concatenate(positions, axis=1)
    bias = jnp.where(position < limit_ref[0], 0.0, LOW)
    for first in range(0, GROUP, count):
        scores = scores_of(query_ref.at[mask], first, count, keys) + bias
        top = jnp.max(scores, axis=1, keepdims=True)
        lanes = range(first, first + count)
        old_top = jnp.concatenate([stats_ref[mask, :, i : i + 1] for i in lanes], axis=0)
        old_sum = jnp.concatenate(
            [stats_ref[mask, :, GROUP + i : GROUP + i + 1] for i in lanes], axis=0
        )
        new_top = jnp.maximum(top, old_top)
        weights = jnp.exp2((scores - new_top) * COEF)
        factor = jnp.exp2((old_top - new_top) * COEF)
        summed = jnp.dot(
            weights.astype(jnp.bfloat16), values, preferred_element_type=jnp.float32
        )
        scale = 1.0 / (summed[:, DH : DH + 1] + old_sum * factor)
        for j in range(count):
            at = slice(j * q_rows, (j + 1) * q_rows)
            columns = slice((first + j) * DH, (first + j + 1) * DH)
            total = summed[at, :DH] + numer_ref[mask, :, columns] * factor[at]
            done_ref[:, columns] = (total * scale[at]).astype(jnp.bfloat16)
    head = jnp.bitwise_xor(place_ref[2], mask)
    for choice in range(KVH):

        @pl.when(head == choice)
        def _():
            columns = slice(choice * wide, (choice + 1) * wide)
            pltpu.make_async_copy(done_ref, out_ref.at[:, columns], sem).start()

    pltpu.make_async_copy(done_ref, out_ref.at[:, :wide], sem).wait()


def attend_prefix(place, limit, held, query, numer, stats, partial, mask):
    _, q_rows, wide = query.shape
    parts = 2 * len(held) // KVH
    pieces = [held[mask + step * KVH] for step in range(parts)]
    length = parts * pieces[0].shape[0] * pieces[0].shape[1]
    return pl.pallas_call(
        functools.partial(prefix_kernel, mask, parts),
        in_specs=[SMEM, SMEM] + [VMEM] * (parts + 3) + [ANY] * len(partial),
        out_specs=ANY,
        out_shape=jax.ShapeDtypeStruct((q_rows, KVH * wide), jnp.bfloat16),
        scratch_shapes=[pltpu.VMEM((q_rows, wide), jnp.bfloat16), pltpu.SemaphoreType.DMA],
        input_output_aliases={2 + parts + 3: 0} if partial else {},
        cost_estimate=pl.CostEstimate(
            flops=4 * q_rows * wide * length, bytes_accessed=2 * 2**20, transcendentals=0
        ),
        compiler_params=pltpu.CompilerParams(vmem_limit_bytes=48 * 2**20),
        name="attend_prefix",
    )(place, limit, *pieces, query, numer, stats, *partial)


def swap(array, blks, mask):
    return lax.ppermute(array, "blk", [(i, i ^ mask) for i in range(blks)])


def per_device(queries, span_kv, kv_store, page_ids, page_owner, prefix_len):
    pools = lax.axis_size("pool")
    blks = lax.axis_size("blk")
    pool_at = lax.axis_index("pool")
    blk_at = lax.axis_index("blk")
    stored, page, _ = kv_store.shape
    parts = blks // KVH
    rows = page // parts
    place = jnp.stack([pool_at, blk_at, blk_at % KVH, blk_at // KVH]).astype(jnp.int32)

    table = page_owner[0] * stored + page_ids[0]
    tables = lax.all_to_all(
        jnp.broadcast_to(table[None, :], (pools, table.shape[0])),
        "pool",
        split_axis=0,
        concat_axis=0,
        tiled=True,
    )
    span = lax.all_gather(span_kv, "blk", axis=0, tiled=True)
    picked = pick_pages(place, tables, kv_store, rows)
    fetched = lax.all_to_all(picked, "pool", split_axis=0, concat_axis=0, tiled=True)
    state = attend_span(place, queries, span)
    fetched, *state = lax.optimization_barrier((fetched, *state))
    numer, stats, query = state
    held = {0: order_pages(table, fetched, stored)}
    bit = blks // 2
    while bit > 1:
        held.update({mask ^ bit: swap(piece, blks, bit) for mask, piece in list(held.items())})
        bit //= 2
    near = {mask: piece for mask, piece in held.items() if mask & (KVH - 1) == 0}
    far = {mask: piece for mask, piece in held.items() if mask & (KVH - 1)}
    near.update({mask ^ 1: swap(piece, blks, 1) for mask, piece in list(near.items())})
    out = attend_prefix(place, prefix_len, near, query, numer, stats, [], 0)
    out = attend_prefix(place, prefix_len, near, query, numer, stats, [out], 1)
    far, out = lax.optimization_barrier((far, out))
    far.update({mask ^ 1: swap(piece, blks, 1) for mask, piece in list(far.items())})
    out = attend_prefix(place, prefix_len, far, query, numer, stats, [out], 2)
    return attend_prefix(place, prefix_len, far, query, numer, stats, [out], 3)


def solution(mesh):
    in_specs = (
        P(("pool", "blk"), None),
        P(("pool", "blk"), None),
        P("pool", None, None),
        P("pool", None),
        P("pool", None),
        P("pool"),
    )
    out_specs = P(("pool", "blk"), None)
    return jax.shard_map(
        per_device, mesh=mesh, in_specs=in_specs, out_specs=out_specs, check_vma=False
    )
```

```python
import functools
import math

import jax
import jax.numpy as jnp
from jax import lax
from jax.experimental import pallas as pl
from jax.experimental.pallas import tpu as pltpu
from jax.sharding import PartitionSpec as P

KVH = 4
DH = 128
GROUP = 8
CAP = 2
COEF = math.log2(math.e) / math.sqrt(DH)
LOW = -1e30
ROWS = 256


SMEM = pl.BlockSpec(memory_space=pltpu.SMEM)
VMEM = pl.BlockSpec(memory_space=pltpu.VMEM)
ANY = pl.BlockSpec(memory_space=pl.ANY)
HBM = pl.BlockSpec(memory_space=pltpu.HBM)


def columns_from(first, count):
    return pl.ds(pl.multiple_of(first * DH, DH), count * DH)


def pick_kernel(place_ref, tables_ref, store_ref, out_ref, table, table_sem, sems):
    pools, listed = tables_ref.shape
    own = place_ref[0]
    stored = store_ref.shape[0]
    load = pltpu.make_async_copy(tables_ref, table, table_sem)
    load.start()
    load.wait()

    def page_copy(request, slot, page):
        return pltpu.make_async_copy(
            store_ref.at[page], out_ref.at[request, slot], sems.at[request, slot]
        )

    def serve(request, carry):
        def visit(entry, state):
            rank, pages = state
            code = table[request, entry]
            hit = (lax.div(code, stored) == own).astype(jnp.int32)
            page = lax.rem(code, stored)
            pages = [
                jnp.where((hit == 1) & (rank == slot), page, pages[slot]) for slot in range(CAP)
            ]
            return rank + hit, pages

        state = (jnp.int32(0), [jnp.int32(0)] * CAP)
        _, pages = lax.fori_loop(0, listed, visit, state, unroll=listed <= 8)
        for slot in range(CAP):
            page_copy(request, slot, pages[slot]).start()
        return carry

    lax.fori_loop(0, pools, serve, 0)

    def finish(request, carry):
        for slot in range(CAP):
            page_copy(request, slot, 0).wait()
        return carry

    lax.fori_loop(0, pools, finish, 0)


def pick_pages(place, tables, kv_store, rows):
    pools = tables.shape[0]
    shape = (kv_store.shape[0], rows, DH)
    keys = lax.dynamic_slice(kv_store, (0, place[3] * rows, place[2] * DH), shape)
    values = lax.dynamic_slice(kv_store, (0, place[3] * rows, (KVH + place[2]) * DH), shape)
    return pl.pallas_call(
        pick_kernel,
        in_specs=[SMEM, ANY, HBM],
        out_specs=HBM,
        out_shape=pltpu.HBM((pools, CAP, rows, 2 * DH), kv_store.dtype),
        scratch_shapes=[
            pltpu.SMEM(tables.shape, jnp.int32),
            pltpu.SemaphoreType.DMA,
            pltpu.SemaphoreType.DMA((pools, CAP)),
        ],
        name="pick_pages",
    )(place, tables, jnp.concatenate([keys, values], axis=2))


def order_kernel(owners_ref, fetched_ref, out_ref, sems):
    listed = out_ref.shape[0]
    copies = []
    for entry in range(listed):
        owner = owners_ref[0, entry]
        rank = jnp.int32(0)
        for earlier in range(entry):
            rank += (owners_ref[0, earlier] == owner).astype(jnp.int32)
        rank = jnp.minimum(rank, CAP - 1)
        copies.append(
            pltpu.make_async_copy(fetched_ref.at[owner, rank], out_ref.at[entry], sems.at[entry])
        )
        copies[-1].start()
    for copy in copies:
        copy.wait()


def order_pages(owners, fetched):
    listed = owners.shape[1]
    rows = fetched.shape[2]
    return pl.pallas_call(
        order_kernel,
        in_specs=[SMEM, HBM],
        out_specs=VMEM,
        out_shape=pltpu.VMEM((listed, rows, 2 * DH), fetched.dtype),
        scratch_shapes=[pltpu.SemaphoreType.DMA((listed,))],
        name="order_pages",
    )(owners, pltpu.with_memory_space_constraint(fetched, pltpu.HBM))


def scores_of(query_ref, first, count, keys):
    heads = [query_ref[:, (first + j) * DH : (first + j + 1) * DH] for j in range(count)]
    stacked = heads[0] if count == 1 else jnp.concatenate(heads, axis=0)
    return lax.dot_general(
        stacked, keys, (((1,), (1,)), ((), ())), preferred_element_type=jnp.float32
    )


def with_ones(values):
    return jnp.concatenate([values, jnp.ones((values.shape[0], DH), values.dtype)], axis=1)


def span_kernel(place_ref, query_ref, keys_ref, values_ref, mean_ref, level_ref, copy_ref):
    q_rows = query_ref.shape[0]
    count = ROWS // q_rows
    length = keys_ref.shape[0]
    copy_ref[0] = query_ref[...]
    keys = keys_ref[...]
    values = with_ones(values_ref[...])
    query_pos = place_ref[1] * q_rows + lax.broadcasted_iota(jnp.int32, (q_rows, length), 0)
    allowed = lax.broadcasted_iota(jnp.int32, (q_rows, length), 1) <= query_pos
    bias = jnp.where(allowed, 0.0, LOW)
    bias = jnp.concatenate([bias] * count, axis=0)
    for first in range(0, GROUP, count):
        scores = scores_of(query_ref, first, count, keys) + bias
        top = jnp.max(scores, axis=1, keepdims=True)
        weights = jnp.exp2((scores - top) * COEF)
        summed = jnp.dot(
            weights.astype(jnp.bfloat16), values, preferred_element_type=jnp.float32
        )
        total = summed[:, DH:]
        level = top * COEF + jnp.log2(total)
        mean = summed[:, :DH] / total
        for j in range(count):
            at = slice(j * q_rows, (j + 1) * q_rows)
            columns = slice((first + j) * DH, (first + j + 1) * DH)
            mean_ref[0, :, columns] = mean[at]
            level_ref[0, :, columns] = level[at]


def attend_span(place, queries, span):
    q_rows = queries.shape[0]
    length = span.shape[0]
    wide = GROUP * DH
    spec = pltpu.PrefetchScalarGridSpec(
        num_scalar_prefetch=1,
        grid=(KVH,),
        in_specs=[
            pl.BlockSpec((q_rows, wide), lambda m, place: (0, place[2] ^ m)),
            pl.BlockSpec((length, DH), lambda m, place: (0, place[2] ^ m)),
            pl.BlockSpec((length, DH), lambda m, place: (0, KVH + (place[2] ^ m))),
        ],
        out_specs=[
            pl.BlockSpec((1, q_rows, wide), lambda m, place: (m, 0, 0)),
            pl.BlockSpec((1, q_rows, wide), lambda m, place: (m, 0, 0)),
            pl.BlockSpec((1, q_rows, wide), lambda m, place: (m, 0, 0)),
        ],
    )
    return pl.pallas_call(
        span_kernel,
        grid_spec=spec,
        out_shape=[
            pltpu.VMEM((KVH, q_rows, wide), jnp.float32),
            pltpu.VMEM((KVH, q_rows, wide), jnp.float32),
            pltpu.VMEM((KVH, q_rows, wide), jnp.bfloat16),
        ],
        cost_estimate=pl.CostEstimate(
            flops=4 * q_rows * KVH * wide * length, bytes_accessed=8 * 2**20, transcendentals=0
        ),
        compiler_params=pltpu.CompilerParams(vmem_limit_bytes=48 * 2**20),
        name="attend_span",
    )(place, queries, span, span)


def prefix_kernel(mask, parts, place_ref, limit_ref, *refs):
    pieces = refs[:parts]
    query_ref, mean_ref, level_ref, *_, out_ref, done_ref, sems = refs[parts:]
    q_rows = query_ref.shape[1]
    count = ROWS // q_rows
    head = jnp.bitwise_xor(place_ref[2], mask)
    listed, rows, _ = pieces[0].shape
    length = listed * rows
    both = [piece[...].reshape(length, 2 * DH) for piece in pieces]
    both = both[0] if parts == 1 else jnp.concatenate(both, axis=0)
    keys = both[:, :DH]
    values = with_ones(both[:, DH:])
    safe = length * 5 // 8 // DH * DH
    index = safe + lax.broadcasted_iota(jnp.int32, (1, length - safe), 1)
    at_page = lax.div(index, rows) * (parts * rows) + lax.rem(index, rows)
    biases = [
        jnp.where(at_page + lax.rem(place_ref[3] + step, parts) * rows < limit_ref[0], 0.0, LOW)
        for step in range(parts)
    ]
    copies = []
    for first in range(0, GROUP, count):
        raw = scores_of(query_ref.at[mask], first, count, keys)
        scores = []
        for step, bias in enumerate(biases):
            scores.append(raw[:, step * length : step * length + safe])
            scores.append(raw[:, step * length + safe : (step + 1) * length] + bias)
        scores = jnp.concatenate(scores, axis=1)
        heads = [slice((first + j) * DH, (first + j + 1) * DH) for j in range(count)]
        level = jnp.concatenate([level_ref[mask, :, columns] for columns in heads], axis=0)
        mean = jnp.concatenate([mean_ref[mask, :, columns] for columns in heads], axis=0)
        top = jnp.maximum(jnp.max(scores, axis=1, keepdims=True) * COEF, level)
        tops = jnp.concatenate([top] * (parts * length // DH), axis=1)
        weights = jnp.exp2(scores * COEF - tops)
        old = jnp.exp2(level - top)
        summed = jnp.dot(
            weights.astype(jnp.bfloat16), values, preferred_element_type=jnp.float32
        )
        result = (summed[:, :DH] + mean * old) / (summed[:, DH:] + old)
        for j, columns in enumerate(heads):
            done_ref[:, columns] = result[j * q_rows : (j + 1) * q_rows].astype(jnp.bfloat16)
        copies.append(
            pltpu.make_async_copy(
                done_ref.at[:, first * DH : (first + count) * DH],
                out_ref.at[:, columns_from(head * GROUP + first, count)],
                sems.at[first // count],
            )
        )
        copies[-1].start()
    for copy in copies:
        copy.wait()


def attend_prefix(place, limit, held, query, mean, level, partial, mask):
    _, q_rows, wide = query.shape
    parts = 2 * len(held) // KVH
    pieces = [held[mask + step * KVH] for step in range(parts)]
    length = parts * pieces[0].shape[0] * pieces[0].shape[1]
    return pl.pallas_call(
        functools.partial(prefix_kernel, mask, parts),
        in_specs=[SMEM, SMEM] + [VMEM] * (parts + 3) + [ANY] * len(partial),
        out_specs=ANY,
        out_shape=jax.ShapeDtypeStruct((q_rows, KVH * wide), jnp.bfloat16),
        scratch_shapes=[
            pltpu.VMEM((q_rows, wide), jnp.bfloat16),
            pltpu.SemaphoreType.DMA((GROUP * q_rows // ROWS,)),
        ],
        input_output_aliases={2 + parts + 3: 0} if partial else {},
        cost_estimate=pl.CostEstimate(
            flops=4 * q_rows * wide * length, bytes_accessed=2 * 2**20, transcendentals=0
        ),
        compiler_params=pltpu.CompilerParams(vmem_limit_bytes=48 * 2**20),
        name="attend_prefix",
    )(place, limit, *pieces, query, mean, level, *partial)


def swap(array, blks, mask):
    return lax.ppermute(array, "blk", [(i, i ^ mask) for i in range(blks)])


def per_device(queries, span_kv, kv_store, page_ids, page_owner, prefix_len):
    pools = lax.axis_size("pool")
    blks = lax.axis_size("blk")
    pool_at = lax.axis_index("pool")
    blk_at = lax.axis_index("blk")
    stored, page, _ = kv_store.shape
    parts = blks // KVH
    rows = page // parts
    place = jnp.stack([pool_at, blk_at, blk_at % KVH, blk_at // KVH]).astype(jnp.int32)

    table = page_owner[0] * stored + page_ids[0]
    tables = lax.all_to_all(
        jnp.broadcast_to(table[None, :], (pools, table.shape[0])),
        "pool",
        split_axis=0,
        concat_axis=0,
        tiled=True,
    )
    span = lax.all_gather(span_kv, "blk", axis=0, tiled=True)
    picked = pick_pages(place, tables, kv_store, rows)
    fetched = lax.all_to_all(picked, "pool", split_axis=0, concat_axis=0, tiled=True)
    state = attend_span(place, queries, span)
    fetched, *state = lax.optimization_barrier((fetched, *state))
    mean, level, query = state
    held = {0: order_pages(page_owner, fetched)}
    bit = blks // 2
    while bit > 1:
        held.update({mask ^ bit: swap(piece, blks, bit) for mask, piece in list(held.items())})
        bit //= 2
    near = {mask: piece for mask, piece in held.items() if mask & (KVH - 1) == 0}
    far = {mask: piece for mask, piece in held.items() if mask & (KVH - 1)}
    near.update({mask ^ 1: swap(piece, blks, 1) for mask, piece in list(near.items())})
    out = attend_prefix(place, prefix_len, near, query, mean, level, [], 0)
    out = attend_prefix(place, prefix_len, near, query, mean, level, [out], 1)
    far, out = lax.optimization_barrier((far, out))
    far.update({mask ^ 1: swap(piece, blks, 1) for mask, piece in list(far.items())})
    out = attend_prefix(place, prefix_len, far, query, mean, level, [out], 2)
    return attend_prefix(place, prefix_len, far, query, mean, level, [out], 3)


def solution(mesh):
    in_specs = (
        P(("pool", "blk"), None),
        P(("pool", "blk"), None),
        P("pool", None, None),
        P("pool", None),
        P("pool", None),
        P("pool"),
    )
    out_specs = P(("pool", "blk"), None)
    return jax.shard_map(
        per_device, mesh=mesh, in_specs=in_specs, out_specs=out_specs, check_vma=False
    )
```

```python
import functools
import math

import jax
import jax.numpy as jnp
from jax import lax
from jax.experimental import pallas as pl
from jax.experimental.pallas import tpu as pltpu
from jax.sharding import PartitionSpec as P

KVH = 4
DH = 128
GROUP = 8
CAP = 2
COEF = math.log2(math.e) / math.sqrt(DH)
LOW = -1e30
ROWS = 256


SMEM = pl.BlockSpec(memory_space=pltpu.SMEM)
VMEM = pl.BlockSpec(memory_space=pltpu.VMEM)
ANY = pl.BlockSpec(memory_space=pl.ANY)
HBM = pl.BlockSpec(memory_space=pltpu.HBM)


def columns_from(first, count):
    return pl.ds(pl.multiple_of(first * DH, DH), count * DH)


def pick_kernel(tables_ref, store_ref, out_ref, table, table_sem, sems):
    pools, _, listed = tables_ref.shape
    load = pltpu.make_async_copy(tables_ref, table, table_sem)
    load.start()
    load.wait()

    def page_copy(request, slot, page):
        return pltpu.make_async_copy(
            store_ref.at[page], out_ref.at[request, slot], sems.at[request, slot]
        )

    def serve(request, carry):
        def visit(entry, state):
            rank, pages = state
            page = table[request, 0, entry]
            hit = page >= 0
            pages = [jnp.where(hit & (rank == slot), page, pages[slot]) for slot in range(CAP)]
            return rank + hit.astype(jnp.int32), pages

        state = (jnp.int32(0), [jnp.int32(0)] * CAP)
        _, pages = lax.fori_loop(0, listed, visit, state, unroll=listed <= 8)
        for slot in range(CAP):
            page_copy(request, slot, pages[slot]).start()
        return carry

    lax.fori_loop(0, pools, serve, 0)

    def finish(request, carry):
        for slot in range(CAP):
            page_copy(request, slot, 0).wait()
        return carry

    lax.fori_loop(0, pools, finish, 0)


def pick_pages(place, tables, kv_store, rows):
    pools = tables.shape[0]
    shape = (kv_store.shape[0], rows, DH)
    keys = lax.dynamic_slice(kv_store, (0, place[3] * rows, place[2] * DH), shape)
    values = lax.dynamic_slice(kv_store, (0, place[3] * rows, (KVH + place[2]) * DH), shape)
    own = jnp.concatenate([keys, values], axis=2)
    return pl.pallas_call(
        pick_kernel,
        in_specs=[ANY, VMEM],
        out_specs=HBM,
        out_shape=pltpu.HBM((pools, CAP, rows, 2 * DH), kv_store.dtype),
        scratch_shapes=[
            pltpu.SMEM(tables.shape, jnp.int32),
            pltpu.SemaphoreType.DMA,
            pltpu.SemaphoreType.DMA((pools, CAP)),
        ],
        name="pick_pages",
    )(tables, in_vmem(own))


def in_vmem(array):
    return pltpu.with_memory_space_constraint(array, pltpu.VMEM)


def order_kernel(owners_ref, fetched_ref, out_ref, sems):
    listed = out_ref.shape[0]
    copies = []
    for entry in range(listed):
        owner = owners_ref[0, entry]
        rank = jnp.int32(0)
        for earlier in range(entry):
            rank += (owners_ref[0, earlier] == owner).astype(jnp.int32)
        rank = jnp.minimum(rank, CAP - 1)
        copies.append(
            pltpu.make_async_copy(fetched_ref.at[owner, rank], out_ref.at[entry], sems.at[entry])
        )
        copies[-1].start()
    for copy in copies:
        copy.wait()


def order_pages(owners, fetched):
    listed = owners.shape[1]
    rows = fetched.shape[2]
    return pl.pallas_call(
        order_kernel,
        in_specs=[SMEM, HBM],
        out_specs=VMEM,
        out_shape=pltpu.VMEM((listed, rows, 2 * DH), fetched.dtype),
        scratch_shapes=[pltpu.SemaphoreType.DMA((listed,))],
        name="order_pages",
    )(owners, pltpu.with_memory_space_constraint(fetched, pltpu.HBM))


def scores_of(query_ref, first, count, keys):
    heads = [query_ref[:, (first + j) * DH : (first + j + 1) * DH] for j in range(count)]
    stacked = heads[0] if count == 1 else jnp.concatenate(heads, axis=0)
    return lax.dot_general(
        stacked, keys, (((1,), (1,)), ((), ())), preferred_element_type=jnp.float32
    )


def with_ones(values):
    return jnp.concatenate([values, jnp.ones((values.shape[0], DH), values.dtype)], axis=1)


def span_kernel(place_ref, query_ref, keys_ref, values_ref, mean_ref, level_ref, copy_ref):
    q_rows = query_ref.shape[0]
    count = ROWS // q_rows
    length = keys_ref.shape[0]
    copy_ref[0] = query_ref[...]
    keys = keys_ref[...]
    values = with_ones(values_ref[...])
    query_pos = place_ref[1] * q_rows + lax.broadcasted_iota(jnp.int32, (q_rows, length), 0)
    allowed = lax.broadcasted_iota(jnp.int32, (q_rows, length), 1) <= query_pos
    bias = jnp.where(allowed, 0.0, LOW)
    bias = jnp.concatenate([bias] * count, axis=0)
    for first in range(0, GROUP, count):
        scores = scores_of(query_ref, first, count, keys) + bias
        top = jnp.max(scores, axis=1, keepdims=True)
        weights = jnp.exp2((scores - top) * COEF)
        summed = jnp.dot(
            weights.astype(jnp.bfloat16), values, preferred_element_type=jnp.float32
        )
        total = summed[:, DH:]
        level = top * COEF + jnp.log2(total)
        mean = summed[:, :DH] / total
        for j in range(count):
            at = slice(j * q_rows, (j + 1) * q_rows)
            columns = slice((first + j) * DH, (first + j + 1) * DH)
            mean_ref[0, :, columns] = mean[at]
            level_ref[0, :, columns] = level[at]


def attend_span(place, queries, span):
    q_rows = queries.shape[0]
    length = span.shape[0]
    wide = GROUP * DH
    spec = pltpu.PrefetchScalarGridSpec(
        num_scalar_prefetch=1,
        grid=(KVH,),
        in_specs=[
            pl.BlockSpec((q_rows, wide), lambda m, place: (0, place[2] ^ m)),
            pl.BlockSpec((length, DH), lambda m, place: (0, place[2] ^ m)),
            pl.BlockSpec((length, DH), lambda m, place: (0, KVH + (place[2] ^ m))),
        ],
        out_specs=[
            pl.BlockSpec((1, q_rows, wide), lambda m, place: (m, 0, 0)),
            pl.BlockSpec((1, q_rows, wide), lambda m, place: (m, 0, 0)),
            pl.BlockSpec((1, q_rows, wide), lambda m, place: (m, 0, 0)),
        ],
    )
    return pl.pallas_call(
        span_kernel,
        grid_spec=spec,
        out_shape=[
            pltpu.VMEM((KVH, q_rows, wide), jnp.float32),
            pltpu.VMEM((KVH, q_rows, wide), jnp.float32),
            pltpu.VMEM((KVH, q_rows, wide), jnp.bfloat16),
        ],
        cost_estimate=pl.CostEstimate(
            flops=4 * q_rows * KVH * wide * length, bytes_accessed=8 * 2**20, transcendentals=0
        ),
        compiler_params=pltpu.CompilerParams(vmem_limit_bytes=48 * 2**20),
        name="attend_span",
    )(place, queries, span, span)


def prefix_kernel(mask, parts, place_ref, limit_ref, *refs):
    pieces = refs[:parts]
    query_ref, mean_ref, level_ref, *_, out_ref, done_ref, sems = refs[parts:]
    q_rows = query_ref.shape[1]
    count = ROWS // q_rows
    head = jnp.bitwise_xor(place_ref[2], mask)
    listed, rows, _ = pieces[0].shape
    length = listed * rows
    both = [piece[...].reshape(length, 2 * DH) for piece in pieces]
    both = both[0] if parts == 1 else jnp.concatenate(both, axis=0)
    keys = both[:, :DH]
    values = with_ones(both[:, DH:])
    safe = length * 5 // 8 // DH * DH
    index = safe + lax.broadcasted_iota(jnp.int32, (1, length - safe), 1)
    at_page = lax.div(index, rows) * (parts * rows) + lax.rem(index, rows)
    biases = [
        jnp.where(at_page + lax.rem(place_ref[3] + step, parts) * rows < limit_ref[0], 0.0, LOW)
        for step in range(parts)
    ]
    copies = []
    for first in range(0, GROUP, count):
        raw = scores_of(query_ref.at[mask], first, count, keys)
        scores = []
        for step, bias in enumerate(biases):
            scores.append(raw[:, step * length : step * length + safe])
            scores.append(raw[:, step * length + safe : (step + 1) * length] + bias)
        scores = jnp.concatenate(scores, axis=1)
        heads = [slice((first + j) * DH, (first + j + 1) * DH) for j in range(count)]
        level = jnp.concatenate([level_ref[mask, :, columns] for columns in heads], axis=0)
        mean = jnp.concatenate([mean_ref[mask, :, columns] for columns in heads], axis=0)
        top = jnp.maximum(jnp.max(scores, axis=1, keepdims=True) * COEF, level)
        tops = jnp.concatenate([top] * (parts * length // DH), axis=1)
        weights = jnp.exp2(scores * COEF - tops)
        old = jnp.exp2(level - top)
        summed = jnp.dot(
            weights.astype(jnp.bfloat16), values, preferred_element_type=jnp.float32
        )
        result = (summed[:, :DH] + mean * old) / (summed[:, DH:] + old)
        for j, columns in enumerate(heads):
            done_ref[:, columns] = result[j * q_rows : (j + 1) * q_rows].astype(jnp.bfloat16)
        copies.append(
            pltpu.make_async_copy(
                done_ref.at[:, first * DH : (first + count) * DH],
                out_ref.at[:, columns_from(head * GROUP + first, count)],
                sems.at[first // count],
            )
        )
        copies[-1].start()
    for copy in copies:
        copy.wait()


def attend_prefix(place, limit, held, query, mean, level, partial, mask):
    _, q_rows, wide = query.shape
    parts = 2 * len(held) // KVH
    pieces = [held[mask + step * KVH] for step in range(parts)]
    length = parts * pieces[0].shape[0] * pieces[0].shape[1]
    return pl.pallas_call(
        functools.partial(prefix_kernel, mask, parts),
        in_specs=[SMEM, SMEM] + [VMEM] * (parts + 3) + [ANY] * len(partial),
        out_specs=ANY,
        out_shape=jax.ShapeDtypeStruct((q_rows, KVH * wide), jnp.bfloat16),
        scratch_shapes=[
            pltpu.VMEM((q_rows, wide), jnp.bfloat16),
            pltpu.SemaphoreType.DMA((GROUP * q_rows // ROWS,)),
        ],
        input_output_aliases={2 + parts + 3: 0} if partial else {},
        cost_estimate=pl.CostEstimate(
            flops=4 * q_rows * wide * length, bytes_accessed=2 * 2**20, transcendentals=0
        ),
        compiler_params=pltpu.CompilerParams(vmem_limit_bytes=48 * 2**20),
        name="attend_prefix",
    )(place, limit, *pieces, in_vmem(query), in_vmem(mean), in_vmem(level), *partial)


def swap(array, blks, mask):
    return lax.ppermute(array, "blk", [(i, i ^ mask) for i in range(blks)])


def per_device(queries, span_kv, kv_store, page_ids, page_owner, prefix_len):
    pools = lax.axis_size("pool")
    blks = lax.axis_size("blk")
    pool_at = lax.axis_index("pool")
    blk_at = lax.axis_index("blk")
    stored, page, _ = kv_store.shape
    parts = blks // KVH
    rows = page // parts
    place = jnp.stack([pool_at, blk_at, blk_at % KVH, blk_at // KVH]).astype(jnp.int32)

    owner = lax.broadcasted_iota(jnp.int32, (pools, 1, page_ids.shape[1]), 0)
    wanted = jnp.where(page_owner[None] == owner, page_ids[None], -1)
    tables = lax.all_to_all(wanted, "pool", split_axis=0, concat_axis=0, tiled=True)
    span = lax.all_gather(span_kv, "blk", axis=0, tiled=True)
    picked = pick_pages(place, tables, kv_store, rows)
    fetched = lax.all_to_all(picked, "pool", split_axis=0, concat_axis=0, tiled=True)
    state = attend_span(place, queries, span)
    fetched, *state = lax.optimization_barrier((fetched, *state))
    mean, level, query = state
    held = {0: order_pages(page_owner, fetched)}
    bit = blks // 2
    while bit > 1:
        held.update({mask ^ bit: swap(piece, blks, bit) for mask, piece in list(held.items())})
        bit //= 2
    near = {mask: piece for mask, piece in held.items() if mask & (KVH - 1) == 0}
    far = {mask: piece for mask, piece in held.items() if mask & (KVH - 1)}
    near.update({mask ^ 1: swap(piece, blks, 1) for mask, piece in list(near.items())})
    out = attend_prefix(place, prefix_len, near, query, mean, level, [], 0)
    out = attend_prefix(place, prefix_len, near, query, mean, level, [out], 1)
    far, out = lax.optimization_barrier((far, out))
    far.update({mask ^ 1: swap(piece, blks, 1) for mask, piece in list(far.items())})
    out = attend_prefix(place, prefix_len, far, query, mean, level, [out], 2)
    return attend_prefix(place, prefix_len, far, query, mean, level, [out], 3)


def solution(mesh):
    in_specs = (
        P(("pool", "blk"), None),
        P(("pool", "blk"), None),
        P("pool", None, None),
        P("pool", None),
        P("pool", None),
        P("pool"),
    )
    out_specs = P(("pool", "blk"), None)
    return jax.shard_map(
        per_device, mesh=mesh, in_specs=in_specs, out_specs=out_specs, check_vma=False
    )
```

```python
import functools
import math

import jax
import jax.numpy as jnp
from jax import lax
from jax.experimental import pallas as pl
from jax.experimental.pallas import tpu as pltpu
from jax.sharding import PartitionSpec as P

KVH = 4
DH = 128
GROUP = 8
CAP = 2
COEF = math.log2(math.e) / math.sqrt(DH)
LOW = -1e30
ROWS = 256


SMEM = pl.BlockSpec(memory_space=pltpu.SMEM)
VMEM = pl.BlockSpec(memory_space=pltpu.VMEM)
ANY = pl.BlockSpec(memory_space=pl.ANY)
HBM = pl.BlockSpec(memory_space=pltpu.HBM)


def columns_from(first, count):
    return pl.ds(pl.multiple_of(first * DH, DH), count * DH)


def pick_kernel(tables_ref, store_ref, out_ref, table, table_sem, sems):
    pools, _, listed = tables_ref.shape
    load = pltpu.make_async_copy(tables_ref, table, table_sem)
    load.start()
    load.wait()

    def page_copy(request, slot, page):
        return pltpu.make_async_copy(
            store_ref.at[page], out_ref.at[request, slot], sems.at[request, slot]
        )

    def serve(request, carry):
        def visit(entry, state):
            rank, pages = state
            page = table[request, 0, entry]
            hit = page >= 0
            pages = [jnp.where(hit & (rank == slot), page, pages[slot]) for slot in range(CAP)]
            return rank + hit.astype(jnp.int32), pages

        state = (jnp.int32(0), [jnp.int32(0)] * CAP)
        _, pages = lax.fori_loop(0, listed, visit, state, unroll=listed <= 8)
        for slot in range(CAP):
            page_copy(request, slot, pages[slot]).start()
        return carry

    lax.fori_loop(0, pools, serve, 0)

    def finish(request, carry):
        for slot in range(CAP):
            page_copy(request, slot, 0).wait()
        return carry

    lax.fori_loop(0, pools, finish, 0)


def pick_pages(place, tables, kv_store, rows):
    pools = tables.shape[0]
    shape = (kv_store.shape[0], rows, DH)
    keys = lax.dynamic_slice(kv_store, (0, place[3] * rows, place[2] * DH), shape)
    values = lax.dynamic_slice(kv_store, (0, place[3] * rows, (KVH + place[2]) * DH), shape)
    own = jnp.concatenate([keys, values], axis=2)
    return pl.pallas_call(
        pick_kernel,
        in_specs=[ANY, VMEM],
        out_specs=HBM,
        out_shape=pltpu.HBM((pools, CAP, rows, 2 * DH), kv_store.dtype),
        scratch_shapes=[
            pltpu.SMEM(tables.shape, jnp.int32),
            pltpu.SemaphoreType.DMA,
            pltpu.SemaphoreType.DMA((pools, CAP)),
        ],
        name="pick_pages",
    )(in_vmem(tables), in_vmem(own))


def in_vmem(array):
    return pltpu.with_memory_space_constraint(array, pltpu.VMEM)


def order_kernel(owners_ref, fetched_ref, out_ref, sems):
    listed = out_ref.shape[0]
    copies = []
    for entry in range(listed):
        owner = owners_ref[0, entry]
        rank = jnp.int32(0)
        for earlier in range(entry):
            rank += (owners_ref[0, earlier] == owner).astype(jnp.int32)
        rank = jnp.minimum(rank, CAP - 1)
        copies.append(
            pltpu.make_async_copy(fetched_ref.at[owner, rank], out_ref.at[entry], sems.at[entry])
        )
        copies[-1].start()
    for copy in copies:
        copy.wait()


def order_pages(owners, fetched):
    listed = owners.shape[1]
    rows = fetched.shape[2]
    return pl.pallas_call(
        order_kernel,
        in_specs=[SMEM, HBM],
        out_specs=VMEM,
        out_shape=pltpu.VMEM((listed, rows, 2 * DH), fetched.dtype),
        scratch_shapes=[pltpu.SemaphoreType.DMA((listed,))],
        name="order_pages",
    )(owners, pltpu.with_memory_space_constraint(fetched, pltpu.HBM))


def scores_of(query_ref, first, count, keys):
    heads = [query_ref[:, (first + j) * DH : (first + j + 1) * DH] for j in range(count)]
    stacked = heads[0] if count == 1 else jnp.concatenate(heads, axis=0)
    return lax.dot_general(
        stacked, keys, (((1,), (1,)), ((), ())), preferred_element_type=jnp.float32
    )


def with_ones(values):
    return jnp.concatenate([values, jnp.ones((values.shape[0], DH), values.dtype)], axis=1)


def span_kernel(masks, place_ref, query_ref, *refs):
    blocks = len(masks)
    keys_refs, values_refs = refs[:blocks], refs[blocks : 2 * blocks]
    mean_ref, level_ref, copy_ref = refs[2 * blocks :]
    q_rows = query_ref.shape[0]
    count = ROWS // q_rows
    copy_ref[0] = query_ref[...]
    keys = jnp.concatenate([ref[...] for ref in keys_refs], axis=0)
    values = with_ones(jnp.concatenate([ref[...] for ref in values_refs], axis=0))
    own = place_ref[1]
    ahead = lax.broadcasted_iota(jnp.int32, (q_rows, q_rows), 0) - lax.broadcasted_iota(
        jnp.int32, (q_rows, q_rows), 1
    )
    bias = [
        jnp.where(ahead >= (jnp.bitwise_xor(own, mask) - own) * q_rows, 0.0, LOW) for mask in masks
    ]
    bias = jnp.concatenate(bias, axis=1)
    bias = jnp.concatenate([bias] * count, axis=0)
    lanes = lax.broadcasted_iota(jnp.int32, (q_rows, DH), 1)
    levels = jnp.zeros((q_rows, DH), jnp.float32)
    for first in range(0, GROUP, count):
        scores = scores_of(query_ref, first, count, keys) + bias
        top = jnp.max(scores, axis=1, keepdims=True)
        weights = jnp.exp2((scores - top) * COEF)
        summed = jnp.dot(
            weights.astype(jnp.bfloat16), values, preferred_element_type=jnp.float32
        )
        total = summed[:, DH:]
        level = top * COEF + jnp.log2(total)
        mean = summed[:, :DH] / total
        for j in range(count):
            at = slice(j * q_rows, (j + 1) * q_rows)
            columns = slice((first + j) * DH, (first + j + 1) * DH)
            mean_ref[0, :, columns] = mean[at].astype(jnp.bfloat16)
            levels = jnp.where(lanes == first + j, level[at], levels)
    level_ref[0] = levels


def attend_span(place, queries, span):
    q_rows = queries.shape[0]
    masks = sorted(span)
    blocks = [span[mask] for mask in masks]
    wide = GROUP * DH
    keys_spec = pl.BlockSpec((q_rows, DH), lambda m, place: (0, place[2] ^ m))
    values_spec = pl.BlockSpec((q_rows, DH), lambda m, place: (0, KVH + (place[2] ^ m)))
    spec = pltpu.PrefetchScalarGridSpec(
        num_scalar_prefetch=1,
        grid=(KVH,),
        in_specs=[pl.BlockSpec((q_rows, wide), lambda m, place: (0, place[2] ^ m))]
        + [keys_spec] * len(masks)
        + [values_spec] * len(masks),
        out_specs=[
            pl.BlockSpec((1, q_rows, wide), lambda m, place: (m, 0, 0)),
            pl.BlockSpec((1, q_rows, DH), lambda m, place: (m, 0, 0)),
            pl.BlockSpec((1, q_rows, wide), lambda m, place: (m, 0, 0)),
        ],
    )
    return pl.pallas_call(
        functools.partial(span_kernel, masks),
        grid_spec=spec,
        out_shape=[
            pltpu.VMEM((KVH, q_rows, wide), jnp.bfloat16),
            pltpu.VMEM((KVH, q_rows, DH), jnp.float32),
            pltpu.VMEM((KVH, q_rows, wide), jnp.bfloat16),
        ],
        cost_estimate=pl.CostEstimate(
            flops=4 * q_rows * KVH * wide * q_rows * len(masks),
            bytes_accessed=8 * 2**20,
            transcendentals=0,
        ),
        compiler_params=pltpu.CompilerParams(vmem_limit_bytes=48 * 2**20),
        name="attend_span",
    )(place, queries, *blocks, *blocks)


def prefix_kernel(mask, parts, place_ref, limit_ref, *refs):
    pieces = refs[:parts]
    query_ref, mean_ref, level_ref, *_, out_ref, done_ref, sems = refs[parts:]
    q_rows = query_ref.shape[1]
    count = ROWS // q_rows
    head = jnp.bitwise_xor(place_ref[2], mask)
    listed, rows, _ = pieces[0].shape
    length = listed * rows
    both = [piece[...].reshape(length, 2 * DH) for piece in pieces]
    both = both[0] if parts == 1 else jnp.concatenate(both, axis=0)
    keys = both[:, :DH]
    values = with_ones(both[:, DH:])
    safe = length * 5 // 8 // DH * DH
    index = safe + lax.broadcasted_iota(jnp.int32, (1, length - safe), 1)
    at_page = lax.div(index, rows) * (parts * rows) + lax.rem(index, rows)
    biases = [
        jnp.where(at_page + lax.rem(place_ref[3] + step, parts) * rows < limit_ref[0], 0.0, LOW)
        for step in range(parts)
    ]
    copies = []
    for first in range(0, GROUP, count):
        raw = scores_of(query_ref.at[mask], first, count, keys)
        scores = []
        for step, bias in enumerate(biases):
            scores.append(raw[:, step * length : step * length + safe])
            scores.append(raw[:, step * length + safe : (step + 1) * length] + bias)
        scores = jnp.concatenate(scores, axis=1)
        heads = [slice((first + j) * DH, (first + j + 1) * DH) for j in range(count)]
        level = jnp.concatenate(
            [
                jnp.broadcast_to(level_ref[mask, :, first + j : first + j + 1], (q_rows, DH))
                for j in range(count)
            ],
            axis=0,
        )
        mean = jnp.concatenate([mean_ref[mask, :, columns] for columns in heads], axis=0)
        top = jnp.maximum(jnp.max(scores, axis=1, keepdims=True) * COEF, level)
        tops = jnp.concatenate([top] * (parts * length // DH), axis=1)
        weights = jnp.exp2(scores * COEF - tops)
        old = jnp.exp2(level - top)
        summed = jnp.dot(
            weights.astype(jnp.bfloat16), values, preferred_element_type=jnp.float32
        )
        result = (summed[:, :DH] + mean.astype(jnp.float32) * old) / (summed[:, DH:] + old)
        for j, columns in enumerate(heads):
            done_ref[:, columns] = result[j * q_rows : (j + 1) * q_rows].astype(jnp.bfloat16)
        copies.append(
            pltpu.make_async_copy(
                done_ref.at[:, first * DH : (first + count) * DH],
                out_ref.at[:, columns_from(head * GROUP + first, count)],
                sems.at[first // count],
            )
        )
        copies[-1].start()
    for copy in copies:
        copy.wait()


def attend_prefix(place, limit, held, query, mean, level, partial, mask):
    _, q_rows, wide = query.shape
    parts = 2 * len(held) // KVH
    pieces = [held[mask + step * KVH] for step in range(parts)]
    length = parts * pieces[0].shape[0] * pieces[0].shape[1]
    return pl.pallas_call(
        functools.partial(prefix_kernel, mask, parts),
        in_specs=[SMEM, SMEM] + [VMEM] * (parts + 3) + [ANY] * len(partial),
        out_specs=ANY,
        out_shape=jax.ShapeDtypeStruct((q_rows, KVH * wide), jnp.bfloat16),
        scratch_shapes=[
            pltpu.VMEM((q_rows, wide), jnp.bfloat16),
            pltpu.SemaphoreType.DMA((GROUP * q_rows // ROWS,)),
        ],
        input_output_aliases={2 + parts + 3: 0} if partial else {},
        cost_estimate=pl.CostEstimate(
            flops=4 * q_rows * wide * length, bytes_accessed=2 * 2**20, transcendentals=0
        ),
        compiler_params=pltpu.CompilerParams(vmem_limit_bytes=48 * 2**20),
        name="attend_prefix",
    )(place, limit, *pieces, in_vmem(query), in_vmem(mean), in_vmem(level), *partial)


def swap(array, blks, mask):
    return lax.ppermute(array, "blk", [(i, i ^ mask) for i in range(blks)])


def per_device(queries, span_kv, kv_store, page_ids, page_owner, prefix_len):
    pools = lax.axis_size("pool")
    blks = lax.axis_size("blk")
    pool_at = lax.axis_index("pool")
    blk_at = lax.axis_index("blk")
    stored, page, _ = kv_store.shape
    parts = blks // KVH
    rows = page // parts
    place = jnp.stack([pool_at, blk_at, blk_at % KVH, blk_at // KVH]).astype(jnp.int32)

    owner = lax.broadcasted_iota(jnp.int32, (pools, 1, page_ids.shape[1]), 0)
    wanted = jnp.where(page_owner[None] == owner, page_ids[None], -1)
    tables = lax.all_to_all(wanted, "pool", split_axis=0, concat_axis=0, tiled=True)
    picked = pick_pages(place, tables, kv_store, rows)
    picked, span_kv = lax.optimization_barrier((picked, span_kv))
    fetched = lax.all_to_all(picked, "pool", split_axis=0, concat_axis=0, tiled=True)
    span = {0: span_kv}
    bit = blks // 2
    while bit:
        span.update({mask ^ bit: swap(rows_of, blks, bit) for mask, rows_of in list(span.items())})
        bit //= 2
    state = attend_span(place, queries, span)
    fetched, *state = lax.optimization_barrier((fetched, *state))
    mean, level, query = state
    held = {0: order_pages(page_owner, fetched)}
    bit = blks // 2
    while bit > 1:
        held.update({mask ^ bit: swap(piece, blks, bit) for mask, piece in list(held.items())})
        bit //= 2
    near = {mask: piece for mask, piece in held.items() if mask & (KVH - 1) == 0}
    far = {mask: piece for mask, piece in held.items() if mask & (KVH - 1)}
    near.update({mask ^ 1: swap(piece, blks, 1) for mask, piece in list(near.items())})
    out = attend_prefix(place, prefix_len, near, query, mean, level, [], 0)
    out = attend_prefix(place, prefix_len, near, query, mean, level, [out], 1)
    far, out = lax.optimization_barrier((far, out))
    far.update({mask ^ 1: swap(piece, blks, 1) for mask, piece in list(far.items())})
    out = attend_prefix(place, prefix_len, far, query, mean, level, [out], 2)
    return attend_prefix(place, prefix_len, far, query, mean, level, [out], 3)


def solution(mesh):
    in_specs = (
        P(("pool", "blk"), None),
        P(("pool", "blk"), None),
        P("pool", None, None),
        P("pool", None),
        P("pool", None),
        P("pool"),
    )
    out_specs = P(("pool", "blk"), None)
    return jax.shard_map(
        per_device, mesh=mesh, in_specs=in_specs, out_specs=out_specs, check_vma=False
    )
```

```python
import functools
import math

import jax
import jax.numpy as jnp
from jax import lax
from jax.experimental import pallas as pl
from jax.experimental.pallas import tpu as pltpu
from jax.sharding import PartitionSpec as P

KVH = 4
DH = 128
GROUP = 8
CAP = 2
COEF = math.log2(math.e) / math.sqrt(DH)
LOW = -1e30
ROWS = 512


SMEM = pl.BlockSpec(memory_space=pltpu.SMEM)
VMEM = pl.BlockSpec(memory_space=pltpu.VMEM)
ANY = pl.BlockSpec(memory_space=pl.ANY)
HBM = pl.BlockSpec(memory_space=pltpu.HBM)


def columns_from(first, count):
    return pl.ds(pl.multiple_of(first * DH, DH), count * DH)


def pick_kernel(tables_ref, store_ref, out_ref, table, table_sem, sems):
    pools, _, listed = tables_ref.shape
    load = pltpu.make_async_copy(tables_ref, table, table_sem)
    load.start()
    load.wait()

    def page_copy(request, slot, page):
        return pltpu.make_async_copy(
            store_ref.at[page], out_ref.at[request, slot], sems.at[request, slot]
        )

    def serve(request, carry):
        def visit(entry, state):
            rank, pages = state
            page = table[request, 0, entry]
            hit = page >= 0
            pages = [jnp.where(hit & (rank == slot), page, pages[slot]) for slot in range(CAP)]
            return rank + hit.astype(jnp.int32), pages

        state = (jnp.int32(0), [jnp.int32(0)] * CAP)
        _, pages = lax.fori_loop(0, listed, visit, state, unroll=listed <= 8)
        for slot in range(CAP):
            page_copy(request, slot, pages[slot]).start()
        return carry

    lax.fori_loop(0, pools, serve, 0)

    def finish(request, carry):
        for slot in range(CAP):
            page_copy(request, slot, 0).wait()
        return carry

    lax.fori_loop(0, pools, finish, 0)


def pick_pages(place, tables, kv_store, rows):
    pools = tables.shape[0]
    shape = (kv_store.shape[0], rows, DH)
    keys = lax.dynamic_slice(kv_store, (0, place[3] * rows, place[2] * DH), shape)
    values = lax.dynamic_slice(kv_store, (0, place[3] * rows, (KVH + place[2]) * DH), shape)
    own = jnp.concatenate([keys, values], axis=2)
    return pl.pallas_call(
        pick_kernel,
        in_specs=[ANY, VMEM],
        out_specs=HBM,
        out_shape=pltpu.HBM((pools, CAP, rows, 2 * DH), kv_store.dtype),
        scratch_shapes=[
            pltpu.SMEM(tables.shape, jnp.int32),
            pltpu.SemaphoreType.DMA,
            pltpu.SemaphoreType.DMA((pools, CAP)),
        ],
        name="pick_pages",
    )(in_vmem(tables), in_vmem(own))


def in_vmem(array):
    return pltpu.with_memory_space_constraint(array, pltpu.VMEM)


def order_kernel(owners_ref, fetched_ref, out_ref, sems):
    listed = out_ref.shape[0]
    copies = []
    for entry in range(listed):
        owner = owners_ref[0, entry]
        rank = jnp.int32(0)
        for earlier in range(entry):
            rank += (owners_ref[0, earlier] == owner).astype(jnp.int32)
        rank = jnp.minimum(rank, CAP - 1)
        copies.append(
            pltpu.make_async_copy(fetched_ref.at[owner, rank], out_ref.at[entry], sems.at[entry])
        )
        copies[-1].start()
    for copy in copies:
        copy.wait()


def order_pages(owners, fetched):
    listed = owners.shape[1]
    rows = fetched.shape[2]
    return pl.pallas_call(
        order_kernel,
        in_specs=[SMEM, HBM],
        out_specs=VMEM,
        out_shape=pltpu.VMEM((listed, rows, 2 * DH), fetched.dtype),
        scratch_shapes=[pltpu.SemaphoreType.DMA((listed,))],
        name="order_pages",
    )(owners, pltpu.with_memory_space_constraint(fetched, pltpu.HBM))


def scores_of(query_ref, first, count, keys):
    heads = [query_ref[:, (first + j) * DH : (first + j + 1) * DH] for j in range(count)]
    stacked = heads[0] if count == 1 else jnp.concatenate(heads, axis=0)
    return lax.dot_general(
        stacked, keys, (((1,), (1,)), ((), ())), preferred_element_type=jnp.float32
    )


def with_ones(values):
    return jnp.concatenate([values, jnp.ones((values.shape[0], DH), values.dtype)], axis=1)


def span_kernel(masks, place_ref, query_ref, *refs):
    blocks = len(masks)
    keys_refs, values_refs = refs[:blocks], refs[blocks : 2 * blocks]
    mean_ref, level_ref, copy_ref = refs[2 * blocks :]
    q_rows = query_ref.shape[0]
    count = ROWS // q_rows
    copy_ref[0] = query_ref[...]
    keys = jnp.concatenate([ref[...] for ref in keys_refs], axis=0)
    values = with_ones(jnp.concatenate([ref[...] for ref in values_refs], axis=0))
    own = place_ref[1]
    ahead = lax.broadcasted_iota(jnp.int32, (q_rows, q_rows), 0) - lax.broadcasted_iota(
        jnp.int32, (q_rows, q_rows), 1
    )
    bias = [
        jnp.where(ahead >= (jnp.bitwise_xor(own, mask) - own) * q_rows, 0.0, LOW) for mask in masks
    ]
    bias = jnp.concatenate(bias, axis=1)
    bias = jnp.concatenate([bias] * count, axis=0)
    lanes = lax.broadcasted_iota(jnp.int32, (q_rows, DH), 1)
    levels = jnp.zeros((q_rows, DH), jnp.float32)
    for first in range(0, GROUP, count):
        scores = scores_of(query_ref, first, count, keys) + bias
        top = jnp.max(scores, axis=1, keepdims=True)
        weights = jnp.exp2((scores - top) * COEF)
        summed = jnp.dot(
            weights.astype(jnp.bfloat16), values, preferred_element_type=jnp.float32
        )
        total = summed[:, DH:]
        level = top * COEF + jnp.log2(total)
        mean = summed[:, :DH] / total
        for j in range(count):
            at = slice(j * q_rows, (j + 1) * q_rows)
            columns = slice((first + j) * DH, (first + j + 1) * DH)
            mean_ref[0, :, columns] = mean[at].astype(jnp.bfloat16)
            levels = jnp.where(lanes == first + j, level[at], levels)
    level_ref[0] = levels


def attend_span(place, queries, span):
    q_rows = queries.shape[0]
    masks = sorted(span)
    blocks = [span[mask] for mask in masks]
    wide = GROUP * DH
    keys_spec = pl.BlockSpec((q_rows, DH), lambda m, place: (0, place[2] ^ m))
    values_spec = pl.BlockSpec((q_rows, DH), lambda m, place: (0, KVH + (place[2] ^ m)))
    spec = pltpu.PrefetchScalarGridSpec(
        num_scalar_prefetch=1,
        grid=(KVH,),
        in_specs=[pl.BlockSpec((q_rows, wide), lambda m, place: (0, place[2] ^ m))]
        + [keys_spec] * len(masks)
        + [values_spec] * len(masks),
        out_specs=[
            pl.BlockSpec((1, q_rows, wide), lambda m, place: (m, 0, 0)),
            pl.BlockSpec((1, q_rows, DH), lambda m, place: (m, 0, 0)),
            pl.BlockSpec((1, q_rows, wide), lambda m, place: (m, 0, 0)),
        ],
    )
    return pl.pallas_call(
        functools.partial(span_kernel, masks),
        grid_spec=spec,
        out_shape=[
            pltpu.VMEM((KVH, q_rows, wide), jnp.bfloat16),
            pltpu.VMEM((KVH, q_rows, DH), jnp.float32),
            pltpu.VMEM((KVH, q_rows, wide), jnp.bfloat16),
        ],
        cost_estimate=pl.CostEstimate(
            flops=4 * q_rows * KVH * wide * q_rows * len(masks),
            bytes_accessed=8 * 2**20,
            transcendentals=0,
        ),
        compiler_params=pltpu.CompilerParams(vmem_limit_bytes=48 * 2**20),
        name="attend_span",
    )(place, pltpu.with_memory_space_constraint(queries, pltpu.HBM), *blocks, *blocks)


def prefix_kernel(mask, parts, place_ref, *refs):
    pieces = refs[:parts]
    query_ref, mean_ref, level_ref, *_, out_ref, done_ref, sems = refs[parts:]
    q_rows = query_ref.shape[1]
    count = ROWS // q_rows
    head = jnp.bitwise_xor(place_ref[2], mask)
    listed, rows, _ = pieces[0].shape
    length = listed * rows
    both = [piece[...].reshape(length, 2 * DH) for piece in pieces]
    both = both[0] if parts == 1 else jnp.concatenate(both, axis=0)
    keys = both[:, :DH]
    values = with_ones(both[:, DH:])
    safe = length * 5 // 8 // DH * DH
    index = safe + lax.broadcasted_iota(jnp.int32, (1, length - safe), 1)
    at_page = lax.div(index, rows) * (parts * rows) + lax.rem(index, rows)
    biases = [
        jnp.where(at_page + lax.rem(place_ref[3] + step, parts) * rows < place_ref[0], 0.0, LOW)
        for step in range(parts)
    ]
    copies = []
    for first in range(0, GROUP, count):
        raw = scores_of(query_ref.at[mask], first, count, keys)
        scores = []
        for step, bias in enumerate(biases):
            scores.append(raw[:, step * length : step * length + safe])
            scores.append(raw[:, step * length + safe : (step + 1) * length] + bias)
        scores = jnp.concatenate(scores, axis=1)
        heads = [slice((first + j) * DH, (first + j + 1) * DH) for j in range(count)]
        level = jnp.concatenate(
            [
                jnp.broadcast_to(level_ref[mask, :, first + j : first + j + 1], (q_rows, DH))
                for j in range(count)
            ],
            axis=0,
        )
        mean = jnp.concatenate([mean_ref[mask, :, columns] for columns in heads], axis=0)
        top = jnp.maximum(jnp.max(scores, axis=1, keepdims=True) * COEF, level)
        tops = jnp.concatenate([top] * (parts * length // DH), axis=1)
        weights = jnp.exp2(scores * COEF - tops)
        old = jnp.exp2(level - top)
        summed = jnp.dot(
            weights.astype(jnp.bfloat16), values, preferred_element_type=jnp.float32
        )
        result = (summed[:, :DH] + mean.astype(jnp.float32) * old) / (summed[:, DH:] + old)
        for j, columns in enumerate(heads):
            done_ref[:, columns] = result[j * q_rows : (j + 1) * q_rows].astype(jnp.bfloat16)
        copies.append(
            pltpu.make_async_copy(
                done_ref.at[:, first * DH : (first + count) * DH],
                out_ref.at[:, columns_from(head * GROUP + first, count)],
                sems.at[first // count],
            )
        )
        copies[-1].start()
    for copy in copies:
        copy.wait()


def attend_prefix(place, held, query, mean, level, partial, mask):
    _, q_rows, wide = query.shape
    pieces = [held[at] for at in sorted(held) if at % KVH == mask]
    parts = len(pieces)
    length = parts * pieces[0].shape[0] * pieces[0].shape[1]
    return pl.pallas_call(
        functools.partial(prefix_kernel, mask, parts),
        in_specs=[SMEM] + [VMEM] * (parts + 3) + [ANY] * len(partial),
        out_specs=ANY,
        out_shape=jax.ShapeDtypeStruct((q_rows, KVH * wide), jnp.bfloat16),
        scratch_shapes=[
            pltpu.VMEM((q_rows, wide), jnp.bfloat16),
            pltpu.SemaphoreType.DMA((GROUP * q_rows // ROWS,)),
        ],
        input_output_aliases={1 + parts + 3: 0} if partial else {},
        cost_estimate=pl.CostEstimate(
            flops=4 * q_rows * wide * length, bytes_accessed=2 * 2**20, transcendentals=0
        ),
        compiler_params=pltpu.CompilerParams(vmem_limit_bytes=48 * 2**20),
        name="attend_prefix",
    )(place, *pieces, in_vmem(query), in_vmem(mean), in_vmem(level), *partial)


def swap(array, blks, mask):
    return lax.ppermute(array, "blk", [(i, i ^ mask) for i in range(blks)])


def per_device(queries, span_kv, kv_store, page_ids, page_owner, prefix_len):
    pools = lax.axis_size("pool")
    blks = lax.axis_size("blk")
    blk_at = lax.axis_index("blk")
    stored, page, _ = kv_store.shape
    parts = blks // KVH
    rows = page // parts
    place = jnp.stack([prefix_len[0], blk_at, blk_at % KVH, blk_at // KVH]).astype(jnp.int32)

    owner = lax.broadcasted_iota(jnp.int32, (pools, 1, page_ids.shape[1]), 0)
    wanted = jnp.where(page_owner[None] == owner, page_ids[None], -1)
    tables = lax.all_to_all(wanted, "pool", split_axis=0, concat_axis=0, tiled=True)
    picked = pick_pages(place, tables, kv_store, rows)
    picked, span_kv = lax.optimization_barrier((picked, span_kv))
    fetched = lax.all_to_all(picked, "pool", split_axis=0, concat_axis=0, tiled=True)
    span = {0: span_kv}
    bit = blks // 2
    while bit:
        span.update({mask ^ bit: swap(rows_of, blks, bit) for mask, rows_of in list(span.items())})
        bit //= 2
    state = attend_span(place, queries, span)
    fetched, *state = lax.optimization_barrier((fetched, *state))
    mean, level, query = state
    held = {0: order_pages(page_owner, fetched)}
    bit = blks // 2
    while bit > 1:
        held.update({mask ^ bit: swap(piece, blks, bit) for mask, piece in list(held.items())})
        bit //= 2
    near = {mask: piece for mask, piece in held.items() if mask & (KVH - 1) == 0}
    far = {mask: piece for mask, piece in held.items() if mask & (KVH - 1)}
    out = attend_prefix(place, near, query, mean, level, [], 0)
    near, out = lax.optimization_barrier((near, out))
    near.update({mask ^ 1: swap(piece, blks, 1) for mask, piece in list(near.items())})
    out = attend_prefix(place, near, query, mean, level, [out], 1)
    far, out = lax.optimization_barrier((far, out))
    far.update({mask ^ 1: swap(piece, blks, 1) for mask, piece in list(far.items())})
    out = attend_prefix(place, far, query, mean, level, [out], 2)
    return attend_prefix(place, far, query, mean, level, [out], 3)


def solution(mesh):
    in_specs = (
        P(("pool", "blk"), None),
        P(("pool", "blk"), None),
        P("pool", None, None),
        P("pool", None),
        P("pool", None),
        P("pool"),
    )
    out_specs = P(("pool", "blk"), None)
    return jax.shard_map(
        per_device, mesh=mesh, in_specs=in_specs, out_specs=out_specs, check_vma=False
    )
```

```python
import functools
import math

import jax
import jax.numpy as jnp
from jax import lax
from jax.experimental import pallas as pl
from jax.experimental.pallas import tpu as pltpu
from jax.sharding import PartitionSpec as P

KVH = 4
DH = 128
GROUP = 8
CAP = 2
COEF = math.log2(math.e) / math.sqrt(DH)
LOW = -1e30
ROWS = 128


SMEM = pl.BlockSpec(memory_space=pltpu.SMEM)
VMEM = pl.BlockSpec(memory_space=pltpu.VMEM)
ANY = pl.BlockSpec(memory_space=pl.ANY)


def columns_from(first, count):
    return pl.ds(pl.multiple_of(first * DH, DH), count * DH)


def pick_kernel(tables_ref, store_ref, out_ref, table, table_sem):
    pools, _, listed = tables_ref.shape
    load = pltpu.make_async_copy(tables_ref, table, table_sem)
    load.start()
    load.wait()

    def serve(request, carry):
        def visit(entry, state):
            rank, pages = state
            page = table[request, 0, entry]
            hit = page >= 0
            pages = [jnp.where(hit & (rank == slot), page, pages[slot]) for slot in range(CAP)]
            return rank + hit.astype(jnp.int32), pages

        state = (jnp.int32(0), [jnp.int32(0)] * CAP)
        _, pages = lax.fori_loop(0, listed, visit, state, unroll=listed <= 8)
        for slot in range(CAP):
            out_ref[request, slot] = store_ref[pages[slot]]
        return carry

    lax.fori_loop(0, pools, serve, 0)


def pick_pages(place, tables, kv_store, rows):
    pools = tables.shape[0]
    shape = (kv_store.shape[0], rows, DH)
    keys = lax.dynamic_slice(kv_store, (0, place[3] * rows, place[2] * DH), shape)
    values = lax.dynamic_slice(kv_store, (0, place[3] * rows, (KVH + place[2]) * DH), shape)
    own = jnp.concatenate([keys, values], axis=2)
    return pl.pallas_call(
        pick_kernel,
        in_specs=[ANY, VMEM],
        out_specs=VMEM,
        out_shape=pltpu.VMEM((pools, CAP, rows, 2 * DH), kv_store.dtype),
        scratch_shapes=[pltpu.SMEM(tables.shape, jnp.int32), pltpu.SemaphoreType.DMA],
        name="pick_pages",
    )(in_vmem(tables), in_vmem(own))


def in_vmem(array):
    return pltpu.with_memory_space_constraint(array, pltpu.VMEM)


def order_kernel(owners_ref, fetched_ref, out_ref):
    for entry in range(out_ref.shape[0]):
        owner = owners_ref[0, entry]
        rank = jnp.int32(0)
        for earlier in range(entry):
            rank += (owners_ref[0, earlier] == owner).astype(jnp.int32)
        out_ref[entry] = fetched_ref[owner, jnp.minimum(rank, CAP - 1)]


def order_pages(owners, fetched):
    listed = owners.shape[1]
    rows = fetched.shape[2]
    return pl.pallas_call(
        order_kernel,
        in_specs=[SMEM, VMEM],
        out_specs=VMEM,
        out_shape=pltpu.VMEM((listed, rows, 2 * DH), fetched.dtype),
        name="order_pages",
    )(owners, in_vmem(fetched))


def scores_of(query_ref, first, count, keys):
    heads = [query_ref[:, (first + j) * DH : (first + j + 1) * DH] for j in range(count)]
    stacked = heads[0] if count == 1 else jnp.concatenate(heads, axis=0)
    return lax.dot_general(
        stacked, keys, (((1,), (1,)), ((), ())), preferred_element_type=jnp.float32
    )


def with_ones(values):
    return jnp.concatenate([values, jnp.ones((values.shape[0], DH), values.dtype)], axis=1)


def span_kernel(masks, place_ref, query_ref, *refs):
    blocks = len(masks)
    keys_refs, values_refs = refs[:blocks], refs[blocks : 2 * blocks]
    mean_ref, level_ref, copy_ref = refs[2 * blocks :]
    q_rows = query_ref.shape[0]
    count = ROWS // q_rows
    copy_ref[0] = query_ref[...]
    keys = jnp.concatenate([ref[...] for ref in keys_refs], axis=0)
    values = with_ones(jnp.concatenate([ref[...] for ref in values_refs], axis=0))
    own = place_ref[1]
    ahead = lax.broadcasted_iota(jnp.int32, (q_rows, q_rows), 0) - lax.broadcasted_iota(
        jnp.int32, (q_rows, q_rows), 1
    )
    bias = [
        jnp.where(ahead >= (jnp.bitwise_xor(own, mask) - own) * q_rows, 0.0, LOW) for mask in masks
    ]
    bias = jnp.concatenate(bias, axis=1)
    bias = jnp.concatenate([bias] * count, axis=0)
    lanes = lax.broadcasted_iota(jnp.int32, (q_rows, DH), 1)
    levels = jnp.zeros((q_rows, DH), jnp.float32)
    for first in range(0, GROUP, count):
        scores = scores_of(query_ref, first, count, keys) + bias
        top = jnp.max(scores, axis=1, keepdims=True)
        weights = jnp.exp2((scores - top) * COEF)
        summed = jnp.dot(
            weights.astype(jnp.bfloat16), values, preferred_element_type=jnp.float32
        )
        total = summed[:, DH:]
        level = top * COEF + jnp.log2(total)
        mean = summed[:, :DH] / total
        for j in range(count):
            at = slice(j * q_rows, (j + 1) * q_rows)
            columns = slice((first + j) * DH, (first + j + 1) * DH)
            mean_ref[0, :, columns] = mean[at].astype(jnp.bfloat16)
            levels = jnp.where(lanes == first + j, level[at], levels)
    level_ref[0] = levels


def attend_span(place, queries, span):
    q_rows = queries.shape[0]
    masks = sorted(span)
    blocks = [span[mask] for mask in masks]
    wide = GROUP * DH
    keys_spec = pl.BlockSpec((q_rows, DH), lambda m, place: (0, place[2] ^ m))
    values_spec = pl.BlockSpec((q_rows, DH), lambda m, place: (0, KVH + (place[2] ^ m)))
    spec = pltpu.PrefetchScalarGridSpec(
        num_scalar_prefetch=1,
        grid=(KVH,),
        in_specs=[pl.BlockSpec((q_rows, wide), lambda m, place: (0, place[2] ^ m))]
        + [keys_spec] * len(masks)
        + [values_spec] * len(masks),
        out_specs=[
            pl.BlockSpec((1, q_rows, wide), lambda m, place: (m, 0, 0)),
            pl.BlockSpec((1, q_rows, DH), lambda m, place: (m, 0, 0)),
            pl.BlockSpec((1, q_rows, wide), lambda m, place: (m, 0, 0)),
        ],
    )
    return pl.pallas_call(
        functools.partial(span_kernel, masks),
        grid_spec=spec,
        out_shape=[
            pltpu.VMEM((KVH, q_rows, wide), jnp.bfloat16),
            pltpu.VMEM((KVH, q_rows, DH), jnp.float32),
            pltpu.VMEM((KVH, q_rows, wide), jnp.bfloat16),
        ],
        cost_estimate=pl.CostEstimate(
            flops=4 * q_rows * KVH * wide * q_rows * len(masks),
            bytes_accessed=8 * 2**20,
            transcendentals=0,
        ),
        compiler_params=pltpu.CompilerParams(vmem_limit_bytes=48 * 2**20),
        name="attend_span",
    )(place, pltpu.with_memory_space_constraint(queries, pltpu.HBM), *blocks, *blocks)


def prefix_kernel(mask, parts, place_ref, *refs):
    pieces = refs[:parts]
    query_ref, mean_ref, level_ref, *_, out_ref, done_ref, sems = refs[parts:]
    q_rows = query_ref.shape[1]
    count = ROWS // q_rows
    head = jnp.bitwise_xor(place_ref[2], mask)
    listed, rows, _ = pieces[0].shape
    length = listed * rows
    both = [piece[...].reshape(length, 2 * DH) for piece in pieces]
    both = both[0] if parts == 1 else jnp.concatenate(both, axis=0)
    keys = both[:, :DH]
    values = with_ones(both[:, DH:])
    safe = length * 5 // 8 // DH * DH
    index = safe + lax.broadcasted_iota(jnp.int32, (1, length - safe), 1)
    at_page = lax.div(index, rows) * (parts * rows) + lax.rem(index, rows)
    biases = [
        jnp.where(at_page + lax.rem(place_ref[3] + step, parts) * rows < place_ref[0], 0.0, LOW)
        for step in range(parts)
    ]
    copies = []
    for first in range(0, GROUP, count):
        raw = scores_of(query_ref.at[mask], first, count, keys)
        scores = []
        for step, bias in enumerate(biases):
            scores.append(raw[:, step * length : step * length + safe])
            scores.append(raw[:, step * length + safe : (step + 1) * length] + bias)
        scores = jnp.concatenate(scores, axis=1)
        heads = [slice((first + j) * DH, (first + j + 1) * DH) for j in range(count)]
        level = jnp.concatenate(
            [
                jnp.broadcast_to(level_ref[mask, :, first + j : first + j + 1], (q_rows, DH))
                for j in range(count)
            ],
            axis=0,
        )
        mean = jnp.concatenate([mean_ref[mask, :, columns] for columns in heads], axis=0)
        top = jnp.maximum(jnp.max(scores, axis=1, keepdims=True) * COEF, level)
        tops = jnp.concatenate([top] * (parts * length // DH), axis=1)
        weights = jnp.exp2(scores * COEF - tops)
        old = jnp.exp2(level - top)
        summed = jnp.dot(
            weights.astype(jnp.bfloat16), values, preferred_element_type=jnp.float32
        )
        result = (summed[:, :DH] + mean.astype(jnp.float32) * old) / (summed[:, DH:] + old)
        for j, columns in enumerate(heads):
            done_ref[:, columns] = result[j * q_rows : (j + 1) * q_rows].astype(jnp.bfloat16)
        copies.append(
            pltpu.make_async_copy(
                done_ref.at[:, first * DH : (first + count) * DH],
                out_ref.at[:, columns_from(head * GROUP + first, count)],
                sems.at[first // count],
            )
        )
        copies[-1].start()
    for copy in copies:
        copy.wait()


def attend_prefix(place, held, query, mean, level, partial, mask):
    _, q_rows, wide = query.shape
    pieces = [held[at] for at in sorted(held) if at % KVH == mask]
    parts = len(pieces)
    length = parts * pieces[0].shape[0] * pieces[0].shape[1]
    return pl.pallas_call(
        functools.partial(prefix_kernel, mask, parts),
        in_specs=[SMEM] + [VMEM] * (parts + 3) + [ANY] * len(partial),
        out_specs=ANY,
        out_shape=jax.ShapeDtypeStruct((q_rows, KVH * wide), jnp.bfloat16),
        scratch_shapes=[
            pltpu.VMEM((q_rows, wide), jnp.bfloat16),
            pltpu.SemaphoreType.DMA((GROUP * q_rows // ROWS,)),
        ],
        input_output_aliases={1 + parts + 3: 0} if partial else {},
        cost_estimate=pl.CostEstimate(
            flops=4 * q_rows * wide * length, bytes_accessed=2 * 2**20, transcendentals=0
        ),
        compiler_params=pltpu.CompilerParams(vmem_limit_bytes=48 * 2**20),
        name="attend_prefix",
    )(place, *pieces, in_vmem(query), in_vmem(mean), in_vmem(level), *partial)


def swap(array, blks, mask):
    return lax.ppermute(array, "blk", [(i, i ^ mask) for i in range(blks)])


def per_device(queries, span_kv, kv_store, page_ids, page_owner, prefix_len):
    pools = lax.axis_size("pool")
    blks = lax.axis_size("blk")
    blk_at = lax.axis_index("blk")
    stored, page, _ = kv_store.shape
    parts = blks // KVH
    rows = page // parts
    place = jnp.stack([prefix_len[0], blk_at, blk_at % KVH, blk_at // KVH]).astype(jnp.int32)

    owner = lax.broadcasted_iota(jnp.int32, (pools, 1, page_ids.shape[1]), 0)
    wanted = jnp.where(page_owner[None] == owner, page_ids[None], -1)
    tables = lax.all_to_all(wanted, "pool", split_axis=0, concat_axis=0, tiled=True)
    picked = pick_pages(place, tables, kv_store, rows)
    picked, span_kv = lax.optimization_barrier((picked, span_kv))
    fetched = lax.all_to_all(picked, "pool", split_axis=0, concat_axis=0, tiled=True)
    span = {0: span_kv}
    bit = blks // 2
    while bit:
        span.update({mask ^ bit: swap(rows_of, blks, bit) for mask, rows_of in list(span.items())})
        bit //= 2
    state = attend_span(place, queries, span)
    fetched, *state = lax.optimization_barrier((fetched, *state))
    mean, level, query = state
    held = {0: order_pages(page_owner, fetched)}
    bit = blks // 2
    while bit > 1:
        held.update({mask ^ bit: swap(piece, blks, bit) for mask, piece in list(held.items())})
        bit //= 2
    near = {mask: piece for mask, piece in held.items() if mask & (KVH - 1) == 0}
    far = {mask: piece for mask, piece in held.items() if mask & (KVH - 1)}
    near.update({mask ^ 1: swap(piece, blks, 1) for mask, piece in list(near.items())})
    out = attend_prefix(place, near, query, mean, level, [], 0)
    out = attend_prefix(place, near, query, mean, level, [out], 1)
    far, out = lax.optimization_barrier((far, out))
    far.update({mask ^ 1: swap(piece, blks, 1) for mask, piece in list(far.items())})
    out = attend_prefix(place, far, query, mean, level, [out], 2)
    return attend_prefix(place, far, query, mean, level, [out], 3)


def solution(mesh):
    in_specs = (
        P(("pool", "blk"), None),
        P(("pool", "blk"), None),
        P("pool", None, None),
        P("pool", None),
        P("pool", None),
        P("pool"),
    )
    out_specs = P(("pool", "blk"), None)
    return jax.shard_map(
        per_device, mesh=mesh, in_specs=in_specs, out_specs=out_specs, check_vma=False
    )
```

```python
import functools
import math

import jax
import jax.numpy as jnp
from jax import lax
from jax.experimental import pallas as pl
from jax.experimental.pallas import tpu as pltpu
from jax.sharding import PartitionSpec as P

KVH = 4
DH = 128
GROUP = 8
CAP = 2
COEF = math.log2(math.e) / math.sqrt(DH)
LOW = -1e30
ROWS = 256


SMEM = pl.BlockSpec(memory_space=pltpu.SMEM)
VMEM = pl.BlockSpec(memory_space=pltpu.VMEM)
ANY = pl.BlockSpec(memory_space=pl.ANY)


def columns_from(first, count):
    return pl.ds(pl.multiple_of(first * DH, DH), count * DH)


def pick_kernel(place_ref, tables_ref, store_ref, out_ref, table, own, sems):
    pools, _, listed = tables_ref.shape
    rows = own.shape[1]
    at_rows = pl.ds(pl.multiple_of(place_ref[3] * rows, rows), rows)
    head = place_ref[2]
    loads = [
        pltpu.make_async_copy(tables_ref, table, sems.at[0]),
        pltpu.make_async_copy(
            store_ref.at[:, at_rows, columns_from(head, 1)], own.at[:, :, :DH], sems.at[1]
        ),
        pltpu.make_async_copy(
            store_ref.at[:, at_rows, columns_from(KVH + head, 1)], own.at[:, :, DH:], sems.at[2]
        ),
    ]
    for load in loads:
        load.start()
    for load in loads:
        load.wait()

    def serve(request, carry):
        def visit(entry, state):
            rank, pages = state
            page = table[request, 0, entry]
            hit = page >= 0
            pages = [jnp.where(hit & (rank == slot), page, pages[slot]) for slot in range(CAP)]
            return rank + hit.astype(jnp.int32), pages

        state = (jnp.int32(0), [jnp.int32(0)] * CAP)
        _, pages = lax.fori_loop(0, listed, visit, state, unroll=listed <= 8)
        for slot in range(CAP):
            out_ref[request, slot] = own[pages[slot]]
        return carry

    lax.fori_loop(0, pools, serve, 0)


def pick_pages(place, tables, kv_store, rows):
    pools = tables.shape[0]
    return pl.pallas_call(
        pick_kernel,
        in_specs=[SMEM, ANY, ANY],
        out_specs=VMEM,
        out_shape=pltpu.VMEM((pools, CAP, rows, 2 * DH), kv_store.dtype),
        scratch_shapes=[
            pltpu.SMEM(tables.shape, jnp.int32),
            pltpu.VMEM((kv_store.shape[0], rows, 2 * DH), kv_store.dtype),
            pltpu.SemaphoreType.DMA((3,)),
        ],
        name="pick_pages",
    )(place, in_vmem(tables), in_hbm(kv_store))


def in_hbm(array):
    return pltpu.with_memory_space_constraint(array, pltpu.HBM)


def in_vmem(array):
    return pltpu.with_memory_space_constraint(array, pltpu.VMEM)


def order_kernel(owners_ref, fetched_ref, out_ref):
    for entry in range(out_ref.shape[0]):
        owner = owners_ref[0, entry]
        rank = jnp.int32(0)
        for earlier in range(entry):
            rank += (owners_ref[0, earlier] == owner).astype(jnp.int32)
        out_ref[entry] = fetched_ref[owner, jnp.minimum(rank, CAP - 1)]


def order_pages(owners, fetched):
    listed = owners.shape[1]
    rows = fetched.shape[2]
    return pl.pallas_call(
        order_kernel,
        in_specs=[SMEM, VMEM],
        out_specs=VMEM,
        out_shape=pltpu.VMEM((listed, rows, 2 * DH), fetched.dtype),
        name="order_pages",
    )(owners, in_vmem(fetched))


def scores_of(query_ref, first, count, keys):
    heads = [query_ref[:, (first + j) * DH : (first + j + 1) * DH] for j in range(count)]
    stacked = heads[0] if count == 1 else jnp.concatenate(heads, axis=0)
    return lax.dot_general(
        stacked, keys, (((1,), (1,)), ((), ())), preferred_element_type=jnp.float32
    )


def with_ones(values):
    return jnp.concatenate([values, jnp.ones((values.shape[0], DH), values.dtype)], axis=1)


def span_kernel(masks, parts, rows, place_ref, query_ref, *refs):
    blocks = len(masks)
    keys_refs, values_refs = refs[:blocks], refs[blocks : 2 * blocks]
    mean_ref, level_ref, copy_ref, bias_ref = refs[2 * blocks :]
    q_rows = query_ref.shape[0]
    count = ROWS // q_rows
    copy_ref[0] = query_ref[...]
    shape = (bias_ref.shape[0], bias_ref.shape[1] // parts)
    index = lax.broadcasted_iota(jnp.int32, shape, 1)
    at_page = lax.div(index, rows) * (parts * rows) + lax.rem(index, rows)
    for step in range(parts):
        position = at_page + lax.rem(place_ref[3] + step, parts) * rows
        bias_ref[:, step * shape[1] : (step + 1) * shape[1]] = jnp.where(
            position < place_ref[0], 0.0, LOW
        )
    keys = jnp.concatenate([ref[...] for ref in keys_refs], axis=0)
    values = with_ones(jnp.concatenate([ref[...] for ref in values_refs], axis=0))
    own = place_ref[1]
    ahead = lax.broadcasted_iota(jnp.int32, (q_rows, q_rows), 0) - lax.broadcasted_iota(
        jnp.int32, (q_rows, q_rows), 1
    )
    bias = [
        jnp.where(ahead >= (jnp.bitwise_xor(own, mask) - own) * q_rows, 0.0, LOW) for mask in masks
    ]
    bias = jnp.concatenate(bias, axis=1)
    bias = jnp.concatenate([bias] * count, axis=0)
    lanes = lax.broadcasted_iota(jnp.int32, (q_rows, DH), 1)
    levels = jnp.zeros((q_rows, DH), jnp.float32)
    for first in range(0, GROUP, count):
        scores = scores_of(query_ref, first, count, keys) + bias
        top = jnp.max(scores, axis=1, keepdims=True)
        weights = jnp.exp2((scores - top) * COEF)
        summed = jnp.dot(
            weights.astype(jnp.bfloat16), values, preferred_element_type=jnp.float32
        )
        total = summed[:, DH:]
        level = top * COEF + jnp.log2(total)
        mean = summed[:, :DH] / total
        for j in range(count):
            at = slice(j * q_rows, (j + 1) * q_rows)
            columns = slice((first + j) * DH, (first + j + 1) * DH)
            mean_ref[0, :, columns] = mean[at].astype(jnp.bfloat16)
            levels = jnp.where(lanes == first + j, level[at], levels)
    level_ref[0] = levels


def attend_span(place, queries, span, length, parts, rows):
    q_rows = queries.shape[0]
    masks = sorted(span)
    blocks = [span[mask] for mask in masks]
    wide = GROUP * DH
    keys_spec = pl.BlockSpec((q_rows, DH), lambda m, place: (0, place[2] ^ m))
    values_spec = pl.BlockSpec((q_rows, DH), lambda m, place: (0, KVH + (place[2] ^ m)))
    spec = pltpu.PrefetchScalarGridSpec(
        num_scalar_prefetch=1,
        grid=(KVH,),
        in_specs=[pl.BlockSpec((q_rows, wide), lambda m, place: (0, place[2] ^ m))]
        + [keys_spec] * len(masks)
        + [values_spec] * len(masks),
        out_specs=[
            pl.BlockSpec((1, q_rows, wide), lambda m, place: (m, 0, 0)),
            pl.BlockSpec((1, q_rows, DH), lambda m, place: (m, 0, 0)),
            pl.BlockSpec((1, q_rows, wide), lambda m, place: (m, 0, 0)),
            pl.BlockSpec((8, length), lambda m, place: (0, 0)),
        ],
    )
    return pl.pallas_call(
        functools.partial(span_kernel, masks, parts, rows),
        grid_spec=spec,
        out_shape=[
            pltpu.VMEM((KVH, q_rows, wide), jnp.bfloat16),
            pltpu.VMEM((KVH, q_rows, DH), jnp.float32),
            pltpu.VMEM((KVH, q_rows, wide), jnp.bfloat16),
            pltpu.VMEM((8, length), jnp.float32),
        ],
        cost_estimate=pl.CostEstimate(
            flops=4 * q_rows * KVH * wide * q_rows * len(masks),
            bytes_accessed=8 * 2**20,
            transcendentals=0,
        ),
        compiler_params=pltpu.CompilerParams(vmem_limit_bytes=48 * 2**20),
        name="attend_span",
    )(place, in_hbm(queries), *blocks, *blocks)


def prefix_kernel(mask, parts, *refs):
    pieces = refs[:parts]
    query_ref, mean_ref, level_ref, bias_ref, *_, out_ref, done_ref, sems = refs[parts:]
    q_rows = query_ref.shape[1]
    count = ROWS // q_rows
    head = jnp.bitwise_xor(lax.rem(lax.axis_index("blk"), KVH), mask)
    listed, rows, _ = pieces[0].shape
    length = listed * rows
    both = [piece[...].reshape(length, 2 * DH) for piece in pieces]
    both = both[0] if parts == 1 else jnp.concatenate(both, axis=0)
    keys = both[:, :DH]
    values = with_ones(both[:, DH:])
    safe = length * 5 // 8 // DH * DH
    biases = [bias_ref[:1, step * length + safe : (step + 1) * length] for step in range(parts)]
    copies = []
    for first in range(0, GROUP, count):
        raw = scores_of(query_ref.at[mask], first, count, keys)
        scores = []
        for step, bias in enumerate(biases):
            scores.append(raw[:, step * length : step * length + safe])
            scores.append(raw[:, step * length + safe : (step + 1) * length] + bias)
        scores = jnp.concatenate(scores, axis=1)
        heads = [slice((first + j) * DH, (first + j + 1) * DH) for j in range(count)]
        level = jnp.concatenate(
            [
                jnp.broadcast_to(level_ref[mask, :, first + j : first + j + 1], (q_rows, DH))
                for j in range(count)
            ],
            axis=0,
        )
        mean = jnp.concatenate([mean_ref[mask, :, columns] for columns in heads], axis=0)
        top = jnp.maximum(jnp.max(scores, axis=1, keepdims=True) * COEF, level)
        tops = jnp.concatenate([top] * (parts * length // DH), axis=1)
        weights = jnp.exp2(scores * COEF - tops)
        old = jnp.exp2(level - top)
        summed = jnp.dot(
            weights.astype(jnp.bfloat16), values, preferred_element_type=jnp.float32
        )
        result = (summed[:, :DH] + mean.astype(jnp.float32) * old) / (summed[:, DH:] + old)
        for j, columns in enumerate(heads):
            done_ref[:, columns] = result[j * q_rows : (j + 1) * q_rows].astype(jnp.bfloat16)
        copies.append(
            pltpu.make_async_copy(
                done_ref.at[:, first * DH : (first + count) * DH],
                out_ref.at[:, columns_from(head * GROUP + first, count)],
                sems.at[first // count],
            )
        )
        copies[-1].start()
    for copy in copies:
        copy.wait()


def attend_prefix(held, state, partial, mask):
    _, q_rows, wide = state[0].shape
    pieces = [held[at] for at in sorted(held) if at % KVH == mask]
    parts = len(pieces)
    length = parts * pieces[0].shape[0] * pieces[0].shape[1]
    return pl.pallas_call(
        functools.partial(prefix_kernel, mask, parts),
        in_specs=[VMEM] * (parts + len(state)) + [ANY] * len(partial),
        out_specs=ANY,
        out_shape=jax.ShapeDtypeStruct((q_rows, KVH * wide), jnp.bfloat16),
        scratch_shapes=[
            pltpu.VMEM((q_rows, wide), jnp.bfloat16),
            pltpu.SemaphoreType.DMA((GROUP * q_rows // ROWS,)),
        ],
        input_output_aliases={parts + len(state): 0} if partial else {},
        cost_estimate=pl.CostEstimate(
            flops=4 * q_rows * wide * length, bytes_accessed=2 * 2**20, transcendentals=0
        ),
        compiler_params=pltpu.CompilerParams(vmem_limit_bytes=48 * 2**20),
        name="attend_prefix",
    )(*pieces, *[in_vmem(array) for array in state], *partial)


def swap(array, blks, mask):
    return lax.ppermute(array, "blk", [(i, i ^ mask) for i in range(blks)])


def per_device(queries, span_kv, kv_store, page_ids, page_owner, prefix_len):
    pools = lax.axis_size("pool")
    blks = lax.axis_size("blk")
    blk_at = lax.axis_index("blk")
    stored, page, _ = kv_store.shape
    parts = blks // KVH
    rows = page // parts
    place = jnp.stack([prefix_len[0], blk_at, blk_at % KVH, blk_at // KVH]).astype(jnp.int32)

    owner = lax.broadcasted_iota(jnp.int32, (pools, 1, page_ids.shape[1]), 0)
    wanted = jnp.where(page_owner[None] == owner, page_ids[None], -1)
    tables = lax.all_to_all(wanted, "pool", split_axis=0, concat_axis=0, tiled=True)
    picked = pick_pages(place, tables, kv_store, rows)
    picked, span_kv = lax.optimization_barrier((picked, span_kv))
    fetched = lax.all_to_all(picked, "pool", split_axis=0, concat_axis=0, tiled=True)
    span = {0: span_kv}
    bit = blks // 2
    while bit:
        span.update({mask ^ bit: swap(rows_of, blks, bit) for mask, rows_of in list(span.items())})
        bit //= 2
    length = page_ids.shape[1] * page
    state = attend_span(place, queries, span, length, parts, rows)
    fetched, *state = lax.optimization_barrier((fetched, *state))
    mean, level, query, bias = state
    state = (query, mean, level, bias)
    held = {0: order_pages(page_owner, fetched)}
    bit = blks // 2
    while bit > 1:
        held.update({mask ^ bit: swap(piece, blks, bit) for mask, piece in list(held.items())})
        bit //= 2
    near = {mask: piece for mask, piece in held.items() if mask & (KVH - 1) == 0}
    far = {mask: piece for mask, piece in held.items() if mask & (KVH - 1)}
    near.update({mask ^ 1: swap(piece, blks, 1) for mask, piece in list(near.items())})
    out = attend_prefix(near, state, [], 0)
    out = attend_prefix(near, state, [out], 1)
    far, out = lax.optimization_barrier((far, out))
    far.update({mask ^ 1: swap(piece, blks, 1) for mask, piece in list(far.items())})
    out = attend_prefix(far, state, [out], 2)
    return attend_prefix(far, state, [out], 3)


def solution(mesh):
    in_specs = (
        P(("pool", "blk"), None),
        P(("pool", "blk"), None),
        P("pool", None, None),
        P("pool", None),
        P("pool", None),
        P("pool"),
    )
    out_specs = P(("pool", "blk"), None)
    return jax.shard_map(
        per_device, mesh=mesh, in_specs=in_specs, out_specs=out_specs, check_vma=False
    )
```

```python
import functools
import math

import jax
import jax.numpy as jnp
from jax import lax
from jax.experimental import pallas as pl
from jax.experimental.pallas import tpu as pltpu
from jax.sharding import PartitionSpec as P

KVH = 4
DH = 128
GROUP = 8
CAP = 2
COEF = math.log2(math.e) / math.sqrt(DH)
LOW = -1e30
ROWS = 256


SMEM = pl.BlockSpec(memory_space=pltpu.SMEM)
VMEM = pl.BlockSpec(memory_space=pltpu.VMEM)
ANY = pl.BlockSpec(memory_space=pl.ANY)


def columns_from(first, count):
    return pl.ds(pl.multiple_of(first * DH, DH), count * DH)


def pick_kernel(tables_ref, store_ref, out_ref, table, table_sem, sems):
    pools, _, listed = tables_ref.shape
    rows = out_ref.shape[2]
    load = pltpu.make_async_copy(tables_ref, table, table_sem)
    load.start()
    own = lax.axis_index("blk")
    head = lax.rem(own, KVH)
    at_rows = pl.ds(pl.multiple_of(lax.div(own, KVH) * rows, rows), rows)
    load.wait()

    def page_copies(request, slot, page):
        return [
            pltpu.make_async_copy(
                store_ref.at[page, at_rows, columns_from(kind * KVH + head, 1)],
                out_ref.at[request, slot, :, kind * DH : (kind + 1) * DH],
                sems.at[request, slot, kind],
            )
            for kind in range(2)
        ]

    def serve(request, carry):
        def visit(entry, state):
            rank, pages = state
            page = table[request, 0, entry]
            hit = page >= 0
            pages = [jnp.where(hit & (rank == slot), page, pages[slot]) for slot in range(CAP)]
            return rank + hit.astype(jnp.int32), pages

        state = (jnp.int32(0), [jnp.int32(0)] * CAP)
        _, pages = lax.fori_loop(0, listed, visit, state, unroll=listed <= 8)
        for slot in range(CAP):
            for copy in page_copies(request, slot, pages[slot]):
                copy.start()
        return carry

    lax.fori_loop(0, pools, serve, 0)

    def finish(request, carry):
        for slot in range(CAP):
            for copy in page_copies(request, slot, 0):
                copy.wait()
        return carry

    lax.fori_loop(0, pools, finish, 0)


def pick_pages(tables, kv_store, rows):
    pools = tables.shape[0]
    return pl.pallas_call(
        pick_kernel,
        in_specs=[ANY, ANY],
        out_specs=ANY,
        out_shape=pltpu.HBM((pools, CAP, rows, 2 * DH), kv_store.dtype),
        scratch_shapes=[
            pltpu.SMEM(tables.shape, jnp.int32),
            pltpu.SemaphoreType.DMA,
            pltpu.SemaphoreType.DMA((pools, CAP, 2)),
        ],
        name="pick_pages",
    )(in_vmem(tables), in_vmem(kv_store))


def in_hbm(array):
    return pltpu.with_memory_space_constraint(array, pltpu.HBM)


def in_vmem(array):
    return pltpu.with_memory_space_constraint(array, pltpu.VMEM)


def order_kernel(owners_ref, fetched_ref, out_ref):
    for entry in range(out_ref.shape[0]):
        owner = owners_ref[0, entry]
        rank = jnp.int32(0)
        for earlier in range(entry):
            rank += (owners_ref[0, earlier] == owner).astype(jnp.int32)
        out_ref[entry] = fetched_ref[owner, jnp.minimum(rank, CAP - 1)]


def order_pages(owners, fetched):
    listed = owners.shape[1]
    rows = fetched.shape[2]
    return pl.pallas_call(
        order_kernel,
        in_specs=[SMEM, VMEM],
        out_specs=VMEM,
        out_shape=pltpu.VMEM((listed, rows, 2 * DH), fetched.dtype),
        name="order_pages",
    )(owners, in_vmem(fetched))


def scores_of(query_ref, first, count, keys):
    heads = [query_ref[:, (first + j) * DH : (first + j + 1) * DH] for j in range(count)]
    stacked = heads[0] if count == 1 else jnp.concatenate(heads, axis=0)
    return lax.dot_general(
        stacked, keys, (((1,), (1,)), ((), ())), preferred_element_type=jnp.float32
    )


def with_ones(values):
    return jnp.concatenate([values, jnp.ones((values.shape[0], DH), values.dtype)], axis=1)


def span_kernel(masks, parts, rows, place_ref, query_ref, *refs):
    blocks = len(masks)
    keys_refs, values_refs = refs[:blocks], refs[blocks : 2 * blocks]
    mean_ref, level_ref, copy_ref, bias_ref = refs[2 * blocks :]
    q_rows = query_ref.shape[0]
    count = ROWS // q_rows
    copy_ref[0] = query_ref[...]
    shape = (bias_ref.shape[0], bias_ref.shape[1] // parts)
    index = lax.broadcasted_iota(jnp.int32, shape, 1)
    at_page = lax.div(index, rows) * (parts * rows) + lax.rem(index, rows)
    for step in range(parts):
        position = at_page + lax.rem(place_ref[3] + step, parts) * rows
        bias_ref[:, step * shape[1] : (step + 1) * shape[1]] = jnp.where(
            position < place_ref[0], 0.0, LOW
        )
    keys = jnp.concatenate([ref[...] for ref in keys_refs], axis=0)
    values = with_ones(jnp.concatenate([ref[...] for ref in values_refs], axis=0))
    own = place_ref[1]
    ahead = lax.broadcasted_iota(jnp.int32, (q_rows, q_rows), 0) - lax.broadcasted_iota(
        jnp.int32, (q_rows, q_rows), 1
    )
    bias = [
        jnp.where(ahead >= (jnp.bitwise_xor(own, mask) - own) * q_rows, 0.0, LOW) for mask in masks
    ]
    bias = jnp.concatenate(bias, axis=1)
    bias = jnp.concatenate([bias] * count, axis=0)
    lanes = lax.broadcasted_iota(jnp.int32, (q_rows, DH), 1)
    levels = jnp.zeros((q_rows, DH), jnp.float32)
    for first in range(0, GROUP, count):
        scores = scores_of(query_ref, first, count, keys) + bias
        top = jnp.max(scores, axis=1, keepdims=True)
        weights = jnp.exp2((scores - top) * COEF)
        summed = jnp.dot(
            weights.astype(jnp.bfloat16), values, preferred_element_type=jnp.float32
        )
        total = summed[:, DH:]
        level = top * COEF + jnp.log2(total)
        mean = summed[:, :DH] / total
        for j in range(count):
            at = slice(j * q_rows, (j + 1) * q_rows)
            columns = slice((first + j) * DH, (first + j + 1) * DH)
            mean_ref[0, :, columns] = mean[at].astype(jnp.bfloat16)
            levels = jnp.where(lanes == first + j, level[at], levels)
    level_ref[0] = levels


def attend_span(place, queries, span, length, parts, rows):
    q_rows = queries.shape[0]
    masks = sorted(span)
    blocks = [span[mask] for mask in masks]
    wide = GROUP * DH
    keys_spec = pl.BlockSpec((q_rows, DH), lambda m, place: (0, place[2] ^ m))
    values_spec = pl.BlockSpec((q_rows, DH), lambda m, place: (0, KVH + (place[2] ^ m)))
    spec = pltpu.PrefetchScalarGridSpec(
        num_scalar_prefetch=1,
        grid=(KVH,),
        in_specs=[pl.BlockSpec((q_rows, wide), lambda m, place: (0, place[2] ^ m))]
        + [keys_spec] * len(masks)
        + [values_spec] * len(masks),
        out_specs=[
            pl.BlockSpec((1, q_rows, wide), lambda m, place: (m, 0, 0)),
            pl.BlockSpec((1, q_rows, DH), lambda m, place: (m, 0, 0)),
            pl.BlockSpec((1, q_rows, wide), lambda m, place: (m, 0, 0)),
            pl.BlockSpec((8, length), lambda m, place: (0, 0)),
        ],
    )
    return pl.pallas_call(
        functools.partial(span_kernel, masks, parts, rows),
        grid_spec=spec,
        out_shape=[
            pltpu.VMEM((KVH, q_rows, wide), jnp.bfloat16),
            pltpu.VMEM((KVH, q_rows, DH), jnp.float32),
            pltpu.VMEM((KVH, q_rows, wide), jnp.bfloat16),
            pltpu.VMEM((8, length), jnp.float32),
        ],
        cost_estimate=pl.CostEstimate(
            flops=4 * q_rows * KVH * wide * q_rows * len(masks),
            bytes_accessed=8 * 2**20,
            transcendentals=0,
        ),
        compiler_params=pltpu.CompilerParams(vmem_limit_bytes=48 * 2**20),
        name="attend_span",
    )(place, in_hbm(queries), *blocks, *blocks)


def prefix_kernel(mask, parts, *refs):
    pieces = refs[:parts]
    query_ref, mean_ref, level_ref, bias_ref, *_, out_ref, done_ref, sems = refs[parts:]
    q_rows = query_ref.shape[1]
    count = ROWS // q_rows
    head = jnp.bitwise_xor(lax.rem(lax.axis_index("blk"), KVH), mask)
    listed, rows, _ = pieces[0].shape
    length = listed * rows
    both = [piece[...].reshape(length, 2 * DH) for piece in pieces]
    both = both[0] if parts == 1 else jnp.concatenate(both, axis=0)
    keys = both[:, :DH]
    values = with_ones(both[:, DH:])
    safe = length * 5 // 8 // DH * DH
    biases = [bias_ref[:1, step * length + safe : (step + 1) * length] for step in range(parts)]
    copies = []
    for first in range(0, GROUP, count):
        raw = scores_of(query_ref.at[mask], first, count, keys)
        scores = []
        for step, bias in enumerate(biases):
            scores.append(raw[:, step * length : step * length + safe])
            scores.append(raw[:, step * length + safe : (step + 1) * length] + bias)
        scores = jnp.concatenate(scores, axis=1)
        heads = [slice((first + j) * DH, (first + j + 1) * DH) for j in range(count)]
        level = jnp.concatenate(
            [
                jnp.broadcast_to(level_ref[mask, :, first + j : first + j + 1], (q_rows, DH))
                for j in range(count)
            ],
            axis=0,
        )
        mean = jnp.concatenate([mean_ref[mask, :, columns] for columns in heads], axis=0)
        top = jnp.maximum(jnp.max(scores, axis=1, keepdims=True) * COEF, level)
        tops = jnp.concatenate([top] * (parts * length // DH), axis=1)
        weights = jnp.exp2(scores * COEF - tops)
        old = jnp.exp2(level - top)
        summed = jnp.dot(
            weights.astype(jnp.bfloat16), values, preferred_element_type=jnp.float32
        )
        result = (summed[:, :DH] + mean.astype(jnp.float32) * old) / (summed[:, DH:] + old)
        for j, columns in enumerate(heads):
            done_ref[:, columns] = result[j * q_rows : (j + 1) * q_rows].astype(jnp.bfloat16)
        copies.append(
            pltpu.make_async_copy(
                done_ref.at[:, first * DH : (first + count) * DH],
                out_ref.at[:, columns_from(head * GROUP + first, count)],
                sems.at[first // count],
            )
        )
        copies[-1].start()
    for copy in copies:
        copy.wait()


def attend_prefix(held, state, partial, mask):
    _, q_rows, wide = state[0].shape
    pieces = [held[at] for at in sorted(held) if at % KVH == mask]
    parts = len(pieces)
    length = parts * pieces[0].shape[0] * pieces[0].shape[1]
    return pl.pallas_call(
        functools.partial(prefix_kernel, mask, parts),
        in_specs=[VMEM] * (parts + len(state)) + [ANY] * len(partial),
        out_specs=ANY,
        out_shape=jax.ShapeDtypeStruct((q_rows, KVH * wide), jnp.bfloat16),
        scratch_shapes=[
            pltpu.VMEM((q_rows, wide), jnp.bfloat16),
            pltpu.SemaphoreType.DMA((GROUP * q_rows // ROWS,)),
        ],
        input_output_aliases={parts + len(state): 0} if partial else {},
        cost_estimate=pl.CostEstimate(
            flops=4 * q_rows * wide * length, bytes_accessed=2 * 2**20, transcendentals=0
        ),
        compiler_params=pltpu.CompilerParams(vmem_limit_bytes=48 * 2**20),
        name="attend_prefix",
    )(*pieces, *[in_vmem(array) for array in state], *partial)


def swap(array, blks, mask):
    return lax.ppermute(array, "blk", [(i, i ^ mask) for i in range(blks)])


def per_device(queries, span_kv, kv_store, page_ids, page_owner, prefix_len):
    pools = lax.axis_size("pool")
    blks = lax.axis_size("blk")
    blk_at = lax.axis_index("blk")
    stored, page, _ = kv_store.shape
    parts = blks // KVH
    rows = page // parts
    place = jnp.stack([prefix_len[0], blk_at, blk_at % KVH, blk_at // KVH]).astype(jnp.int32)

    owner = lax.broadcasted_iota(jnp.int32, (pools, 1, page_ids.shape[1]), 0)
    wanted = jnp.where(page_owner[None] == owner, page_ids[None], -1)
    tables = lax.all_to_all(wanted, "pool", split_axis=0, concat_axis=0, tiled=True)
    picked = pick_pages(tables, kv_store, rows)
    picked, span_kv = lax.optimization_barrier((picked, span_kv))
    fetched = lax.all_to_all(picked, "pool", split_axis=0, concat_axis=0, tiled=True)
    span = {0: span_kv}
    bit = blks // 2
    while bit:
        span.update({mask ^ bit: swap(rows_of, blks, bit) for mask, rows_of in list(span.items())})
        bit //= 2
    length = page_ids.shape[1] * page
    state = attend_span(place, queries, span, length, parts, rows)
    fetched, *state = lax.optimization_barrier((fetched, *state))
    mean, level, query, bias = state
    state = (query, mean, level, bias)
    held = {0: order_pages(page_owner, fetched)}
    bit = blks // 2
    while bit > 1:
        held.update({mask ^ bit: swap(piece, blks, bit) for mask, piece in list(held.items())})
        bit //= 2
    near = {mask: piece for mask, piece in held.items() if mask & (KVH - 1) == 0}
    far = {mask: piece for mask, piece in held.items() if mask & (KVH - 1)}
    near.update({mask ^ 1: swap(piece, blks, 1) for mask, piece in list(near.items())})
    out = attend_prefix(near, state, [], 0)
    out = attend_prefix(near, state, [out], 1)
    far, out = lax.optimization_barrier((far, out))
    far.update({mask ^ 1: swap(piece, blks, 1) for mask, piece in list(far.items())})
    out = attend_prefix(far, state, [out], 2)
    return attend_prefix(far, state, [out], 3)


def solution(mesh):
    in_specs = (
        P(("pool", "blk"), None),
        P(("pool", "blk"), None),
        P("pool", None, None),
        P("pool", None),
        P("pool", None),
        P("pool"),
    )
    out_specs = P(("pool", "blk"), None)
    return jax.shard_map(
        per_device, mesh=mesh, in_specs=in_specs, out_specs=out_specs, check_vma=False
    )
```

```python
import functools
import math

import jax
import jax.numpy as jnp
from jax import lax
from jax.experimental import pallas as pl
from jax.experimental.pallas import tpu as pltpu
from jax.sharding import PartitionSpec as P

KVH = 4
DH = 128
GROUP = 8
CAP = 2
COEF = math.log2(math.e) / math.sqrt(DH)
LOW = -1e30
ROWS = 256
LOADS = 4


SMEM = pl.BlockSpec(memory_space=pltpu.SMEM)
VMEM = pl.BlockSpec(memory_space=pltpu.VMEM)
ANY = pl.BlockSpec(memory_space=pl.ANY)


def columns_from(first, count):
    return pl.ds(pl.multiple_of(first * DH, DH), count * DH)


def pick_kernel(tables_ref, store_ref, out_ref, table, own, load_sems, sems):
    pools, _, listed = tables_ref.shape
    stored, rows, _ = own.shape
    blk = lax.axis_index("blk")
    head = lax.rem(blk, KVH)
    at_rows = pl.ds(pl.multiple_of(lax.div(blk, KVH) * rows, rows), rows)
    loads = [pltpu.make_async_copy(tables_ref, table, load_sems.at[0])]
    for kind in range(2):
        for first in range(0, stored, stored // LOADS):
            pages = slice(first, first + stored // LOADS)
            loads.append(
                pltpu.make_async_copy(
                    store_ref.at[pages, at_rows, columns_from(kind * KVH + head, 1)],
                    own.at[pages, :, kind * DH : (kind + 1) * DH],
                    load_sems.at[len(loads)],
                )
            )
    for load in loads:
        load.start()
    for load in loads:
        load.wait()

    def page_copy(request, slot, page):
        return pltpu.make_async_copy(
            own.at[page], out_ref.at[request, slot], sems.at[request, slot]
        )

    def serve(request, carry):
        def visit(entry, state):
            rank, pages = state
            page = table[request, 0, entry]
            hit = page >= 0
            pages = [jnp.where(hit & (rank == slot), page, pages[slot]) for slot in range(CAP)]
            return rank + hit.astype(jnp.int32), pages

        state = (jnp.int32(0), [jnp.int32(0)] * CAP)
        _, pages = lax.fori_loop(0, listed, visit, state, unroll=listed <= 8)
        for slot in range(CAP):
            page_copy(request, slot, pages[slot]).start()
        return carry

    lax.fori_loop(0, pools, serve, 0)

    def finish(request, carry):
        for slot in range(CAP):
            page_copy(request, slot, 0).wait()
        return carry

    lax.fori_loop(0, pools, finish, 0)


def pick_pages(tables, kv_store, rows):
    pools = tables.shape[0]
    return pl.pallas_call(
        pick_kernel,
        in_specs=[ANY, ANY],
        out_specs=ANY,
        out_shape=pltpu.HBM((pools, CAP, rows, 2 * DH), kv_store.dtype),
        scratch_shapes=[
            pltpu.SMEM(tables.shape, jnp.int32),
            pltpu.VMEM((kv_store.shape[0], rows, 2 * DH), kv_store.dtype),
            pltpu.SemaphoreType.DMA((1 + 2 * LOADS,)),
            pltpu.SemaphoreType.DMA((pools, CAP)),
        ],
        name="pick_pages",
    )(in_vmem(tables), in_hbm(kv_store))


def in_hbm(array):
    return pltpu.with_memory_space_constraint(array, pltpu.HBM)


def in_vmem(array):
    return pltpu.with_memory_space_constraint(array, pltpu.VMEM)


def order_kernel(owners_ref, fetched_ref, out_ref):
    for entry in range(out_ref.shape[0]):
        owner = owners_ref[0, entry]
        rank = jnp.int32(0)
        for earlier in range(entry):
            rank += (owners_ref[0, earlier] == owner).astype(jnp.int32)
        out_ref[entry] = fetched_ref[owner, jnp.minimum(rank, CAP - 1)]


def order_pages(owners, fetched):
    listed = owners.shape[1]
    rows = fetched.shape[2]
    return pl.pallas_call(
        order_kernel,
        in_specs=[SMEM, VMEM],
        out_specs=VMEM,
        out_shape=pltpu.VMEM((listed, rows, 2 * DH), fetched.dtype),
        name="order_pages",
    )(owners, in_vmem(fetched))


def scores_of(query_ref, first, count, keys):
    heads = [query_ref[:, (first + j) * DH : (first + j + 1) * DH] for j in range(count)]
    stacked = heads[0] if count == 1 else jnp.concatenate(heads, axis=0)
    return lax.dot_general(
        stacked, keys, (((1,), (1,)), ((), ())), preferred_element_type=jnp.float32
    )


def with_ones(values):
    return jnp.concatenate([values, jnp.ones((values.shape[0], DH), values.dtype)], axis=1)


def span_kernel(masks, parts, rows, limit_ref, query_ref, *refs):
    blocks = len(masks)
    keys_refs, values_refs = refs[:blocks], refs[blocks : 2 * blocks]
    mean_ref, level_ref, copy_ref, bias_ref = refs[2 * blocks :]
    q_rows = query_ref.shape[0]
    count = ROWS // q_rows
    copy_ref[0] = query_ref[...]
    own = lax.axis_index("blk")
    shape = (bias_ref.shape[0], bias_ref.shape[1] // parts)
    index = lax.broadcasted_iota(jnp.int32, shape, 1)
    at_page = lax.div(index, rows) * (parts * rows) + lax.rem(index, rows)
    for step in range(parts):
        position = at_page + lax.rem(lax.div(own, KVH) + step, parts) * rows
        bias_ref[:, step * shape[1] : (step + 1) * shape[1]] = jnp.where(
            position < limit_ref[0], 0.0, LOW
        )
    keys = jnp.concatenate([ref[...] for ref in keys_refs], axis=0)
    values = with_ones(jnp.concatenate([ref[...] for ref in values_refs], axis=0))
    ahead = lax.broadcasted_iota(jnp.int32, (q_rows, q_rows), 0) - lax.broadcasted_iota(
        jnp.int32, (q_rows, q_rows), 1
    )
    bias = [
        jnp.where(ahead >= (jnp.bitwise_xor(own, mask) - own) * q_rows, 0.0, LOW) for mask in masks
    ]
    bias = jnp.concatenate(bias, axis=1)
    bias = jnp.concatenate([bias] * count, axis=0)
    lanes = lax.broadcasted_iota(jnp.int32, (q_rows, DH), 1)
    levels = jnp.zeros((q_rows, DH), jnp.float32)
    for first in range(0, GROUP, count):
        scores = scores_of(query_ref, first, count, keys) + bias
        top = jnp.max(scores, axis=1, keepdims=True)
        weights = jnp.exp2((scores - top) * COEF)
        summed = jnp.dot(
            weights.astype(jnp.bfloat16), values, preferred_element_type=jnp.float32
        )
        total = summed[:, DH:]
        level = top * COEF + jnp.log2(total)
        mean = summed[:, :DH] / total
        for j in range(count):
            at = slice(j * q_rows, (j + 1) * q_rows)
            columns = slice((first + j) * DH, (first + j + 1) * DH)
            mean_ref[0, :, columns] = mean[at].astype(jnp.bfloat16)
            levels = jnp.where(lanes == first + j, level[at], levels)
    level_ref[0] = levels


def attend_span(limit, queries, span, length, parts, rows):
    q_rows = queries.shape[0]
    masks = sorted(span)
    blocks = [span[mask] for mask in masks]
    wide = GROUP * DH

    def head(m):
        return lax.rem(lax.axis_index("blk"), KVH) ^ m

    keys_spec = pl.BlockSpec((q_rows, DH), lambda m: (0, head(m)))
    values_spec = pl.BlockSpec((q_rows, DH), lambda m: (0, KVH + head(m)))
    return pl.pallas_call(
        functools.partial(span_kernel, masks, parts, rows),
        grid=(KVH,),
        in_specs=[SMEM, pl.BlockSpec((q_rows, wide), lambda m: (0, head(m)))]
        + [keys_spec] * len(masks)
        + [values_spec] * len(masks),
        out_specs=[
            pl.BlockSpec((1, q_rows, wide), lambda m: (m, 0, 0)),
            pl.BlockSpec((1, q_rows, DH), lambda m: (m, 0, 0)),
            pl.BlockSpec((1, q_rows, wide), lambda m: (m, 0, 0)),
            pl.BlockSpec((8, length), lambda m: (0, 0)),
        ],
        out_shape=[
            pltpu.VMEM((KVH, q_rows, wide), jnp.bfloat16),
            pltpu.VMEM((KVH, q_rows, DH), jnp.float32),
            pltpu.VMEM((KVH, q_rows, wide), jnp.bfloat16),
            pltpu.VMEM((8, length), jnp.float32),
        ],
        cost_estimate=pl.CostEstimate(
            flops=4 * q_rows * KVH * wide * q_rows * len(masks),
            bytes_accessed=8 * 2**20,
            transcendentals=0,
        ),
        compiler_params=pltpu.CompilerParams(vmem_limit_bytes=48 * 2**20),
        name="attend_span",
    )(limit, in_hbm(queries), *blocks, *blocks)


def prefix_kernel(mask, parts, *refs):
    pieces = refs[:parts]
    query_ref, mean_ref, level_ref, bias_ref, *_, out_ref, done_ref, sems = refs[parts:]
    q_rows = query_ref.shape[1]
    count = ROWS // q_rows
    head = jnp.bitwise_xor(lax.rem(lax.axis_index("blk"), KVH), mask)
    listed, rows, _ = pieces[0].shape
    length = listed * rows
    both = [piece[...].reshape(length, 2 * DH) for piece in pieces]
    both = both[0] if parts == 1 else jnp.concatenate(both, axis=0)
    keys = both[:, :DH]
    values = with_ones(both[:, DH:])
    safe = length * 5 // 8 // DH * DH
    biases = [bias_ref[:1, step * length + safe : (step + 1) * length] for step in range(parts)]
    copies = []
    for first in range(0, GROUP, count):
        raw = scores_of(query_ref.at[mask], first, count, keys)
        scores = []
        for step, bias in enumerate(biases):
            scores.append(raw[:, step * length : step * length + safe])
            scores.append(raw[:, step * length + safe : (step + 1) * length] + bias)
        scores = jnp.concatenate(scores, axis=1)
        heads = [slice((first + j) * DH, (first + j + 1) * DH) for j in range(count)]
        level = jnp.concatenate(
            [
                jnp.broadcast_to(level_ref[mask, :, first + j : first + j + 1], (q_rows, DH))
                for j in range(count)
            ],
            axis=0,
        )
        mean = jnp.concatenate([mean_ref[mask, :, columns] for columns in heads], axis=0)
        top = jnp.maximum(jnp.max(scores, axis=1, keepdims=True) * COEF, level)
        tops = jnp.concatenate([top] * (parts * length // DH), axis=1)
        weights = jnp.exp2(scores * COEF - tops)
        old = jnp.exp2(level - top)
        summed = jnp.dot(
            weights.astype(jnp.bfloat16), values, preferred_element_type=jnp.float32
        )
        result = (summed[:, :DH] + mean.astype(jnp.float32) * old) / (summed[:, DH:] + old)
        for j, columns in enumerate(heads):
            done_ref[:, columns] = result[j * q_rows : (j + 1) * q_rows].astype(jnp.bfloat16)
        copies.append(
            pltpu.make_async_copy(
                done_ref.at[:, first * DH : (first + count) * DH],
                out_ref.at[:, columns_from(head * GROUP + first, count)],
                sems.at[first // count],
            )
        )
        copies[-1].start()
    for copy in copies:
        copy.wait()


def attend_prefix(held, state, partial, mask):
    _, q_rows, wide = state[0].shape
    pieces = [held[at] for at in sorted(held) if at % KVH == mask]
    parts = len(pieces)
    length = parts * pieces[0].shape[0] * pieces[0].shape[1]
    return pl.pallas_call(
        functools.partial(prefix_kernel, mask, parts),
        in_specs=[VMEM] * (parts + len(state)) + [ANY] * len(partial),
        out_specs=ANY,
        out_shape=jax.ShapeDtypeStruct((q_rows, KVH * wide), jnp.bfloat16),
        scratch_shapes=[
            pltpu.VMEM((q_rows, wide), jnp.bfloat16),
            pltpu.SemaphoreType.DMA((GROUP * q_rows // ROWS,)),
        ],
        input_output_aliases={parts + len(state): 0} if partial else {},
        cost_estimate=pl.CostEstimate(
            flops=4 * q_rows * wide * length, bytes_accessed=2 * 2**20, transcendentals=0
        ),
        compiler_params=pltpu.CompilerParams(vmem_limit_bytes=48 * 2**20),
        name="attend_prefix",
    )(*pieces, *[in_vmem(array) for array in state], *partial)


def swap(array, blks, mask):
    return lax.ppermute(array, "blk", [(i, i ^ mask) for i in range(blks)])


def per_device(queries, span_kv, kv_store, page_ids, page_owner, prefix_len):
    pools = lax.axis_size("pool")
    blks = lax.axis_size("blk")
    stored, page, _ = kv_store.shape
    parts = blks // KVH
    rows = page // parts

    owner = lax.broadcasted_iota(jnp.int32, (pools, 1, page_ids.shape[1]), 0)
    wanted = jnp.where(page_owner[None] == owner, page_ids[None], -1)
    tables = lax.all_to_all(wanted, "pool", split_axis=0, concat_axis=0, tiled=True)
    picked = pick_pages(tables, kv_store, rows)
    picked, span_kv = lax.optimization_barrier((picked, span_kv))
    fetched = lax.all_to_all(picked, "pool", split_axis=0, concat_axis=0, tiled=True)
    span = {0: span_kv}
    bit = blks // 2
    while bit:
        span.update({mask ^ bit: swap(rows_of, blks, bit) for mask, rows_of in list(span.items())})
        bit //= 2
    length = page_ids.shape[1] * page
    state = attend_span(prefix_len, queries, span, length, parts, rows)
    fetched, *state = lax.optimization_barrier((fetched, *state))
    mean, level, query, bias = state
    state = (query, mean, level, bias)
    held = {0: order_pages(page_owner, fetched)}
    bit = blks // 2
    while bit > 1:
        held.update({mask ^ bit: swap(piece, blks, bit) for mask, piece in list(held.items())})
        bit //= 2
    near = {mask: piece for mask, piece in held.items() if mask & (KVH - 1) == 0}
    far = {mask: piece for mask, piece in held.items() if mask & (KVH - 1)}
    near.update({mask ^ 1: swap(piece, blks, 1) for mask, piece in list(near.items())})
    out = attend_prefix(near, state, [], 0)
    out = attend_prefix(near, state, [out], 1)
    far, out = lax.optimization_barrier((far, out))
    far.update({mask ^ 1: swap(piece, blks, 1) for mask, piece in list(far.items())})
    out = attend_prefix(far, state, [out], 2)
    return attend_prefix(far, state, [out], 3)


def solution(mesh):
    in_specs = (
        P(("pool", "blk"), None),
        P(("pool", "blk"), None),
        P("pool", None, None),
        P("pool", None),
        P("pool", None),
        P("pool"),
    )
    out_specs = P(("pool", "blk"), None)
    return jax.shard_map(
        per_device, mesh=mesh, in_specs=in_specs, out_specs=out_specs, check_vma=False
    )
```

```python
import functools
import math

import jax
import jax.numpy as jnp
from jax import lax
from jax.experimental import pallas as pl
from jax.experimental.pallas import tpu as pltpu
from jax.sharding import PartitionSpec as P

KVH = 4
DH = 128
GROUP = 8
CAP = 2
COEF = math.log2(math.e) / math.sqrt(DH)
LOW = -1e30
ROWS = 256
LOADS = 4


SMEM = pl.BlockSpec(memory_space=pltpu.SMEM)
VMEM = pl.BlockSpec(memory_space=pltpu.VMEM)
ANY = pl.BlockSpec(memory_space=pl.ANY)


def columns_from(first, count):
    return pl.ds(pl.multiple_of(first * DH, DH), count * DH)


def pick_kernel(tables_ref, store_ref, out_ref, table, own, load_sems, sems):
    pools, _, listed = tables_ref.shape
    stored, rows, _ = own.shape
    blk = lax.axis_index("blk")
    head = lax.rem(blk, KVH)
    at_rows = pl.ds(pl.multiple_of(lax.div(blk, KVH) * rows, rows), rows)
    loads = [pltpu.make_async_copy(tables_ref, table, load_sems.at[0])]
    for kind in range(2):
        for first in range(0, stored, stored // LOADS):
            pages = slice(first, first + stored // LOADS)
            loads.append(
                pltpu.make_async_copy(
                    store_ref.at[pages, at_rows, columns_from(kind * KVH + head, 1)],
                    own.at[pages, :, kind * DH : (kind + 1) * DH],
                    load_sems.at[len(loads)],
                )
            )
    for load in loads:
        load.start()
    for load in loads:
        load.wait()

    def page_copy(request, slot, page):
        return pltpu.make_async_copy(
            own.at[page], out_ref.at[request, slot], sems.at[request, slot]
        )

    def serve(request, carry):
        def visit(entry, state):
            rank, pages = state
            page = table[request, 0, entry]
            hit = page >= 0
            pages = [jnp.where(hit & (rank == slot), page, pages[slot]) for slot in range(CAP)]
            return rank + hit.astype(jnp.int32), pages

        state = (jnp.int32(0), [jnp.int32(0)] * CAP)
        _, pages = lax.fori_loop(0, listed, visit, state, unroll=listed <= 8)
        for slot in range(CAP):
            page_copy(request, slot, pages[slot]).start()
        return carry

    lax.fori_loop(0, pools, serve, 0)

    def finish(request, carry):
        for slot in range(CAP):
            page_copy(request, slot, 0).wait()
        return carry

    lax.fori_loop(0, pools, finish, 0)


def pick_pages(tables, kv_store, rows):
    pools = tables.shape[0]
    return pl.pallas_call(
        pick_kernel,
        in_specs=[ANY, ANY],
        out_specs=ANY,
        out_shape=pltpu.HBM((pools, CAP, rows, 2 * DH), kv_store.dtype),
        scratch_shapes=[
            pltpu.SMEM(tables.shape, jnp.int32),
            pltpu.VMEM((kv_store.shape[0], rows, 2 * DH), kv_store.dtype),
            pltpu.SemaphoreType.DMA((1 + 2 * LOADS,)),
            pltpu.SemaphoreType.DMA((pools, CAP)),
        ],
        name="pick_pages",
    )(in_vmem(tables), in_hbm(kv_store))


def in_hbm(array):
    return pltpu.with_memory_space_constraint(array, pltpu.HBM)


def in_vmem(array):
    return pltpu.with_memory_space_constraint(array, pltpu.VMEM)


def order_kernel(owners_ref, fetched_ref, out_ref):
    for entry in range(out_ref.shape[0]):
        owner = owners_ref[0, entry]
        rank = jnp.int32(0)
        for earlier in range(entry):
            rank += (owners_ref[0, earlier] == owner).astype(jnp.int32)
        out_ref[entry] = fetched_ref[owner, jnp.minimum(rank, CAP - 1)]


def order_pages(owners, fetched):
    listed = owners.shape[1]
    rows = fetched.shape[2]
    return pl.pallas_call(
        order_kernel,
        in_specs=[SMEM, VMEM],
        out_specs=VMEM,
        out_shape=pltpu.VMEM((listed, rows, 2 * DH), fetched.dtype),
        name="order_pages",
    )(owners, in_vmem(fetched))


def scores_of(query_ref, first, count, keys):
    heads = [query_ref[:, (first + j) * DH : (first + j + 1) * DH] for j in range(count)]
    stacked = heads[0] if count == 1 else jnp.concatenate(heads, axis=0)
    return lax.dot_general(
        stacked, keys, (((1,), (1,)), ((), ())), preferred_element_type=jnp.float32
    )


def with_ones(values):
    return jnp.concatenate([values, jnp.ones((values.shape[0], DH), values.dtype)], axis=1)


def span_kernel(masks, parts, rows, limit_ref, query_ref, *refs):
    blocks = len(masks)
    keys_refs, values_refs = refs[:blocks], refs[blocks : 2 * blocks]
    mean_ref, level_ref, copy_ref, bias_ref = refs[2 * blocks :]
    q_rows = query_ref.shape[0]
    count = ROWS // q_rows
    copy_ref[0] = query_ref[...]
    own = lax.axis_index("blk")
    shape = (bias_ref.shape[0], bias_ref.shape[1] // parts)
    index = lax.broadcasted_iota(jnp.int32, shape, 1)
    at_page = lax.div(index, rows) * (parts * rows) + lax.rem(index, rows)
    for step in range(parts):
        position = at_page + lax.rem(lax.div(own, KVH) + step, parts) * rows
        bias_ref[:, step * shape[1] : (step + 1) * shape[1]] = jnp.where(
            position < limit_ref[0], 0.0, LOW
        )
    keys = jnp.concatenate([ref[...] for ref in keys_refs], axis=0)
    values = with_ones(jnp.concatenate([ref[...] for ref in values_refs], axis=0))
    ahead = lax.broadcasted_iota(jnp.int32, (q_rows, q_rows), 0) - lax.broadcasted_iota(
        jnp.int32, (q_rows, q_rows), 1
    )
    bias = [
        jnp.where(ahead >= (jnp.bitwise_xor(own, mask) - own) * q_rows, 0.0, LOW) for mask in masks
    ]
    bias = jnp.concatenate(bias, axis=1)
    bias = jnp.concatenate([bias] * count, axis=0)
    lanes = lax.broadcasted_iota(jnp.int32, (q_rows, DH), 1)
    levels = jnp.zeros((q_rows, DH), jnp.float32)
    for first in range(0, GROUP, count):
        scores = scores_of(query_ref, first, count, keys) + bias
        top = jnp.max(scores, axis=1, keepdims=True)
        weights = jnp.exp2((scores - top) * COEF)
        summed = jnp.dot(
            weights.astype(jnp.bfloat16), values, preferred_element_type=jnp.float32
        )
        total = summed[:, DH:]
        level = top * COEF + jnp.log2(total)
        mean = summed[:, :DH] / total
        for j in range(count):
            at = slice(j * q_rows, (j + 1) * q_rows)
            columns = slice((first + j) * DH, (first + j + 1) * DH)
            mean_ref[0, :, columns] = mean[at].astype(jnp.bfloat16)
            levels = jnp.where(lanes == first + j, level[at], levels)
    level_ref[0] = levels


def attend_span(limit, queries, span, length, parts, rows):
    q_rows = queries.shape[0]
    masks = sorted(span)
    blocks = [span[mask] for mask in masks]
    wide = GROUP * DH

    def head(m):
        return lax.rem(lax.axis_index("blk"), KVH) ^ m

    keys_spec = pl.BlockSpec((q_rows, DH), lambda m: (0, head(m)))
    values_spec = pl.BlockSpec((q_rows, DH), lambda m: (0, KVH + head(m)))
    return pl.pallas_call(
        functools.partial(span_kernel, masks, parts, rows),
        grid=(KVH,),
        in_specs=[SMEM, pl.BlockSpec((q_rows, wide), lambda m: (0, head(m)))]
        + [keys_spec] * len(masks)
        + [values_spec] * len(masks),
        out_specs=[
            pl.BlockSpec((1, q_rows, wide), lambda m: (m, 0, 0)),
            pl.BlockSpec((1, q_rows, DH), lambda m: (m, 0, 0)),
            pl.BlockSpec((1, q_rows, wide), lambda m: (m, 0, 0)),
            pl.BlockSpec((8, length), lambda m: (0, 0)),
        ],
        out_shape=[
            pltpu.VMEM((KVH, q_rows, wide), jnp.bfloat16),
            pltpu.VMEM((KVH, q_rows, DH), jnp.float32),
            pltpu.VMEM((KVH, q_rows, wide), jnp.bfloat16),
            pltpu.VMEM((8, length), jnp.float32),
        ],
        cost_estimate=pl.CostEstimate(
            flops=4 * q_rows * KVH * wide * q_rows * len(masks),
            bytes_accessed=8 * 2**20,
            transcendentals=0,
        ),
        compiler_params=pltpu.CompilerParams(vmem_limit_bytes=48 * 2**20),
        name="attend_span",
    )(limit, in_hbm(queries), *blocks, *blocks)


def prefix_kernel(mask, parts, *refs):
    pieces = refs[:parts]
    query_ref, mean_ref, level_ref, bias_ref, *_, out_ref, done_ref, sems = refs[parts:]
    q_rows = query_ref.shape[1]
    count = ROWS // q_rows
    head = jnp.bitwise_xor(lax.rem(lax.axis_index("blk"), KVH), mask)
    listed, rows, _ = pieces[0].shape
    length = listed * rows
    both = [piece[...].reshape(length, 2 * DH) for piece in pieces]
    both = both[0] if parts == 1 else jnp.concatenate(both, axis=0)
    keys = both[:, :DH]
    values = with_ones(both[:, DH:])
    safe = length * 5 // 8 // DH * DH
    biases = [bias_ref[:1, step * length + safe : (step + 1) * length] for step in range(parts)]
    copies = []
    for first in range(0, GROUP, count):
        raw = scores_of(query_ref.at[mask], first, count, keys)
        scores = []
        for step, bias in enumerate(biases):
            scores.append(raw[:, step * length : step * length + safe])
            scores.append(raw[:, step * length + safe : (step + 1) * length] + bias)
        scores = jnp.concatenate(scores, axis=1)
        heads = [slice((first + j) * DH, (first + j + 1) * DH) for j in range(count)]
        level = jnp.concatenate(
            [
                jnp.broadcast_to(level_ref[mask, :, first + j : first + j + 1], (q_rows, DH))
                for j in range(count)
            ],
            axis=0,
        )
        mean = jnp.concatenate([mean_ref[mask, :, columns] for columns in heads], axis=0)
        top = jnp.maximum(jnp.max(scores, axis=1, keepdims=True) * COEF, level)
        tops = jnp.concatenate([top] * (parts * length // DH), axis=1)
        weights = jnp.exp2(scores * COEF - tops)
        old = jnp.exp2(level - top)
        summed = jnp.dot(
            weights.astype(jnp.bfloat16), values, preferred_element_type=jnp.float32
        )
        result = (summed[:, :DH] + mean.astype(jnp.float32) * old) / (summed[:, DH:] + old)
        for j, columns in enumerate(heads):
            done_ref[:, columns] = result[j * q_rows : (j + 1) * q_rows].astype(jnp.bfloat16)
        copies.append(
            pltpu.make_async_copy(
                done_ref.at[:, first * DH : (first + count) * DH],
                out_ref.at[:, columns_from(head * GROUP + first, count)],
                sems.at[first // count],
            )
        )
        copies[-1].start()
    for copy in copies:
        copy.wait()


def attend_prefix(held, state, partial, mask):
    _, q_rows, wide = state[0].shape
    pieces = [held[at] for at in sorted(held) if at % KVH == mask]
    parts = len(pieces)
    length = parts * pieces[0].shape[0] * pieces[0].shape[1]
    return pl.pallas_call(
        functools.partial(prefix_kernel, mask, parts),
        in_specs=[VMEM] * (parts + len(state)) + [ANY] * len(partial),
        out_specs=ANY,
        out_shape=jax.ShapeDtypeStruct((q_rows, KVH * wide), jnp.bfloat16),
        scratch_shapes=[
            pltpu.VMEM((q_rows, wide), jnp.bfloat16),
            pltpu.SemaphoreType.DMA((GROUP * q_rows // ROWS,)),
        ],
        input_output_aliases={parts + len(state): 0} if partial else {},
        cost_estimate=pl.CostEstimate(
            flops=64 * q_rows * wide * length, bytes_accessed=2**20, transcendentals=0
        ),
        compiler_params=pltpu.CompilerParams(vmem_limit_bytes=48 * 2**20),
        name="attend_prefix",
    )(*pieces, *[in_vmem(array) for array in state], *partial)


def swap(array, blks, mask):
    return lax.ppermute(array, "blk", [(i, i ^ mask) for i in range(blks)])


def per_device(queries, span_kv, kv_store, page_ids, page_owner, prefix_len):
    pools = lax.axis_size("pool")
    blks = lax.axis_size("blk")
    stored, page, _ = kv_store.shape
    parts = blks // KVH
    rows = page // parts

    owner = lax.broadcasted_iota(jnp.int32, (pools, 1, page_ids.shape[1]), 0)
    wanted = jnp.where(page_owner[None] == owner, page_ids[None], -1)
    tables = lax.all_to_all(wanted, "pool", split_axis=0, concat_axis=0, tiled=True)
    picked = pick_pages(tables, kv_store, rows)
    picked, span_kv = lax.optimization_barrier((picked, span_kv))
    fetched = lax.all_to_all(picked, "pool", split_axis=0, concat_axis=0, tiled=True)
    span = {0: span_kv}
    bit = blks // 2
    while bit:
        span.update({mask ^ bit: swap(rows_of, blks, bit) for mask, rows_of in list(span.items())})
        bit //= 2
    length = page_ids.shape[1] * page
    state = attend_span(prefix_len, queries, span, length, parts, rows)
    fetched, *state = lax.optimization_barrier((fetched, *state))
    mean, level, query, bias = state
    state = (query, mean, level, bias)
    held = {0: order_pages(page_owner, fetched)}
    held[1] = swap(held[0], blks, 1)
    bit = blks // 2
    while bit > 1:
        pieces = [(mask, piece) for mask, piece in held.items() if mask % 2 == 0]
        held.update({mask ^ bit: swap(piece, blks, bit) for mask, piece in pieces})
        bit //= 2
    for mask in range(KVH, blks, KVH):
        held[mask ^ 1] = swap(held[mask], blks, 1)
    out = attend_prefix(held, state, [], 0)
    out = attend_prefix(held, state, [out], 1)
    far = {mask: piece for mask, piece in held.items() if mask % KVH == 2}
    out, far = lax.optimization_barrier((out, far))
    far.update({mask ^ 1: swap(piece, blks, 1) for mask, piece in list(far.items())})
    out = attend_prefix(far, state, [out], 2)
    return attend_prefix(far, state, [out], 3)


def solution(mesh):
    in_specs = (
        P(("pool", "blk"), None),
        P(("pool", "blk"), None),
        P("pool", None, None),
        P("pool", None),
        P("pool", None),
        P("pool"),
    )
    out_specs = P(("pool", "blk"), None)
    return jax.shard_map(
        per_device, mesh=mesh, in_specs=in_specs, out_specs=out_specs, check_vma=False
    )
```

```python
import functools
import math

import jax
import jax.numpy as jnp
from jax import lax
from jax.experimental import pallas as pl
from jax.experimental.pallas import tpu as pltpu
from jax.sharding import PartitionSpec as P

KVH = 4
DH = 128
GROUP = 8
CAP = 2
COEF = math.log2(math.e) / math.sqrt(DH)
LOW = -1e30
ROWS = 256
LOADS = 4


SMEM = pl.BlockSpec(memory_space=pltpu.SMEM)
VMEM = pl.BlockSpec(memory_space=pltpu.VMEM)
ANY = pl.BlockSpec(memory_space=pl.ANY)


def columns_from(first, count):
    return pl.ds(pl.multiple_of(first * DH, DH), count * DH)


def pick_kernel(tables_ref, store_ref, out_ref, table, own, load_sems, sems):
    pools, _, listed = tables_ref.shape
    stored, rows, _ = own.shape
    blk = lax.axis_index("blk")
    head = lax.rem(blk, KVH)
    at_rows = pl.ds(pl.multiple_of(lax.div(blk, KVH) * rows, rows), rows)
    loads = [pltpu.make_async_copy(tables_ref, table, load_sems.at[0])]
    for kind in range(2):
        for first in range(0, stored, stored // LOADS):
            pages = slice(first, first + stored // LOADS)
            loads.append(
                pltpu.make_async_copy(
                    store_ref.at[pages, at_rows, columns_from(kind * KVH + head, 1)],
                    own.at[pages, :, kind * DH : (kind + 1) * DH],
                    load_sems.at[len(loads)],
                )
            )
    for load in loads:
        load.start()
    for load in loads:
        load.wait()

    def page_copy(request, slot, page):
        return pltpu.make_async_copy(
            own.at[page], out_ref.at[request, slot], sems.at[request, slot]
        )

    def serve(request, carry):
        def visit(entry, state):
            rank, pages = state
            page = table[request, 0, entry]
            hit = page >= 0
            pages = [jnp.where(hit & (rank == slot), page, pages[slot]) for slot in range(CAP)]
            return rank + hit.astype(jnp.int32), pages

        state = (jnp.int32(0), [jnp.int32(0)] * CAP)
        _, pages = lax.fori_loop(0, listed, visit, state, unroll=listed <= 8)
        for slot in range(CAP):
            page_copy(request, slot, pages[slot]).start()
        return carry

    lax.fori_loop(0, pools, serve, 0)

    def finish(request, carry):
        for slot in range(CAP):
            page_copy(request, slot, 0).wait()
        return carry

    lax.fori_loop(0, pools, finish, 0)


def pick_pages(tables, kv_store, rows):
    pools = tables.shape[0]
    return pl.pallas_call(
        pick_kernel,
        in_specs=[ANY, ANY],
        out_specs=ANY,
        out_shape=pltpu.HBM((pools, CAP, rows, 2 * DH), kv_store.dtype),
        scratch_shapes=[
            pltpu.SMEM(tables.shape, jnp.int32),
            pltpu.VMEM((kv_store.shape[0], rows, 2 * DH), kv_store.dtype),
            pltpu.SemaphoreType.DMA((1 + 2 * LOADS,)),
            pltpu.SemaphoreType.DMA((pools, CAP)),
        ],
        name="pick_pages",
    )(in_vmem(tables), in_hbm(kv_store))


def in_hbm(array):
    return pltpu.with_memory_space_constraint(array, pltpu.HBM)


def in_vmem(array):
    return pltpu.with_memory_space_constraint(array, pltpu.VMEM)


def order_kernel(owners_ref, fetched_ref, out_ref):
    for entry in range(out_ref.shape[0]):
        owner = owners_ref[0, entry]
        rank = jnp.int32(0)
        for earlier in range(entry):
            rank += (owners_ref[0, earlier] == owner).astype(jnp.int32)
        out_ref[entry] = fetched_ref[owner, jnp.minimum(rank, CAP - 1)]


def order_pages(owners, fetched):
    listed = owners.shape[1]
    rows = fetched.shape[2]
    return pl.pallas_call(
        order_kernel,
        in_specs=[SMEM, VMEM],
        out_specs=VMEM,
        out_shape=pltpu.VMEM((listed, rows, 2 * DH), fetched.dtype),
        name="order_pages",
    )(owners, in_vmem(fetched))


def scores_of(query_ref, first, count, keys):
    heads = [query_ref[:, (first + j) * DH : (first + j + 1) * DH] for j in range(count)]
    stacked = heads[0] if count == 1 else jnp.concatenate(heads, axis=0)
    return lax.dot_general(
        stacked, keys, (((1,), (1,)), ((), ())), preferred_element_type=jnp.float32
    )


def with_ones(values):
    return jnp.concatenate([values, jnp.ones((values.shape[0], DH), values.dtype)], axis=1)


def span_kernel(masks, parts, rows, limit_ref, query_ref, *refs):
    blocks = len(masks)
    keys_refs, values_refs = refs[:blocks], refs[blocks : 2 * blocks]
    mean_ref, level_ref, copy_ref, bias_ref = refs[2 * blocks :]
    q_rows = query_ref.shape[0]
    count = ROWS // q_rows
    copy_ref[0] = query_ref[...]
    own = lax.axis_index("blk")
    shape = (bias_ref.shape[0], bias_ref.shape[1] // parts)
    index = lax.broadcasted_iota(jnp.int32, shape, 1)
    at_page = lax.div(index, rows) * (parts * rows) + lax.rem(index, rows)
    for step in range(parts):
        position = at_page + lax.rem(lax.div(own, KVH) + step, parts) * rows
        bias_ref[:, step * shape[1] : (step + 1) * shape[1]] = jnp.where(
            position < limit_ref[0], 0.0, LOW
        )
    keys = jnp.concatenate([ref[...] for ref in keys_refs], axis=0)
    values = with_ones(jnp.concatenate([ref[...] for ref in values_refs], axis=0))
    ahead = lax.broadcasted_iota(jnp.int32, (q_rows, q_rows), 0) - lax.broadcasted_iota(
        jnp.int32, (q_rows, q_rows), 1
    )
    bias = [
        jnp.where(ahead >= (jnp.bitwise_xor(own, mask) - own) * q_rows, 0.0, LOW) for mask in masks
    ]
    bias = jnp.concatenate(bias, axis=1)
    bias = jnp.concatenate([bias] * count, axis=0)
    lanes = lax.broadcasted_iota(jnp.int32, (q_rows, DH), 1)
    levels = jnp.zeros((q_rows, DH), jnp.float32)
    for first in range(0, GROUP, count):
        scores = scores_of(query_ref, first, count, keys) + bias
        top = jnp.max(scores, axis=1, keepdims=True)
        weights = jnp.exp2((scores - top) * COEF)
        summed = jnp.dot(
            weights.astype(jnp.bfloat16), values, preferred_element_type=jnp.float32
        )
        total = summed[:, DH:]
        level = top * COEF + jnp.log2(total)
        mean = summed[:, :DH] / total
        for j in range(count):
            at = slice(j * q_rows, (j + 1) * q_rows)
            columns = slice((first + j) * DH, (first + j + 1) * DH)
            mean_ref[0, :, columns] = mean[at].astype(jnp.bfloat16)
            levels = jnp.where(lanes == first + j, level[at], levels)
    level_ref[0] = levels


def attend_span(limit, queries, span, length, parts, rows):
    q_rows = queries.shape[0]
    masks = sorted(span)
    blocks = [span[mask] for mask in masks]
    wide = GROUP * DH

    def head(m):
        return lax.rem(lax.axis_index("blk"), KVH) ^ m

    keys_spec = pl.BlockSpec((q_rows, DH), lambda m: (0, head(m)))
    values_spec = pl.BlockSpec((q_rows, DH), lambda m: (0, KVH + head(m)))
    return pl.pallas_call(
        functools.partial(span_kernel, masks, parts, rows),
        grid=(KVH,),
        in_specs=[SMEM, pl.BlockSpec((q_rows, wide), lambda m: (0, head(m)))]
        + [keys_spec] * len(masks)
        + [values_spec] * len(masks),
        out_specs=[
            pl.BlockSpec((1, q_rows, wide), lambda m: (m, 0, 0)),
            pl.BlockSpec((1, q_rows, DH), lambda m: (m, 0, 0)),
            pl.BlockSpec((1, q_rows, wide), lambda m: (m, 0, 0)),
            pl.BlockSpec((8, length), lambda m: (0, 0)),
        ],
        out_shape=[
            pltpu.VMEM((KVH, q_rows, wide), jnp.bfloat16),
            pltpu.VMEM((KVH, q_rows, DH), jnp.float32),
            pltpu.VMEM((KVH, q_rows, wide), jnp.bfloat16),
            pltpu.VMEM((8, length), jnp.float32),
        ],
        cost_estimate=pl.CostEstimate(
            flops=4 * q_rows * KVH * wide * q_rows * len(masks),
            bytes_accessed=8 * 2**20,
            transcendentals=0,
        ),
        compiler_params=pltpu.CompilerParams(vmem_limit_bytes=48 * 2**20),
        name="attend_span",
    )(limit, in_hbm(queries), *blocks, *blocks)


def prefix_kernel(mask, parts, *refs):
    pieces = refs[:parts]
    query_ref, mean_ref, level_ref, bias_ref, *_, out_ref, done_ref, sems = refs[parts:]
    q_rows = query_ref.shape[1]
    count = ROWS // q_rows
    head = jnp.bitwise_xor(lax.rem(lax.axis_index("blk"), KVH), mask)
    listed, rows, _ = pieces[0].shape
    length = listed * rows
    both = [piece[...].reshape(length, 2 * DH) for piece in pieces]
    both = both[0] if parts == 1 else jnp.concatenate(both, axis=0)
    keys = both[:, :DH]
    values = with_ones(both[:, DH:])
    safe = length * 5 // 8 // DH * DH
    biases = [bias_ref[:1, step * length + safe : (step + 1) * length] for step in range(parts)]
    starts = range(0, GROUP, count)
    ahead = scores_of(query_ref.at[mask], 0, count, keys)
    for first in starts:
        raw = ahead
        if first + count < GROUP:
            ahead = scores_of(query_ref.at[mask], first + count, count, keys)
        scores = []
        for step, bias in enumerate(biases):
            scores.append(raw[:, step * length : step * length + safe])
            scores.append(raw[:, step * length + safe : (step + 1) * length] + bias)
        scores = jnp.concatenate(scores, axis=1)
        heads = [slice((first + j) * DH, (first + j + 1) * DH) for j in range(count)]
        level = jnp.concatenate(
            [
                jnp.broadcast_to(level_ref[mask, :, first + j : first + j + 1], (q_rows, DH))
                for j in range(count)
            ],
            axis=0,
        )
        mean = jnp.concatenate([mean_ref[mask, :, columns] for columns in heads], axis=0)
        top = jnp.maximum(jnp.max(scores, axis=1, keepdims=True) * COEF, level)
        tops = jnp.concatenate([top] * (parts * length // DH), axis=1)
        weights = jnp.exp2(scores * COEF - tops)
        old = jnp.exp2(level - top)
        summed = jnp.dot(
            weights.astype(jnp.bfloat16), values, preferred_element_type=jnp.float32
        )
        result = (summed[:, :DH] + mean.astype(jnp.float32) * old) / (summed[:, DH:] + old)
        for j, columns in enumerate(heads):
            done_ref[:, columns] = result[j * q_rows : (j + 1) * q_rows].astype(jnp.bfloat16)
    copies = [
        pltpu.make_async_copy(
            done_ref.at[:, first * DH : (first + count) * DH],
            out_ref.at[:, columns_from(head * GROUP + first, count)],
            sems.at[first // count],
        )
        for first in starts
    ]
    for copy in copies:
        copy.start()
    for copy in copies:
        copy.wait()


def attend_prefix(held, state, partial, mask):
    _, q_rows, wide = state[0].shape
    pieces = [held[at] for at in sorted(held) if at % KVH == mask]
    parts = len(pieces)
    length = parts * pieces[0].shape[0] * pieces[0].shape[1]
    return pl.pallas_call(
        functools.partial(prefix_kernel, mask, parts),
        in_specs=[VMEM] * (parts + len(state)) + [ANY] * len(partial),
        out_specs=ANY,
        out_shape=jax.ShapeDtypeStruct((q_rows, KVH * wide), jnp.bfloat16),
        scratch_shapes=[
            pltpu.VMEM((q_rows, wide), jnp.bfloat16),
            pltpu.SemaphoreType.DMA((GROUP * q_rows // ROWS,)),
        ],
        input_output_aliases={parts + len(state): 0} if partial else {},
        cost_estimate=pl.CostEstimate(
            flops=64 * q_rows * wide * length, bytes_accessed=2**20, transcendentals=0
        ),
        compiler_params=pltpu.CompilerParams(vmem_limit_bytes=48 * 2**20),
        name="attend_prefix",
    )(*pieces, *[in_vmem(array) for array in state], *partial)


def swap(array, blks, mask):
    return lax.ppermute(array, "blk", [(i, i ^ mask) for i in range(blks)])


def per_device(queries, span_kv, kv_store, page_ids, page_owner, prefix_len):
    pools = lax.axis_size("pool")
    blks = lax.axis_size("blk")
    stored, page, _ = kv_store.shape
    parts = blks // KVH
    rows = page // parts

    owner = lax.broadcasted_iota(jnp.int32, (pools, 1, page_ids.shape[1]), 0)
    wanted = jnp.where(page_owner[None] == owner, page_ids[None], -1)
    tables = lax.all_to_all(wanted, "pool", split_axis=0, concat_axis=0, tiled=True)
    picked = pick_pages(tables, kv_store, rows)
    picked, span_kv = lax.optimization_barrier((picked, span_kv))
    fetched = lax.all_to_all(picked, "pool", split_axis=0, concat_axis=0, tiled=True)
    span = {0: span_kv}
    bit = blks // 2
    while bit:
        span.update({mask ^ bit: swap(rows_of, blks, bit) for mask, rows_of in list(span.items())})
        bit //= 2
    length = page_ids.shape[1] * page
    state = attend_span(prefix_len, queries, span, length, parts, rows)
    fetched, *state = lax.optimization_barrier((fetched, *state))
    mean, level, query, bias = state
    state = (query, mean, level, bias)
    held = {0: order_pages(page_owner, fetched)}
    held[1] = swap(held[0], blks, 1)
    bit = blks // 2
    while bit > 1:
        pieces = [(mask, piece) for mask, piece in held.items() if mask % 2 == 0]
        held.update({mask ^ bit: swap(piece, blks, bit) for mask, piece in pieces})
        bit //= 2
    for mask in range(KVH, blks, KVH):
        held[mask ^ 1] = swap(held[mask], blks, 1)
    out = attend_prefix(held, state, [], 0)
    out = attend_prefix(held, state, [out], 1)
    far = {mask: piece for mask, piece in held.items() if mask % KVH == 2}
    out, far = lax.optimization_barrier((out, far))
    far.update({mask ^ 1: swap(piece, blks, 1) for mask, piece in list(far.items())})
    out = attend_prefix(far, state, [out], 2)
    return attend_prefix(far, state, [out], 3)


def solution(mesh):
    in_specs = (
        P(("pool", "blk"), None),
        P(("pool", "blk"), None),
        P("pool", None, None),
        P("pool", None),
        P("pool", None),
        P("pool"),
    )
    out_specs = P(("pool", "blk"), None)
    return jax.shard_map(
        per_device, mesh=mesh, in_specs=in_specs, out_specs=out_specs, check_vma=False
    )
```

```python
import functools
import math

import jax
import jax.numpy as jnp
from jax import lax
from jax.experimental import pallas as pl
from jax.experimental.pallas import tpu as pltpu
from jax.sharding import PartitionSpec as P

KVH = 4
HALF = KVH // 2
DH = 128
GROUP = 8
CAP = 2
COEF = math.log2(math.e) / math.sqrt(DH)
LOW = -1e30
ROWS = 256
LOADS = 4


SMEM = pl.BlockSpec(memory_space=pltpu.SMEM)
VMEM = pl.BlockSpec(memory_space=pltpu.VMEM)
ANY = pl.BlockSpec(memory_space=pl.ANY)


def columns_from(first, count):
    return pl.ds(pl.multiple_of(first * DH, DH), count * DH)


def pick_kernel(tables_ref, store_ref, out_ref, table, own, load_sems, sems):
    pools, _, listed = tables_ref.shape
    stored, rows, _ = own.shape
    blk = lax.axis_index("blk")
    head = lax.rem(blk, KVH)
    at_rows = pl.ds(pl.multiple_of(lax.div(blk, KVH) * rows, rows), rows)
    loads = [pltpu.make_async_copy(tables_ref, table, load_sems.at[0])]
    for kind in range(2):
        for first in range(0, stored, stored // LOADS):
            pages = slice(first, first + stored // LOADS)
            loads.append(
                pltpu.make_async_copy(
                    store_ref.at[pages, at_rows, columns_from(kind * KVH + head, 1)],
                    own.at[pages, :, kind * DH : (kind + 1) * DH],
                    load_sems.at[len(loads)],
                )
            )
    for load in loads:
        load.start()
    for load in loads:
        load.wait()

    def page_copy(request, slot, page):
        return pltpu.make_async_copy(
            own.at[page], out_ref.at[request, slot], sems.at[request, slot]
        )

    def serve(request, carry):
        def visit(entry, state):
            rank, pages = state
            page = table[request, 0, entry]
            hit = page >= 0
            pages = [jnp.where(hit & (rank == slot), page, pages[slot]) for slot in range(CAP)]
            return rank + hit.astype(jnp.int32), pages

        state = (jnp.int32(0), [jnp.int32(0)] * CAP)
        _, pages = lax.fori_loop(0, listed, visit, state, unroll=listed <= 8)
        for slot in range(CAP):
            page_copy(request, slot, pages[slot]).start()
        return carry

    lax.fori_loop(0, pools, serve, 0)

    def finish(request, carry):
        for slot in range(CAP):
            page_copy(request, slot, 0).wait()
        return carry

    lax.fori_loop(0, pools, finish, 0)


def pick_pages(tables, kv_store, rows):
    pools = tables.shape[0]
    return pl.pallas_call(
        pick_kernel,
        in_specs=[ANY, ANY],
        out_specs=ANY,
        out_shape=pltpu.HBM((pools, CAP, rows, 2 * DH), kv_store.dtype),
        scratch_shapes=[
            pltpu.SMEM(tables.shape, jnp.int32),
            pltpu.VMEM((kv_store.shape[0], rows, 2 * DH), kv_store.dtype),
            pltpu.SemaphoreType.DMA((1 + 2 * LOADS,)),
            pltpu.SemaphoreType.DMA((pools, CAP)),
        ],
        name="pick_pages",
    )(in_vmem(tables), in_hbm(kv_store))


def in_hbm(array):
    return pltpu.with_memory_space_constraint(array, pltpu.HBM)


def in_vmem(array):
    return pltpu.with_memory_space_constraint(array, pltpu.VMEM)


def order_kernel(owners_ref, fetched_ref, out_ref):
    for entry in range(out_ref.shape[0]):
        owner = owners_ref[0, entry]
        rank = jnp.int32(0)
        for earlier in range(entry):
            rank += (owners_ref[0, earlier] == owner).astype(jnp.int32)
        out_ref[entry] = fetched_ref[owner, jnp.minimum(rank, CAP - 1)]


def order_pages(owners, fetched):
    listed = owners.shape[1]
    rows = fetched.shape[2]
    return pl.pallas_call(
        order_kernel,
        in_specs=[SMEM, VMEM],
        out_specs=VMEM,
        out_shape=pltpu.VMEM((listed, rows, 2 * DH), fetched.dtype),
        name="order_pages",
    )(owners, in_vmem(fetched))


def scores_of(query_ref, first, count, keys):
    heads = [query_ref[:, (first + j) * DH : (first + j + 1) * DH] for j in range(count)]
    stacked = heads[0] if count == 1 else jnp.concatenate(heads, axis=0)
    return lax.dot_general(
        stacked, keys, (((1,), (1,)), ((), ())), preferred_element_type=jnp.float32
    )


def with_ones(values):
    return jnp.concatenate([values, jnp.ones((values.shape[0], DH), values.dtype)], axis=1)


def span_kernel(masks, parts, rows, limit_ref, query_ref, *refs):
    blocks = len(masks)
    keys_refs, values_refs = refs[:blocks], refs[blocks : 2 * blocks]
    mean_ref, level_ref, copy_ref, bias_ref = refs[2 * blocks :]
    q_rows = query_ref.shape[0]
    count = ROWS // q_rows
    copy_ref[0] = query_ref[...]
    own = lax.axis_index("blk")
    shape = (bias_ref.shape[0], bias_ref.shape[1] // parts)
    index = lax.broadcasted_iota(jnp.int32, shape, 1)
    at_page = lax.div(index, rows) * (parts * rows) + lax.rem(index, rows)
    for step in range(parts):
        position = at_page + lax.rem(lax.div(own, KVH) + step, parts) * rows
        bias_ref[:, step * shape[1] : (step + 1) * shape[1]] = jnp.where(
            position < limit_ref[0], 0.0, LOW
        )
    keys = jnp.concatenate([ref[...] for ref in keys_refs], axis=0)
    values = with_ones(jnp.concatenate([ref[...] for ref in values_refs], axis=0))
    ahead = lax.broadcasted_iota(jnp.int32, (q_rows, q_rows), 0) - lax.broadcasted_iota(
        jnp.int32, (q_rows, q_rows), 1
    )
    bias = [
        jnp.where(ahead >= (jnp.bitwise_xor(own, mask) - own) * q_rows, 0.0, LOW) for mask in masks
    ]
    bias = jnp.concatenate(bias, axis=1)
    bias = jnp.concatenate([bias] * count, axis=0)
    lanes = lax.broadcasted_iota(jnp.int32, (q_rows, DH), 1)
    levels = jnp.zeros((q_rows, DH), jnp.float32)
    for first in range(0, GROUP, count):
        scores = scores_of(query_ref, first, count, keys) + bias
        top = jnp.max(scores, axis=1, keepdims=True)
        weights = jnp.exp2((scores - top) * COEF)
        summed = jnp.dot(
            weights.astype(jnp.bfloat16), values, preferred_element_type=jnp.float32
        )
        total = summed[:, DH:]
        level = top * COEF + jnp.log2(total)
        mean = summed[:, :DH] / total
        for j in range(count):
            at = slice(j * q_rows, (j + 1) * q_rows)
            columns = slice((first + j) * DH, (first + j + 1) * DH)
            mean_ref[0, :, columns] = mean[at].astype(jnp.bfloat16)
            levels = jnp.where(lanes == first + j, level[at], levels)
    level_ref[0] = levels


def attend_span(limit, queries, span, length, parts, rows, base):
    q_rows = queries.shape[0]
    masks = sorted(span)
    blocks = [span[mask] for mask in masks]
    wide = GROUP * DH

    def head(m):
        return lax.rem(lax.axis_index("blk"), KVH) ^ (base + m)

    keys_spec = pl.BlockSpec((q_rows, DH), lambda m: (0, head(m)))
    values_spec = pl.BlockSpec((q_rows, DH), lambda m: (0, KVH + head(m)))
    return pl.pallas_call(
        functools.partial(span_kernel, masks, parts, rows),
        grid=(HALF,),
        in_specs=[SMEM, pl.BlockSpec((q_rows, wide), lambda m: (0, head(m)))]
        + [keys_spec] * len(masks)
        + [values_spec] * len(masks),
        out_specs=[
            pl.BlockSpec((1, q_rows, wide), lambda m: (m, 0, 0)),
            pl.BlockSpec((1, q_rows, DH), lambda m: (m, 0, 0)),
            pl.BlockSpec((1, q_rows, wide), lambda m: (m, 0, 0)),
            pl.BlockSpec((8, length), lambda m: (0, 0)),
        ],
        out_shape=[
            pltpu.VMEM((HALF, q_rows, wide), jnp.bfloat16),
            pltpu.VMEM((HALF, q_rows, DH), jnp.float32),
            pltpu.VMEM((HALF, q_rows, wide), jnp.bfloat16),
            pltpu.VMEM((8, length), jnp.float32),
        ],
        cost_estimate=pl.CostEstimate(
            flops=32 * q_rows * HALF * wide * q_rows * len(masks),
            bytes_accessed=2**20,
            transcendentals=0,
        ),
        compiler_params=pltpu.CompilerParams(vmem_limit_bytes=48 * 2**20),
        name="attend_span",
    )(limit, in_hbm(queries), *blocks, *blocks)


def prefix_kernel(mask, parts, *refs):
    pieces = refs[:parts]
    query_ref, mean_ref, level_ref, bias_ref, *_, out_ref, done_ref, sems = refs[parts:]
    q_rows = query_ref.shape[1]
    count = ROWS // q_rows
    head = jnp.bitwise_xor(lax.rem(lax.axis_index("blk"), KVH), mask)
    listed, rows, _ = pieces[0].shape
    length = listed * rows
    both = [piece[...].reshape(length, 2 * DH) for piece in pieces]
    both = both[0] if parts == 1 else jnp.concatenate(both, axis=0)
    keys = both[:, :DH]
    values = with_ones(both[:, DH:])
    safe = length * 5 // 8 // DH * DH
    biases = [bias_ref[:1, step * length + safe : (step + 1) * length] for step in range(parts)]
    copies = []
    for first in range(0, GROUP, count):
        raw = scores_of(query_ref.at[mask % HALF], first, count, keys)
        scores = []
        for step, bias in enumerate(biases):
            scores.append(raw[:, step * length : step * length + safe])
            scores.append(raw[:, step * length + safe : (step + 1) * length] + bias)
        scores = jnp.concatenate(scores, axis=1)
        heads = [slice((first + j) * DH, (first + j + 1) * DH) for j in range(count)]
        level = jnp.concatenate(
            [
                jnp.broadcast_to(level_ref[mask % HALF, :, first + j : first + j + 1], (q_rows, DH))
                for j in range(count)
            ],
            axis=0,
        )
        mean = jnp.concatenate([mean_ref[mask % HALF, :, columns] for columns in heads], axis=0)
        top = jnp.maximum(jnp.max(scores, axis=1, keepdims=True) * COEF, level)
        tops = jnp.concatenate([top] * (parts * length // DH), axis=1)
        weights = jnp.exp2(scores * COEF - tops)
        old = jnp.exp2(level - top)
        summed = jnp.dot(
            weights.astype(jnp.bfloat16), values, preferred_element_type=jnp.float32
        )
        result = (summed[:, :DH] + mean.astype(jnp.float32) * old) / (summed[:, DH:] + old)
        for j, columns in enumerate(heads):
            done_ref[:, columns] = result[j * q_rows : (j + 1) * q_rows].astype(jnp.bfloat16)
        copies.append(
            pltpu.make_async_copy(
                done_ref.at[:, first * DH : (first + count) * DH],
                out_ref.at[:, columns_from(head * GROUP + first, count)],
                sems.at[first // count],
            )
        )
        copies[-1].start()
    for copy in copies:
        copy.wait()


def attend_prefix(held, state, partial, mask):
    mean, level, query, bias = state
    _, q_rows, wide = query.shape
    pieces = [held[at] for at in sorted(held) if at % KVH == mask]
    parts = len(pieces)
    length = parts * pieces[0].shape[0] * pieces[0].shape[1]
    return pl.pallas_call(
        functools.partial(prefix_kernel, mask, parts),
        in_specs=[VMEM] * (parts + len(state)) + [ANY] * len(partial),
        out_specs=ANY,
        out_shape=jax.ShapeDtypeStruct((q_rows, KVH * wide), jnp.bfloat16),
        scratch_shapes=[
            pltpu.VMEM((q_rows, wide), jnp.bfloat16),
            pltpu.SemaphoreType.DMA((GROUP * q_rows // ROWS,)),
        ],
        input_output_aliases={parts + len(state): 0} if partial else {},
        cost_estimate=pl.CostEstimate(
            flops=64 * q_rows * wide * length, bytes_accessed=2**20, transcendentals=0
        ),
        compiler_params=pltpu.CompilerParams(vmem_limit_bytes=48 * 2**20),
        name="attend_prefix",
    )(*pieces, in_vmem(query), in_vmem(mean), in_vmem(level), in_vmem(bias), *partial)


def swap(array, blks, mask):
    return lax.ppermute(array, "blk", [(i, i ^ mask) for i in range(blks)])


def per_device(queries, span_kv, kv_store, page_ids, page_owner, prefix_len):
    pools = lax.axis_size("pool")
    blks = lax.axis_size("blk")
    stored, page, _ = kv_store.shape
    parts = blks // KVH
    rows = page // parts

    owner = lax.broadcasted_iota(jnp.int32, (pools, 1, page_ids.shape[1]), 0)
    wanted = jnp.where(page_owner[None] == owner, page_ids[None], -1)
    tables = lax.all_to_all(wanted, "pool", split_axis=0, concat_axis=0, tiled=True)
    picked = pick_pages(tables, kv_store, rows)
    picked, span_kv = lax.optimization_barrier((picked, span_kv))
    fetched = lax.all_to_all(picked, "pool", split_axis=0, concat_axis=0, tiled=True)
    span = {0: span_kv}
    bit = blks // 2
    while bit:
        span.update({mask ^ bit: swap(rows_of, blks, bit) for mask, rows_of in list(span.items())})
        bit //= 2
    length = page_ids.shape[1] * page
    attend = functools.partial(attend_span, prefix_len, queries, span, length, parts, rows)
    early = attend(0)
    fetched, *early = lax.optimization_barrier((fetched, *early))
    held = {0: order_pages(page_owner, fetched)}
    held[1] = swap(held[0], blks, 1)
    bit = blks // 2
    while bit > 1:
        pieces = [(mask, piece) for mask, piece in held.items() if mask % 2 == 0]
        held.update({mask ^ bit: swap(piece, blks, bit) for mask, piece in pieces})
        bit //= 2
    for mask in range(KVH, blks, KVH):
        held[mask ^ 1] = swap(held[mask], blks, 1)
    out = attend_prefix(held, early, [], 0)
    out = attend_prefix(held, early, [out], 1)
    late = attend(HALF)
    far = {mask: piece for mask, piece in held.items() if mask % KVH == 2}
    out, far, *late = lax.optimization_barrier((out, far, *late))
    far.update({mask ^ 1: swap(piece, blks, 1) for mask, piece in list(far.items())})
    out = attend_prefix(far, late, [out], 2)
    return attend_prefix(far, late, [out], 3)


def solution(mesh):
    in_specs = (
        P(("pool", "blk"), None),
        P(("pool", "blk"), None),
        P("pool", None, None),
        P("pool", None),
        P("pool", None),
        P("pool"),
    )
    out_specs = P(("pool", "blk"), None)
    return jax.shard_map(
        per_device, mesh=mesh, in_specs=in_specs, out_specs=out_specs, check_vma=False
    )
```

```python
import functools
import math

import jax
import jax.numpy as jnp
from jax import lax
from jax.experimental import pallas as pl
from jax.experimental.pallas import tpu as pltpu
from jax.sharding import PartitionSpec as P

KVH = 4
DH = 128
GROUP = 8
CAP = 2
COEF = math.log2(math.e) / math.sqrt(DH)
LOW = -1e30
ROWS = 256
LOADS = 4


SMEM = pl.BlockSpec(memory_space=pltpu.SMEM)
VMEM = pl.BlockSpec(memory_space=pltpu.VMEM)
ANY = pl.BlockSpec(memory_space=pl.ANY)


def columns_from(first, count):
    return pl.ds(pl.multiple_of(first * DH, DH), count * DH)


def pick_kernel(tables_ref, store_ref, out_ref, table, own, load_sems, sems):
    pools, _, listed = tables_ref.shape
    stored, rows, _ = own.shape
    blk = lax.axis_index("blk")
    head = lax.rem(blk, KVH)
    at_rows = pl.ds(pl.multiple_of(lax.div(blk, KVH) * rows, rows), rows)
    loads = [pltpu.make_async_copy(tables_ref, table, load_sems.at[0])]
    for kind in range(2):
        for first in range(0, stored, stored // LOADS):
            pages = slice(first, first + stored // LOADS)
            loads.append(
                pltpu.make_async_copy(
                    store_ref.at[pages, at_rows, columns_from(kind * KVH + head, 1)],
                    own.at[pages, :, kind * DH : (kind + 1) * DH],
                    load_sems.at[len(loads)],
                )
            )
    for load in loads:
        load.start()
    for load in loads:
        load.wait()

    def page_copy(request, slot, page):
        return pltpu.make_async_copy(
            own.at[page], out_ref.at[request, slot], sems.at[request, slot]
        )

    def serve(request, carry):
        def visit(entry, state):
            rank, pages = state
            page = table[request, 0, entry]
            hit = page >= 0
            pages = [jnp.where(hit & (rank == slot), page, pages[slot]) for slot in range(CAP)]
            return rank + hit.astype(jnp.int32), pages

        state = (jnp.int32(0), [jnp.int32(0)] * CAP)
        _, pages = lax.fori_loop(0, listed, visit, state, unroll=listed <= 8)
        for slot in range(CAP):
            page_copy(request, slot, pages[slot]).start()
        return carry

    lax.fori_loop(0, pools, serve, 0)

    def finish(request, carry):
        for slot in range(CAP):
            page_copy(request, slot, 0).wait()
        return carry

    lax.fori_loop(0, pools, finish, 0)


def pick_pages(tables, kv_store, rows):
    pools = tables.shape[0]
    return pl.pallas_call(
        pick_kernel,
        in_specs=[ANY, ANY],
        out_specs=ANY,
        out_shape=pltpu.HBM((pools, CAP, rows, 2 * DH), kv_store.dtype),
        scratch_shapes=[
            pltpu.SMEM(tables.shape, jnp.int32),
            pltpu.VMEM((kv_store.shape[0], rows, 2 * DH), kv_store.dtype),
            pltpu.SemaphoreType.DMA((1 + 2 * LOADS,)),
            pltpu.SemaphoreType.DMA((pools, CAP)),
        ],
        name="pick_pages",
    )(in_vmem(tables), in_hbm(kv_store))


def in_hbm(array):
    return pltpu.with_memory_space_constraint(array, pltpu.HBM)


def in_vmem(array):
    return pltpu.with_memory_space_constraint(array, pltpu.VMEM)


def order_kernel(owners_ref, fetched_ref, out_ref, first_ref, second_ref):
    listed = out_ref.shape[0]
    half = listed // 2
    for entry in range(listed):
        owner = owners_ref[0, entry]
        rank = jnp.int32(0)
        for earlier in range(entry):
            rank += (owners_ref[0, earlier] == owner).astype(jnp.int32)
        page = fetched_ref[owner, jnp.minimum(rank, CAP - 1)]
        out_ref[entry] = page
        half_ref = first_ref if entry < half else second_ref
        half_ref[entry % half] = page


def order_pages(owners, fetched):
    listed = owners.shape[1]
    shape = (fetched.shape[2], 2 * DH)
    return pl.pallas_call(
        order_kernel,
        in_specs=[SMEM, VMEM],
        out_specs=[VMEM] * 3,
        out_shape=[
            pltpu.VMEM((listed, *shape), fetched.dtype),
            pltpu.VMEM((listed // 2, *shape), fetched.dtype),
            pltpu.VMEM((listed // 2, *shape), fetched.dtype),
        ],
        name="order_pages",
    )(owners, in_vmem(fetched))


def scores_of(query_ref, first, count, keys):
    heads = [query_ref[:, (first + j) * DH : (first + j + 1) * DH] for j in range(count)]
    stacked = heads[0] if count == 1 else jnp.concatenate(heads, axis=0)
    return lax.dot_general(
        stacked, keys, (((1,), (1,)), ((), ())), preferred_element_type=jnp.float32
    )


def with_ones(values):
    return jnp.concatenate([values, jnp.ones((values.shape[0], DH), values.dtype)], axis=1)


def span_kernel(masks, parts, rows, limit_ref, query_ref, *refs):
    blocks = len(masks)
    keys_refs, values_refs = refs[:blocks], refs[blocks : 2 * blocks]
    mean_ref, level_ref, copy_ref, bias_ref = refs[2 * blocks :]
    q_rows = query_ref.shape[0]
    count = ROWS // q_rows
    copy_ref[0] = query_ref[...]
    own = lax.axis_index("blk")
    shape = (bias_ref.shape[0], bias_ref.shape[1] // parts)
    index = lax.broadcasted_iota(jnp.int32, shape, 1)
    at_page = lax.div(index, rows) * (parts * rows) + lax.rem(index, rows)
    for step in range(parts):
        position = at_page + lax.rem(lax.div(own, KVH) + step, parts) * rows
        bias_ref[:, step * shape[1] : (step + 1) * shape[1]] = jnp.where(
            position < limit_ref[0], 0.0, LOW
        )
    keys = jnp.concatenate([ref[...] for ref in keys_refs], axis=0)
    values = with_ones(jnp.concatenate([ref[...] for ref in values_refs], axis=0))
    ahead = lax.broadcasted_iota(jnp.int32, (q_rows, q_rows), 0) - lax.broadcasted_iota(
        jnp.int32, (q_rows, q_rows), 1
    )
    bias = [
        jnp.where(ahead >= (jnp.bitwise_xor(own, mask) - own) * q_rows, 0.0, LOW) for mask in masks
    ]
    bias = jnp.concatenate(bias, axis=1)
    bias = jnp.concatenate([bias] * count, axis=0)
    lanes = lax.broadcasted_iota(jnp.int32, (q_rows, DH), 1)
    levels = jnp.zeros((q_rows, DH), jnp.float32)
    for first in range(0, GROUP, count):
        scores = scores_of(query_ref, first, count, keys) + bias
        top = jnp.max(scores, axis=1, keepdims=True)
        weights = jnp.exp2((scores - top) * COEF)
        summed = jnp.dot(
            weights.astype(jnp.bfloat16), values, preferred_element_type=jnp.float32
        )
        total = summed[:, DH:]
        level = top * COEF + jnp.log2(total)
        mean = summed[:, :DH] / total
        for j in range(count):
            at = slice(j * q_rows, (j + 1) * q_rows)
            columns = slice((first + j) * DH, (first + j + 1) * DH)
            mean_ref[0, :, columns] = mean[at].astype(jnp.bfloat16)
            levels = jnp.where(lanes == first + j, level[at], levels)
    level_ref[0] = levels


def attend_span(limit, queries, span, length, parts, rows):
    q_rows = queries.shape[0]
    masks = sorted(span)
    blocks = [span[mask] for mask in masks]
    wide = GROUP * DH

    def head(m):
        return lax.rem(lax.axis_index("blk"), KVH) ^ m

    keys_spec = pl.BlockSpec((q_rows, DH), lambda m: (0, head(m)))
    values_spec = pl.BlockSpec((q_rows, DH), lambda m: (0, KVH + head(m)))
    return pl.pallas_call(
        functools.partial(span_kernel, masks, parts, rows),
        grid=(KVH,),
        in_specs=[SMEM, pl.BlockSpec((q_rows, wide), lambda m: (0, head(m)))]
        + [keys_spec] * len(masks)
        + [values_spec] * len(masks),
        out_specs=[
            pl.BlockSpec((1, q_rows, wide), lambda m: (m, 0, 0)),
            pl.BlockSpec((1, q_rows, DH), lambda m: (m, 0, 0)),
            pl.BlockSpec((1, q_rows, wide), lambda m: (m, 0, 0)),
            pl.BlockSpec((8, length), lambda m: (0, 0)),
        ],
        out_shape=[
            pltpu.VMEM((KVH, q_rows, wide), jnp.bfloat16),
            pltpu.VMEM((KVH, q_rows, DH), jnp.float32),
            pltpu.VMEM((KVH, q_rows, wide), jnp.bfloat16),
            pltpu.VMEM((8, length), jnp.float32),
        ],
        cost_estimate=pl.CostEstimate(
            flops=4 * q_rows * KVH * wide * q_rows * len(masks),
            bytes_accessed=8 * 2**20,
            transcendentals=0,
        ),
        compiler_params=pltpu.CompilerParams(vmem_limit_bytes=48 * 2**20),
        name="attend_span",
    )(limit, in_hbm(queries), *blocks, *blocks)


def prefix_kernel(mask, at, parts, offset, final, *refs):
    pieces = refs[:parts]
    query_ref, mean_ref, level_ref, bias_ref, *refs = refs[parts:]
    q_rows = query_ref.shape[1]
    count = ROWS // q_rows
    pages, rows, _ = pieces[0].shape
    length = pages * rows
    both = [piece[...].reshape(length, 2 * DH) for piece in pieces]
    both = both[0] if parts == 1 else jnp.concatenate(both, axis=0)
    keys = both[:, :DH]
    values = with_ones(both[:, DH:])
    whole = bias_ref.shape[1] // parts
    safe = min(max(whole * 5 // 8 // DH * DH - offset, 0), length)
    lanes = lax.broadcasted_iota(jnp.int32, (q_rows, DH), 1)
    levels = jnp.zeros((q_rows, DH), jnp.float32)
    copies = []
    for first in range(0, GROUP, count):
        raw = scores_of(query_ref.at[mask], first, count, keys)
        scores = []
        for step in range(parts):
            scores.append(raw[:, step * length : step * length + safe])
            if safe < length:
                bias = bias_ref[:1, step * whole + offset + safe : step * whole + offset + length]
                scores.append(raw[:, step * length + safe : (step + 1) * length] + bias)
        scores = jnp.concatenate([part for part in scores if part.shape[1]], axis=1)
        heads = [slice((first + j) * DH, (first + j + 1) * DH) for j in range(count)]
        level = jnp.concatenate(
            [
                jnp.broadcast_to(level_ref[at, :, first + j : first + j + 1], (q_rows, DH))
                for j in range(count)
            ],
            axis=0,
        )
        mean = jnp.concatenate([mean_ref[at, :, columns] for columns in heads], axis=0)
        top = jnp.maximum(jnp.max(scores, axis=1, keepdims=True) * COEF, level)
        tops = jnp.concatenate([top] * (parts * length // DH), axis=1)
        weights = jnp.exp2(scores * COEF - tops)
        old = jnp.exp2(level - top)
        summed = jnp.dot(
            weights.astype(jnp.bfloat16), values, preferred_element_type=jnp.float32
        )
        total = summed[:, DH:] + old
        result = (summed[:, :DH] + mean.astype(jnp.float32) * old) / total
        if final:
            *_, out_ref, done_ref, sems = refs
            for j, columns in enumerate(heads):
                done_ref[:, columns] = result[j * q_rows : (j + 1) * q_rows].astype(jnp.bfloat16)
            head = jnp.bitwise_xor(lax.rem(lax.axis_index("blk"), KVH), mask)
            copies.append(
                pltpu.make_async_copy(
                    done_ref.at[:, first * DH : (first + count) * DH],
                    out_ref.at[:, columns_from(head * GROUP + first, count)],
                    sems.at[first // count],
                )
            )
            copies[-1].start()
        else:
            new_mean_ref, new_level_ref = refs
            new_level = top + jnp.log2(total)
            for j, columns in enumerate(heads):
                part = slice(j * q_rows, (j + 1) * q_rows)
                new_mean_ref[0, :, columns] = result[part].astype(jnp.bfloat16)
                levels = jnp.where(lanes == first + j, new_level[part], levels)
    for copy in copies:
        copy.wait()
    if not final:
        new_level_ref[0] = levels


def attend_prefix(held, query, state, bias, mask, partial=None, offset=0):
    _, q_rows, wide = query.shape
    pieces = [held[at] for at in sorted(held) if at % KVH == mask]
    parts = len(pieces)
    length = parts * pieces[0].shape[0] * pieces[0].shape[1]
    final = partial is not None
    at = mask if state[0].shape[0] == KVH else 0
    if final:
        out_specs = ANY
        out_shape = jax.ShapeDtypeStruct((q_rows, KVH * wide), jnp.bfloat16)
        scratch = [
            pltpu.VMEM((q_rows, wide), jnp.bfloat16),
            pltpu.SemaphoreType.DMA((GROUP * q_rows // ROWS,)),
        ]
    else:
        out_specs = [VMEM, VMEM]
        out_shape = [
            pltpu.VMEM((1, q_rows, wide), jnp.bfloat16),
            pltpu.VMEM((1, q_rows, DH), jnp.float32),
        ]
        scratch = []
    partial = partial or []
    return pl.pallas_call(
        functools.partial(prefix_kernel, mask, at, parts, offset, final),
        in_specs=[VMEM] * (parts + 4) + [ANY] * len(partial),
        out_specs=out_specs,
        out_shape=out_shape,
        scratch_shapes=scratch,
        input_output_aliases={parts + 4: 0} if partial else {},
        cost_estimate=pl.CostEstimate(
            flops=64 * q_rows * wide * length, bytes_accessed=2**20, transcendentals=0
        ),
        compiler_params=pltpu.CompilerParams(vmem_limit_bytes=48 * 2**20),
        name="attend_prefix",
    )(*pieces, *[in_vmem(array) for array in (query, *state, bias)], *partial)


def swap(array, blks, mask):
    return lax.ppermute(array, "blk", [(i, i ^ mask) for i in range(blks)])


def per_device(queries, span_kv, kv_store, page_ids, page_owner, prefix_len):
    pools = lax.axis_size("pool")
    blks = lax.axis_size("blk")
    stored, page, _ = kv_store.shape
    parts = blks // KVH
    rows = page // parts

    owner = lax.broadcasted_iota(jnp.int32, (pools, 1, page_ids.shape[1]), 0)
    wanted = jnp.where(page_owner[None] == owner, page_ids[None], -1)
    tables = lax.all_to_all(wanted, "pool", split_axis=0, concat_axis=0, tiled=True)
    picked = pick_pages(tables, kv_store, rows)
    picked, span_kv = lax.optimization_barrier((picked, span_kv))
    fetched = lax.all_to_all(picked, "pool", split_axis=0, concat_axis=0, tiled=True)
    span = {0: span_kv}
    bit = blks // 2
    while bit:
        span.update({mask ^ bit: swap(rows_of, blks, bit) for mask, rows_of in list(span.items())})
        bit //= 2
    length = page_ids.shape[1] * page
    state = attend_span(prefix_len, queries, span, length, parts, rows)
    fetched, *state = lax.optimization_barrier((fetched, *state))
    mean, level, query, bias = state
    state = (mean, level)
    ordered, first, second = order_pages(page_owner, fetched)

    def across(piece):
        held = {0: piece}
        bit = blks // 2
        while bit > 1:
            held.update({mask ^ bit: swap(part, blks, bit) for mask, part in list(held.items())})
            bit //= 2
        return {mask: part for mask, part in held.items() if mask % KVH == 2}

    def relayed(held):
        return {mask ^ 1: swap(part, blks, 1) for mask, part in held.items()}

    near = {1: swap(ordered, blks, 1), 0: ordered}
    for mask in range(KVH, blks, KVH):
        near[mask] = swap(ordered, blks, mask)
        near[mask ^ 1] = swap(near[mask], blks, 1)
    far, rest = across(first), across(second)
    out = attend_prefix(near, query, state, bias, 0, [])
    out = attend_prefix(near, query, state, bias, 1, [out])
    out, far = lax.optimization_barrier((out, far))
    far.update(relayed(far))
    states = [attend_prefix(far, query, state, bias, mask) for mask in (2, 3)]
    states, rest = lax.optimization_barrier((states, rest))
    rest.update(relayed(rest))
    offset = first.shape[0] * first.shape[1]
    for mask in (2, 3):
        out = attend_prefix(rest, query, states[mask - 2], bias, mask, [out], offset)
    return out


def solution(mesh):
    in_specs = (
        P(("pool", "blk"), None),
        P(("pool", "blk"), None),
        P("pool", None, None),
        P("pool", None),
        P("pool", None),
        P("pool"),
    )
    out_specs = P(("pool", "blk"), None)
    return jax.shard_map(
        per_device, mesh=mesh, in_specs=in_specs, out_specs=out_specs, check_vma=False
    )
```

```python
import functools
import math

import jax
import jax.numpy as jnp
from jax import lax
from jax.experimental import pallas as pl
from jax.experimental.pallas import tpu as pltpu
from jax.sharding import PartitionSpec as P

KVH = 4
DH = 128
GROUP = 8
CAP = 2
COEF = math.log2(math.e) / math.sqrt(DH)
LOW = -1e30
ROWS = 256
LOADS = 4


SMEM = pl.BlockSpec(memory_space=pltpu.SMEM)
VMEM = pl.BlockSpec(memory_space=pltpu.VMEM)
ANY = pl.BlockSpec(memory_space=pl.ANY)


def columns_from(first, count):
    return pl.ds(pl.multiple_of(first * DH, DH), count * DH)


def pick_kernel(tables_ref, store_ref, out_ref, table, own, load_sems, sems):
    pools, _, listed = tables_ref.shape
    stored, rows, _ = own.shape
    blk = lax.axis_index("blk")
    head = lax.rem(blk, KVH)
    at_rows = pl.ds(pl.multiple_of(lax.div(blk, KVH) * rows, rows), rows)
    loads = [pltpu.make_async_copy(tables_ref, table, load_sems.at[0])]
    for kind in range(2):
        for first in range(0, stored, stored // LOADS):
            pages = slice(first, first + stored // LOADS)
            loads.append(
                pltpu.make_async_copy(
                    store_ref.at[pages, at_rows, columns_from(kind * KVH + head, 1)],
                    own.at[pages, :, kind * DH : (kind + 1) * DH],
                    load_sems.at[len(loads)],
                )
            )
    for load in loads:
        load.start()
    for load in loads:
        load.wait()

    def page_copy(request, slot, page):
        return pltpu.make_async_copy(
            own.at[page], out_ref.at[request, slot], sems.at[request, slot]
        )

    def serve(request, carry):
        def visit(entry, state):
            rank, pages = state
            page = table[request, 0, entry]
            hit = page >= 0
            pages = [jnp.where(hit & (rank == slot), page, pages[slot]) for slot in range(CAP)]
            return rank + hit.astype(jnp.int32), pages

        state = (jnp.int32(0), [jnp.int32(0)] * CAP)
        _, pages = lax.fori_loop(0, listed, visit, state, unroll=listed <= 8)
        for slot in range(CAP):
            page_copy(request, slot, pages[slot]).start()
        return carry

    lax.fori_loop(0, pools, serve, 0)

    def finish(request, carry):
        for slot in range(CAP):
            page_copy(request, slot, 0).wait()
        return carry

    lax.fori_loop(0, pools, finish, 0)


def pick_pages(tables, kv_store, rows):
    pools = tables.shape[0]
    return pl.pallas_call(
        pick_kernel,
        in_specs=[ANY, ANY],
        out_specs=ANY,
        out_shape=pltpu.HBM((pools, CAP, rows, 2 * DH), kv_store.dtype),
        scratch_shapes=[
            pltpu.SMEM(tables.shape, jnp.int32),
            pltpu.VMEM((kv_store.shape[0], rows, 2 * DH), kv_store.dtype),
            pltpu.SemaphoreType.DMA((1 + 2 * LOADS,)),
            pltpu.SemaphoreType.DMA((pools, CAP)),
        ],
        name="pick_pages",
    )(in_vmem(tables), in_hbm(kv_store))


def in_hbm(array):
    return pltpu.with_memory_space_constraint(array, pltpu.HBM)


def in_vmem(array):
    return pltpu.with_memory_space_constraint(array, pltpu.VMEM)


def order_kernel(owners_ref, fetched_ref, first_ref, second_ref):
    half = first_ref.shape[0]
    for entry in range(2 * half):
        owner = owners_ref[0, entry]
        rank = jnp.int32(0)
        for earlier in range(entry):
            rank += (owners_ref[0, earlier] == owner).astype(jnp.int32)
        half_ref = first_ref if entry < half else second_ref
        half_ref[entry % half] = fetched_ref[owner, jnp.minimum(rank, CAP - 1)]


def order_pages(owners, fetched):
    shape = (owners.shape[1] // 2, fetched.shape[2], 2 * DH)
    return pl.pallas_call(
        order_kernel,
        in_specs=[SMEM, VMEM],
        out_specs=[VMEM] * 2,
        out_shape=[pltpu.VMEM(shape, fetched.dtype)] * 2,
        name="order_pages",
    )(owners, in_vmem(fetched))


def scores_of(query_ref, first, count, keys):
    heads = [query_ref[:, (first + j) * DH : (first + j + 1) * DH] for j in range(count)]
    stacked = heads[0] if count == 1 else jnp.concatenate(heads, axis=0)
    return lax.dot_general(
        stacked, keys, (((1,), (1,)), ((), ())), preferred_element_type=jnp.float32
    )


def with_ones(values):
    return jnp.concatenate([values, jnp.ones((values.shape[0], DH), values.dtype)], axis=1)


def span_kernel(masks, parts, rows, limit_ref, query_ref, *refs):
    blocks = len(masks)
    keys_refs, values_refs = refs[:blocks], refs[blocks : 2 * blocks]
    mean_ref, level_ref, copy_ref, bias_ref = refs[2 * blocks :]
    q_rows = query_ref.shape[0]
    count = ROWS // q_rows
    copy_ref[0] = query_ref[...]
    own = lax.axis_index("blk")
    shape = (bias_ref.shape[0], bias_ref.shape[1] // parts)
    index = lax.broadcasted_iota(jnp.int32, shape, 1)
    at_page = lax.div(index, rows) * (parts * rows) + lax.rem(index, rows)
    for step in range(parts):
        position = at_page + lax.rem(lax.div(own, KVH) + step, parts) * rows
        bias_ref[:, step * shape[1] : (step + 1) * shape[1]] = jnp.where(
            position < limit_ref[0], 0.0, LOW
        )
    keys = jnp.concatenate([ref[...] for ref in keys_refs], axis=0)
    values = with_ones(jnp.concatenate([ref[...] for ref in values_refs], axis=0))
    ahead = lax.broadcasted_iota(jnp.int32, (q_rows, q_rows), 0) - lax.broadcasted_iota(
        jnp.int32, (q_rows, q_rows), 1
    )
    bias = [
        jnp.where(ahead >= (jnp.bitwise_xor(own, mask) - own) * q_rows, 0.0, LOW) for mask in masks
    ]
    bias = jnp.concatenate(bias, axis=1)
    bias = jnp.concatenate([bias] * count, axis=0)
    lanes = lax.broadcasted_iota(jnp.int32, (q_rows, DH), 1)
    levels = jnp.zeros((q_rows, DH), jnp.float32)
    for first in range(0, GROUP, count):
        scores = scores_of(query_ref, first, count, keys) + bias
        top = jnp.max(scores, axis=1, keepdims=True)
        weights = jnp.exp2((scores - top) * COEF)
        summed = jnp.dot(
            weights.astype(jnp.bfloat16), values, preferred_element_type=jnp.float32
        )
        total = summed[:, DH:]
        level = top * COEF + jnp.log2(total)
        mean = summed[:, :DH] / total
        for j in range(count):
            at = slice(j * q_rows, (j + 1) * q_rows)
            columns = slice((first + j) * DH, (first + j + 1) * DH)
            mean_ref[0, :, columns] = mean[at].astype(jnp.bfloat16)
            levels = jnp.where(lanes == first + j, level[at], levels)
    level_ref[0] = levels


def attend_span(limit, queries, span, length, parts, rows):
    q_rows = queries.shape[0]
    masks = sorted(span)
    blocks = [span[mask] for mask in masks]
    wide = GROUP * DH

    def head(m):
        return lax.rem(lax.axis_index("blk"), KVH) ^ m

    keys_spec = pl.BlockSpec((q_rows, DH), lambda m: (0, head(m)))
    values_spec = pl.BlockSpec((q_rows, DH), lambda m: (0, KVH + head(m)))
    return pl.pallas_call(
        functools.partial(span_kernel, masks, parts, rows),
        grid=(KVH,),
        in_specs=[SMEM, pl.BlockSpec((q_rows, wide), lambda m: (0, head(m)))]
        + [keys_spec] * len(masks)
        + [values_spec] * len(masks),
        out_specs=[
            pl.BlockSpec((1, q_rows, wide), lambda m: (m, 0, 0)),
            pl.BlockSpec((1, q_rows, DH), lambda m: (m, 0, 0)),
            pl.BlockSpec((1, q_rows, wide), lambda m: (m, 0, 0)),
            pl.BlockSpec((8, length), lambda m: (0, 0)),
        ],
        out_shape=[
            pltpu.VMEM((KVH, q_rows, wide), jnp.bfloat16),
            pltpu.VMEM((KVH, q_rows, DH), jnp.float32),
            pltpu.VMEM((KVH, q_rows, wide), jnp.bfloat16),
            pltpu.VMEM((8, length), jnp.float32),
        ],
        cost_estimate=pl.CostEstimate(
            flops=4 * q_rows * KVH * wide * q_rows * len(masks),
            bytes_accessed=8 * 2**20,
            transcendentals=0,
        ),
        compiler_params=pltpu.CompilerParams(vmem_limit_bytes=48 * 2**20),
        name="attend_span",
    )(limit, in_hbm(queries), *blocks, *blocks)


def prefix_kernel(mask, at, parts, count_in, offset, mode, waiting, *refs):
    pieces = refs[:count_in]
    query_ref, mean_ref, level_ref, bias_ref, *refs = refs[count_in:]
    q_rows = query_ref.shape[1]
    count = ROWS // q_rows
    pages, rows, _ = pieces[0].shape
    length = count_in // parts * pages * rows
    both = [piece[...].reshape(pages * rows, 2 * DH) for piece in pieces]
    both = both[0] if count_in == 1 else jnp.concatenate(both, axis=0)
    keys = both[:, :DH]
    values = with_ones(both[:, DH:])
    own_head = lax.rem(lax.axis_index("blk"), KVH)
    copies = []
    if mode == "write":
        *_, out_ref, done_ref, sems = refs
        if waiting is not None:
            held_head = jnp.bitwise_xor(own_head, waiting)
            copies.append(
                pltpu.make_async_copy(
                    refs[0], out_ref.at[:, columns_from(held_head * GROUP, GROUP)], sems.at[0]
                )
            )
            copies[-1].start()
    elif mode == "hold":
        (done_ref,) = refs
    else:
        new_mean_ref, new_level_ref = refs
    whole = bias_ref.shape[1] // parts
    safe = min(max(whole * 5 // 8 // DH * DH - offset, 0), length)
    lanes = lax.broadcasted_iota(jnp.int32, (q_rows, DH), 1)
    levels = jnp.zeros((q_rows, DH), jnp.float32)
    for first in range(0, GROUP, count):
        raw = scores_of(query_ref.at[mask], first, count, keys)
        scores = []
        for step in range(parts):
            scores.append(raw[:, step * length : step * length + safe])
            if safe < length:
                bias = bias_ref[:1, step * whole + offset + safe : step * whole + offset + length]
                scores.append(raw[:, step * length + safe : (step + 1) * length] + bias)
        scores = jnp.concatenate([part for part in scores if part.shape[1]], axis=1)
        heads = [slice((first + j) * DH, (first + j + 1) * DH) for j in range(count)]
        level = jnp.concatenate(
            [
                jnp.broadcast_to(level_ref[at, :, first + j : first + j + 1], (q_rows, DH))
                for j in range(count)
            ],
            axis=0,
        )
        mean = jnp.concatenate([mean_ref[at, :, columns] for columns in heads], axis=0)
        top = jnp.maximum(jnp.max(scores, axis=1, keepdims=True) * COEF, level)
        tops = jnp.concatenate([top] * (parts * length // DH), axis=1)
        weights = jnp.exp2(scores * COEF - tops)
        old = jnp.exp2(level - top)
        summed = jnp.dot(
            weights.astype(jnp.bfloat16), values, preferred_element_type=jnp.float32
        )
        total = summed[:, DH:] + old
        result = (summed[:, :DH] + mean.astype(jnp.float32) * old) / total
        if mode == "state":
            new_level = top + jnp.log2(total)
            for j, columns in enumerate(heads):
                part = slice(j * q_rows, (j + 1) * q_rows)
                new_mean_ref[0, :, columns] = result[part].astype(jnp.bfloat16)
                levels = jnp.where(lanes == first + j, new_level[part], levels)
        else:
            for j, columns in enumerate(heads):
                done_ref[:, columns] = result[j * q_rows : (j + 1) * q_rows].astype(jnp.bfloat16)
        if mode == "write":
            head = jnp.bitwise_xor(own_head, mask)
            copies.append(
                pltpu.make_async_copy(
                    done_ref.at[:, first * DH : (first + count) * DH],
                    out_ref.at[:, columns_from(head * GROUP + first, count)],
                    sems.at[1 + first // count],
                )
            )
            copies[-1].start()
    for copy in copies:
        copy.wait()
    if mode == "state":
        new_level_ref[0] = levels


def attend_prefix(held, query, state, bias, mask, mode, partial=(), offset=0, waiting=None):
    _, q_rows, wide = query.shape
    groups = [held[at] for at in sorted(held) if at % KVH == mask]
    parts = len(groups)
    pieces = [piece for group in groups for piece in group]
    length = len(pieces) * pieces[0].shape[0] * pieces[0].shape[1]
    at = mask if state[0].shape[0] == KVH else 0
    scratch = []
    if mode == "write":
        out_specs = ANY
        out_shape = jax.ShapeDtypeStruct((q_rows, KVH * wide), jnp.bfloat16)
        scratch = [
            pltpu.VMEM((q_rows, wide), jnp.bfloat16),
            pltpu.SemaphoreType.DMA((1 + GROUP * q_rows // ROWS,)),
        ]
    elif mode == "hold":
        out_specs = VMEM
        out_shape = pltpu.VMEM((q_rows, wide), jnp.bfloat16)
    else:
        out_specs = [VMEM, VMEM]
        out_shape = [
            pltpu.VMEM((1, q_rows, wide), jnp.bfloat16),
            pltpu.VMEM((1, q_rows, DH), jnp.float32),
        ]
    operands = [*pieces, *[in_vmem(array) for array in (query, *state, bias)]]
    if waiting is not None:
        operands.append(in_vmem(waiting[1]))
    waiting_mask = None if waiting is None else waiting[0]
    return pl.pallas_call(
        functools.partial(
            prefix_kernel, mask, at, parts, len(pieces), offset, mode, waiting_mask
        ),
        in_specs=[VMEM] * len(operands) + [ANY] * len(partial),
        out_specs=out_specs,
        out_shape=out_shape,
        scratch_shapes=scratch,
        input_output_aliases={len(operands): 0} if partial else {},
        cost_estimate=pl.CostEstimate(
            flops=64 * q_rows * wide * length, bytes_accessed=2**20, transcendentals=0
        ),
        compiler_params=pltpu.CompilerParams(vmem_limit_bytes=48 * 2**20),
        name="attend_prefix",
    )(*operands, *partial)


def swap(array, blks, mask):
    return lax.ppermute(array, "blk", [(i, i ^ mask) for i in range(blks)])


def per_device(queries, span_kv, kv_store, page_ids, page_owner, prefix_len):
    pools = lax.axis_size("pool")
    blks = lax.axis_size("blk")
    stored, page, _ = kv_store.shape
    parts = blks // KVH
    rows = page // parts

    owner = lax.broadcasted_iota(jnp.int32, (pools, 1, page_ids.shape[1]), 0)
    wanted = jnp.where(page_owner[None] == owner, page_ids[None], -1)
    tables = lax.all_to_all(wanted, "pool", split_axis=0, concat_axis=0, tiled=True)
    picked = pick_pages(tables, kv_store, rows)
    picked, span_kv = lax.optimization_barrier((picked, span_kv))
    fetched = lax.all_to_all(picked, "pool", split_axis=0, concat_axis=0, tiled=True)
    span = {0: span_kv}
    bit = blks // 2
    while bit:
        span.update({mask ^ bit: swap(rows_of, blks, bit) for mask, rows_of in list(span.items())})
        bit //= 2
    length = page_ids.shape[1] * page
    state = attend_span(prefix_len, queries, span, length, parts, rows)
    fetched, *state = lax.optimization_barrier((fetched, *state))
    mean, level, query, bias = state
    state = (mean, level)
    first, second = order_pages(page_owner, fetched)

    def across(piece):
        held = {0: [piece]}
        bit = blks // 2
        while bit > 1:
            held.update(
                {mask ^ bit: [swap(part[0], blks, bit)] for mask, part in list(held.items())}
            )
            bit //= 2
        return {mask: part for mask, part in held.items() if mask % KVH == 2}

    def relayed(held):
        return {mask ^ 1: [swap(part, blks, 1) for part in parts] for mask, parts in held.items()}

    near = {0: [first, second]}
    for mask in range(KVH, blks, KVH):
        near[mask] = [swap(first, blks, mask), swap(second, blks, mask)]
    near.update(relayed(near))
    far, rest = across(first), across(second)
    attend = functools.partial(attend_prefix, query=query, bias=bias)
    out = attend(near, state=state, mask=0, mode="write")
    out = attend(near, state=state, mask=1, mode="write", partial=[out])
    out, far = lax.optimization_barrier((out, far))
    far.update(relayed(far))
    states = [attend(far, state=state, mask=mask, mode="state") for mask in (2, 3)]
    states, rest = lax.optimization_barrier((states, rest))
    rest.update(relayed(rest))
    offset = first.shape[0] * first.shape[1]
    out = attend(
        rest, state=states[0], mask=2, mode="write", partial=[out], offset=offset
    )
    return attend(
        rest, state=states[1], mask=3, mode="write", partial=[out], offset=offset
    )


def solution(mesh):
    in_specs = (
        P(("pool", "blk"), None),
        P(("pool", "blk"), None),
        P("pool", None, None),
        P("pool", None),
        P("pool", None),
        P("pool"),
    )
    out_specs = P(("pool", "blk"), None)
    return jax.shard_map(
        per_device, mesh=mesh, in_specs=in_specs, out_specs=out_specs, check_vma=False
    )
```

```python
import functools
import math

import jax
import jax.numpy as jnp
from jax import lax
from jax.experimental import pallas as pl
from jax.experimental.pallas import tpu as pltpu
from jax.sharding import PartitionSpec as P

KVH = 4
DH = 128
GROUP = 8
CAP = 2
COEF = math.log2(math.e) / math.sqrt(DH)
LOW = -1e30
ROWS = 256
LOADS = 4


SMEM = pl.BlockSpec(memory_space=pltpu.SMEM)
VMEM = pl.BlockSpec(memory_space=pltpu.VMEM)
ANY = pl.BlockSpec(memory_space=pl.ANY)


def columns_from(first, count):
    return pl.ds(pl.multiple_of(first * DH, DH), count * DH)


def pick_kernel(tables_ref, store_ref, out_ref, table, own, load_sems, sems):
    pools, _, listed = tables_ref.shape
    stored, rows, _ = own.shape
    blk = lax.axis_index("blk")
    head = lax.rem(blk, KVH)
    at_rows = pl.ds(pl.multiple_of(lax.div(blk, KVH) * rows, rows), rows)
    loads = [pltpu.make_async_copy(tables_ref, table, load_sems.at[0])]
    for kind in range(2):
        for first in range(0, stored, stored // LOADS):
            pages = slice(first, first + stored // LOADS)
            loads.append(
                pltpu.make_async_copy(
                    store_ref.at[pages, at_rows, columns_from(kind * KVH + head, 1)],
                    own.at[pages, :, kind * DH : (kind + 1) * DH],
                    load_sems.at[len(loads)],
                )
            )
    for load in loads:
        load.start()
    for load in loads:
        load.wait()

    def page_copy(request, slot, page):
        return pltpu.make_async_copy(
            own.at[page], out_ref.at[request, slot], sems.at[request, slot]
        )

    def serve(request, carry):
        def visit(entry, state):
            rank, pages = state
            page = table[request, 0, entry]
            hit = page >= 0
            pages = [jnp.where(hit & (rank == slot), page, pages[slot]) for slot in range(CAP)]
            return rank + hit.astype(jnp.int32), pages

        state = (jnp.int32(0), [jnp.int32(0)] * CAP)
        _, pages = lax.fori_loop(0, listed, visit, state, unroll=listed <= 8)
        for slot in range(CAP):
            page_copy(request, slot, pages[slot]).start()
        return carry

    lax.fori_loop(0, pools, serve, 0)

    def finish(request, carry):
        for slot in range(CAP):
            page_copy(request, slot, 0).wait()
        return carry

    lax.fori_loop(0, pools, finish, 0)


def pick_pages(tables, kv_store, rows):
    pools = tables.shape[0]
    return pl.pallas_call(
        pick_kernel,
        in_specs=[ANY, ANY],
        out_specs=ANY,
        out_shape=pltpu.HBM((pools, CAP, rows, 2 * DH), kv_store.dtype),
        scratch_shapes=[
            pltpu.SMEM(tables.shape, jnp.int32),
            pltpu.VMEM((kv_store.shape[0], rows, 2 * DH), kv_store.dtype),
            pltpu.SemaphoreType.DMA((1 + 2 * LOADS,)),
            pltpu.SemaphoreType.DMA((pools, CAP)),
        ],
        name="pick_pages",
    )(in_vmem(tables), in_hbm(kv_store))


def in_hbm(array):
    return pltpu.with_memory_space_constraint(array, pltpu.HBM)


def in_vmem(array):
    return pltpu.with_memory_space_constraint(array, pltpu.VMEM)


def order_kernel(owners_ref, fetched_ref, first_ref, second_ref):
    half = first_ref.shape[0]
    for entry in range(2 * half):
        owner = owners_ref[0, entry]
        rank = jnp.int32(0)
        for earlier in range(entry):
            rank += (owners_ref[0, earlier] == owner).astype(jnp.int32)
        half_ref = first_ref if entry < half else second_ref
        half_ref[entry % half] = fetched_ref[owner, jnp.minimum(rank, CAP - 1)]


def order_pages(owners, fetched):
    shape = (owners.shape[1] // 2, fetched.shape[2], 2 * DH)
    return pl.pallas_call(
        order_kernel,
        in_specs=[SMEM, VMEM],
        out_specs=[VMEM] * 2,
        out_shape=[pltpu.VMEM(shape, fetched.dtype)] * 2,
        name="order_pages",
    )(owners, in_vmem(fetched))


def scores_of(query_ref, first, count, keys):
    heads = [query_ref[:, (first + j) * DH : (first + j + 1) * DH] for j in range(count)]
    stacked = heads[0] if count == 1 else jnp.concatenate(heads, axis=0)
    return lax.dot_general(
        stacked, keys, (((1,), (1,)), ((), ())), preferred_element_type=jnp.float32
    )


def with_ones(values):
    return jnp.concatenate([values, jnp.ones((values.shape[0], DH), values.dtype)], axis=1)


def span_kernel(masks, parts, rows, limit_ref, query_ref, *refs):
    blocks = len(masks)
    keys_refs, values_refs = refs[:blocks], refs[blocks : 2 * blocks]
    mean_ref, level_ref, copy_ref, bias_ref = refs[2 * blocks :]
    q_rows = query_ref.shape[0]
    count = ROWS // q_rows
    copy_ref[0] = query_ref[...]
    own = lax.axis_index("blk")
    shape = (bias_ref.shape[0], bias_ref.shape[1] // parts)
    index = lax.broadcasted_iota(jnp.int32, shape, 1)
    at_page = lax.div(index, rows) * (parts * rows) + lax.rem(index, rows)
    for step in range(parts):
        position = at_page + lax.rem(lax.div(own, KVH) + step, parts) * rows
        bias_ref[:, step * shape[1] : (step + 1) * shape[1]] = jnp.where(
            position < limit_ref[0], 0.0, LOW
        )
    keys = jnp.concatenate([ref[...] for ref in keys_refs], axis=0)
    values = with_ones(jnp.concatenate([ref[...] for ref in values_refs], axis=0))
    ahead = lax.broadcasted_iota(jnp.int32, (q_rows, q_rows), 0) - lax.broadcasted_iota(
        jnp.int32, (q_rows, q_rows), 1
    )
    bias = [
        jnp.where(ahead >= (jnp.bitwise_xor(own, mask) - own) * q_rows, 0.0, LOW) for mask in masks
    ]
    bias = jnp.concatenate(bias, axis=1)
    bias = jnp.concatenate([bias] * count, axis=0)
    lanes = lax.broadcasted_iota(jnp.int32, (q_rows, DH), 1)
    levels = jnp.zeros((q_rows, DH), jnp.float32)
    for first in range(0, GROUP, count):
        scores = scores_of(query_ref, first, count, keys) + bias
        top = jnp.max(scores, axis=1, keepdims=True)
        weights = jnp.exp2((scores - top) * COEF)
        summed = jnp.dot(
            weights.astype(jnp.bfloat16), values, preferred_element_type=jnp.float32
        )
        total = summed[:, DH:]
        level = top * COEF + jnp.log2(total)
        mean = summed[:, :DH] / total
        for j in range(count):
            at = slice(j * q_rows, (j + 1) * q_rows)
            columns = slice((first + j) * DH, (first + j + 1) * DH)
            mean_ref[0, :, columns] = mean[at].astype(jnp.bfloat16)
            levels = jnp.where(lanes == first + j, level[at], levels)
    level_ref[0] = levels


def attend_span(limit, queries, span, length, parts, rows):
    q_rows = queries.shape[0]
    masks = sorted(span)
    blocks = [span[mask] for mask in masks]
    wide = GROUP * DH

    def head(m):
        return lax.rem(lax.axis_index("blk"), KVH) ^ m

    keys_spec = pl.BlockSpec((q_rows, DH), lambda m: (0, head(m)))
    values_spec = pl.BlockSpec((q_rows, DH), lambda m: (0, KVH + head(m)))
    return pl.pallas_call(
        functools.partial(span_kernel, masks, parts, rows),
        grid=(KVH,),
        in_specs=[SMEM, pl.BlockSpec((q_rows, wide), lambda m: (0, head(m)))]
        + [keys_spec] * len(masks)
        + [values_spec] * len(masks),
        out_specs=[
            pl.BlockSpec((1, q_rows, wide), lambda m: (m, 0, 0)),
            pl.BlockSpec((1, q_rows, DH), lambda m: (m, 0, 0)),
            pl.BlockSpec((1, q_rows, wide), lambda m: (m, 0, 0)),
            pl.BlockSpec((8, length), lambda m: (0, 0)),
        ],
        out_shape=[
            pltpu.VMEM((KVH, q_rows, wide), jnp.bfloat16),
            pltpu.VMEM((KVH, q_rows, DH), jnp.float32),
            pltpu.VMEM((KVH, q_rows, wide), jnp.bfloat16),
            pltpu.VMEM((8, length), jnp.float32),
        ],
        cost_estimate=pl.CostEstimate(
            flops=4 * q_rows * KVH * wide * q_rows * len(masks),
            bytes_accessed=8 * 2**20,
            transcendentals=0,
        ),
        compiler_params=pltpu.CompilerParams(vmem_limit_bytes=48 * 2**20),
        name="attend_span",
    )(limit, in_hbm(queries), *blocks, *blocks)


def prefix_kernel(mask, at, parts, count_in, offset, mode, waiting, *refs):
    pieces = refs[:count_in]
    query_ref, mean_ref, level_ref, bias_ref, *refs = refs[count_in:]
    q_rows = query_ref.shape[1]
    count = ROWS // q_rows
    pages, rows, _ = pieces[0].shape
    length = count_in // parts * pages * rows
    both = [piece[...].reshape(pages * rows, 2 * DH) for piece in pieces]
    both = both[0] if count_in == 1 else jnp.concatenate(both, axis=0)
    keys = both[:, :DH]
    values = with_ones(both[:, DH:])
    own_head = lax.rem(lax.axis_index("blk"), KVH)
    copies = []
    if mode == "write":
        *_, out_ref, done_ref, sems = refs
    else:
        new_mean_ref, new_level_ref = refs
    whole = bias_ref.shape[1] // parts
    safe = min(max(whole * 5 // 8 // DH * DH - offset, 0), length)
    lanes = lax.broadcasted_iota(jnp.int32, (q_rows, DH), 1)
    levels = jnp.zeros((q_rows, DH), jnp.float32)
    for first in range(0, GROUP, count):
        raw = scores_of(query_ref.at[mask], first, count, keys)
        scores = []
        for step in range(parts):
            scores.append(raw[:, step * length : step * length + safe])
            if safe < length:
                bias = bias_ref[:1, step * whole + offset + safe : step * whole + offset + length]
                scores.append(raw[:, step * length + safe : (step + 1) * length] + bias)
        scores = jnp.concatenate([part for part in scores if part.shape[1]], axis=1)
        heads = [slice((first + j) * DH, (first + j + 1) * DH) for j in range(count)]
        level = jnp.concatenate(
            [
                jnp.broadcast_to(level_ref[at, :, first + j : first + j + 1], (q_rows, DH))
                for j in range(count)
            ],
            axis=0,
        )
        mean = jnp.concatenate([mean_ref[at, :, columns] for columns in heads], axis=0)
        top = jnp.maximum(jnp.max(scores, axis=1, keepdims=True) * COEF, level)
        tops = jnp.concatenate([top] * (parts * length // DH), axis=1)
        weights = jnp.exp2(scores * COEF - tops)
        old = jnp.exp2(level - top)
        summed = jnp.dot(
            weights.astype(jnp.bfloat16), values, preferred_element_type=jnp.float32
        )
        total = summed[:, DH:] + old
        result = (summed[:, :DH] + mean.astype(jnp.float32) * old) / total
        if mode == "state":
            new_level = top + jnp.log2(total)
            for j, columns in enumerate(heads):
                part = slice(j * q_rows, (j + 1) * q_rows)
                new_mean_ref[0, :, columns] = result[part].astype(jnp.bfloat16)
                levels = jnp.where(lanes == first + j, new_level[part], levels)
        else:
            for j, columns in enumerate(heads):
                done_ref[0, :, columns] = result[j * q_rows : (j + 1) * q_rows].astype(jnp.bfloat16)
        if mode == "write":
            head = jnp.bitwise_xor(own_head, mask)
            copies.append(
                pltpu.make_async_copy(
                    done_ref.at[0, :, first * DH : (first + count) * DH],
                    out_ref.at[:, columns_from(head * GROUP + first, count)],
                    sems.at[1 + first // count],
                )
            )
            copies[-1].start()
        if mode == "write" and first == 0 and waiting is not None:
            done_ref[1] = refs[0][0]
            head = jnp.bitwise_xor(own_head, waiting)
            copies.append(
                pltpu.make_async_copy(
                    done_ref.at[1], out_ref.at[:, columns_from(head * GROUP, GROUP)], sems.at[0]
                )
            )
            copies[-1].start()
    for copy in copies:
        copy.wait()
    if mode == "state":
        new_level_ref[0] = levels


def attend_prefix(held, query, state, bias, mask, mode, partial=(), offset=0, waiting=None):
    _, q_rows, wide = query.shape
    groups = [held[at] for at in sorted(held) if at % KVH == mask]
    parts = len(groups)
    pieces = [piece for group in groups for piece in group]
    length = len(pieces) * pieces[0].shape[0] * pieces[0].shape[1]
    at = mask if state[0].shape[0] == KVH else 0
    scratch = []
    if mode == "write":
        out_specs = ANY
        out_shape = jax.ShapeDtypeStruct((q_rows, KVH * wide), jnp.bfloat16)
        scratch = [
            pltpu.VMEM((2, q_rows, wide), jnp.bfloat16),
            pltpu.SemaphoreType.DMA((1 + GROUP * q_rows // ROWS,)),
        ]
    else:
        out_specs = [VMEM, VMEM]
        out_shape = [
            pltpu.VMEM((1, q_rows, wide), jnp.bfloat16),
            pltpu.VMEM((1, q_rows, DH), jnp.float32),
        ]
    operands = [*pieces, *[in_vmem(array) for array in (query, *state, bias)]]
    if waiting is not None:
        operands.append(in_vmem(waiting[1]))
    waiting_mask = None if waiting is None else waiting[0]
    return pl.pallas_call(
        functools.partial(
            prefix_kernel, mask, at, parts, len(pieces), offset, mode, waiting_mask
        ),
        in_specs=[VMEM] * len(operands) + [ANY] * len(partial),
        out_specs=out_specs,
        out_shape=out_shape,
        scratch_shapes=scratch,
        input_output_aliases={len(operands): 0} if partial else {},
        cost_estimate=pl.CostEstimate(
            flops=64 * q_rows * wide * length, bytes_accessed=2**20, transcendentals=0
        ),
        compiler_params=pltpu.CompilerParams(vmem_limit_bytes=48 * 2**20),
        name="attend_prefix",
    )(*operands, *partial)


def swap(array, blks, mask):
    return lax.ppermute(array, "blk", [(i, i ^ mask) for i in range(blks)])


def per_device(queries, span_kv, kv_store, page_ids, page_owner, prefix_len):
    pools = lax.axis_size("pool")
    blks = lax.axis_size("blk")
    stored, page, _ = kv_store.shape
    parts = blks // KVH
    rows = page // parts

    owner = lax.broadcasted_iota(jnp.int32, (pools, 1, page_ids.shape[1]), 0)
    wanted = jnp.where(page_owner[None] == owner, page_ids[None], -1)
    tables = lax.all_to_all(wanted, "pool", split_axis=0, concat_axis=0, tiled=True)
    picked = pick_pages(tables, kv_store, rows)
    picked, span_kv = lax.optimization_barrier((picked, span_kv))
    fetched = lax.all_to_all(picked, "pool", split_axis=0, concat_axis=0, tiled=True)
    span = {0: span_kv}
    bit = blks // 2
    while bit:
        span.update({mask ^ bit: swap(rows_of, blks, bit) for mask, rows_of in list(span.items())})
        bit //= 2
    length = page_ids.shape[1] * page
    state = attend_span(prefix_len, queries, span, length, parts, rows)
    fetched, *state = lax.optimization_barrier((fetched, *state))
    mean, level, query, bias = state
    state = (mean, level)
    first, second = order_pages(page_owner, fetched)

    def across(piece):
        held = {0: [piece]}
        bit = blks // 2
        while bit > 1:
            held.update(
                {mask ^ bit: [swap(part[0], blks, bit)] for mask, part in list(held.items())}
            )
            bit //= 2
        return {mask: part for mask, part in held.items() if mask % KVH == 2}

    def relayed(held):
        return {mask ^ 1: [swap(part, blks, 1) for part in parts] for mask, parts in held.items()}

    near = {0: [first, second]}
    for mask in range(KVH, blks, KVH):
        near[mask] = [swap(first, blks, mask), swap(second, blks, mask)]
    near.update(relayed(near))
    far, rest = across(first), across(second)
    attend = functools.partial(attend_prefix, query=query, bias=bias)
    out = attend(near, state=state, mask=0, mode="write")
    out = attend(near, state=state, mask=1, mode="write", partial=[out])
    out, far = lax.optimization_barrier((out, far))
    far.update(relayed(far))
    states = [attend(far, state=state, mask=mask, mode="state") for mask in (2, 3)]
    states, rest = lax.optimization_barrier((states, rest))
    rest.update(relayed(rest))
    offset = first.shape[0] * first.shape[1]
    done, _ = attend(rest, state=states[0], mask=2, mode="state", offset=offset)
    return attend(
        rest,
        state=states[1],
        mask=3,
        mode="write",
        partial=[out],
        offset=offset,
        waiting=(2, done),
    )


def solution(mesh):
    in_specs = (
        P(("pool", "blk"), None),
        P(("pool", "blk"), None),
        P("pool", None, None),
        P("pool", None),
        P("pool", None),
        P("pool"),
    )
    out_specs = P(("pool", "blk"), None)
    return jax.shard_map(
        per_device, mesh=mesh, in_specs=in_specs, out_specs=out_specs, check_vma=False
    )
```

```python
import functools
import math

import jax
import jax.numpy as jnp
from jax import lax
from jax.experimental import pallas as pl
from jax.experimental.pallas import tpu as pltpu
from jax.sharding import PartitionSpec as P

KVH = 4
DH = 128
GROUP = 8
CAP = 2
COEF = math.log2(math.e) / math.sqrt(DH)
LOW = -1e30
ROWS = 256
LOADS = 4


SMEM = pl.BlockSpec(memory_space=pltpu.SMEM)
VMEM = pl.BlockSpec(memory_space=pltpu.VMEM)
ANY = pl.BlockSpec(memory_space=pl.ANY)


def columns_from(first, count):
    return pl.ds(pl.multiple_of(first * DH, DH), count * DH)


def pick_kernel(tables_ref, store_ref, out_ref, table, own, load_sems, sems):
    pools, _, listed = tables_ref.shape
    stored, rows, _ = own.shape
    blk = lax.axis_index("blk")
    head = lax.rem(blk, KVH)
    at_rows = pl.ds(pl.multiple_of(lax.div(blk, KVH) * rows, rows), rows)
    loads = [pltpu.make_async_copy(tables_ref, table, load_sems.at[0])]
    for kind in range(2):
        for first in range(0, stored, stored // LOADS):
            pages = slice(first, first + stored // LOADS)
            loads.append(
                pltpu.make_async_copy(
                    store_ref.at[pages, at_rows, columns_from(kind * KVH + head, 1)],
                    own.at[pages, :, kind * DH : (kind + 1) * DH],
                    load_sems.at[len(loads)],
                )
            )
    for load in loads:
        load.start()
    for load in loads:
        load.wait()

    def page_copy(request, slot, page):
        return pltpu.make_async_copy(
            own.at[page], out_ref.at[request, slot], sems.at[request, slot]
        )

    def serve(request, carry):
        def visit(entry, state):
            rank, pages = state
            page = table[request, 0, entry]
            hit = page >= 0
            pages = [jnp.where(hit & (rank == slot), page, pages[slot]) for slot in range(CAP)]
            return rank + hit.astype(jnp.int32), pages

        state = (jnp.int32(0), [jnp.int32(0)] * CAP)
        _, pages = lax.fori_loop(0, listed, visit, state, unroll=listed <= 8)
        for slot in range(CAP):
            page_copy(request, slot, pages[slot]).start()
        return carry

    lax.fori_loop(0, pools, serve, 0)

    def finish(request, carry):
        for slot in range(CAP):
            page_copy(request, slot, 0).wait()
        return carry

    lax.fori_loop(0, pools, finish, 0)


def pick_pages(tables, kv_store, rows):
    pools = tables.shape[0]
    return pl.pallas_call(
        pick_kernel,
        in_specs=[ANY, ANY],
        out_specs=ANY,
        out_shape=pltpu.HBM((pools, CAP, rows, 2 * DH), kv_store.dtype),
        scratch_shapes=[
            pltpu.SMEM(tables.shape, jnp.int32),
            pltpu.VMEM((kv_store.shape[0], rows, 2 * DH), kv_store.dtype),
            pltpu.SemaphoreType.DMA((1 + 2 * LOADS,)),
            pltpu.SemaphoreType.DMA((pools, CAP)),
        ],
        name="pick_pages",
    )(in_vmem(tables), in_hbm(kv_store))


def in_hbm(array):
    return pltpu.with_memory_space_constraint(array, pltpu.HBM)


def in_vmem(array):
    return pltpu.with_memory_space_constraint(array, pltpu.VMEM)


def order_kernel(owners_ref, fetched_ref, first_ref, second_ref):
    half = first_ref.shape[0]
    for entry in range(2 * half):
        owner = owners_ref[0, entry]
        rank = jnp.int32(0)
        for earlier in range(entry):
            rank += (owners_ref[0, earlier] == owner).astype(jnp.int32)
        half_ref = first_ref if entry < half else second_ref
        half_ref[entry % half] = fetched_ref[owner, jnp.minimum(rank, CAP - 1)]


def order_pages(owners, fetched):
    shape = (owners.shape[1] // 2, fetched.shape[2], 2 * DH)
    return pl.pallas_call(
        order_kernel,
        in_specs=[SMEM, VMEM],
        out_specs=[VMEM] * 2,
        out_shape=[pltpu.VMEM(shape, fetched.dtype)] * 2,
        name="order_pages",
    )(owners, in_vmem(fetched))


def scores_of(query_ref, first, count, keys):
    heads = [query_ref[:, (first + j) * DH : (first + j + 1) * DH] for j in range(count)]
    stacked = heads[0] if count == 1 else jnp.concatenate(heads, axis=0)
    return lax.dot_general(
        stacked, keys, (((1,), (1,)), ((), ())), preferred_element_type=jnp.float32
    )


def with_ones(values):
    return jnp.concatenate([values, jnp.ones((values.shape[0], DH), values.dtype)], axis=1)


def span_kernel(masks, parts, rows, limit_ref, query_ref, *refs):
    blocks = len(masks)
    keys_refs, values_refs = refs[:blocks], refs[blocks : 2 * blocks]
    mean_ref, level_ref, copy_ref, bias_ref = refs[2 * blocks :]
    q_rows = query_ref.shape[0]
    count = ROWS // q_rows
    copy_ref[0] = query_ref[...]
    own = lax.axis_index("blk")
    shape = (bias_ref.shape[0], bias_ref.shape[1] // parts)
    index = lax.broadcasted_iota(jnp.int32, shape, 1)
    at_page = lax.div(index, rows) * (parts * rows) + lax.rem(index, rows)
    for step in range(parts):
        position = at_page + lax.rem(lax.div(own, KVH) + step, parts) * rows
        bias_ref[:, step * shape[1] : (step + 1) * shape[1]] = jnp.where(
            position < limit_ref[0], 0.0, LOW
        )
    keys = jnp.concatenate([ref[...] for ref in keys_refs], axis=0)
    values = with_ones(jnp.concatenate([ref[...] for ref in values_refs], axis=0))
    ahead = lax.broadcasted_iota(jnp.int32, (q_rows, q_rows), 0) - lax.broadcasted_iota(
        jnp.int32, (q_rows, q_rows), 1
    )
    bias = [
        jnp.where(ahead >= (jnp.bitwise_xor(own, mask) - own) * q_rows, 0.0, LOW) for mask in masks
    ]
    bias = jnp.concatenate(bias, axis=1)
    bias = jnp.concatenate([bias] * count, axis=0)
    lanes = lax.broadcasted_iota(jnp.int32, (q_rows, DH), 1)
    levels = jnp.zeros((q_rows, DH), jnp.float32)
    for first in range(0, GROUP, count):
        scores = scores_of(query_ref, first, count, keys) + bias
        top = jnp.max(scores, axis=1, keepdims=True)
        weights = jnp.exp2((scores - top) * COEF)
        summed = jnp.dot(
            weights.astype(jnp.bfloat16), values, preferred_element_type=jnp.float32
        )
        total = summed[:, DH:]
        level = top * COEF + jnp.log2(total)
        mean = summed[:, :DH] / total
        for j in range(count):
            at = slice(j * q_rows, (j + 1) * q_rows)
            columns = slice((first + j) * DH, (first + j + 1) * DH)
            mean_ref[0, :, columns] = mean[at].astype(jnp.bfloat16)
            levels = jnp.where(lanes == first + j, level[at], levels)
    level_ref[0] = levels


def attend_span(limit, queries, span, length, parts, rows):
    q_rows = queries.shape[0]
    masks = sorted(span)
    blocks = [span[mask] for mask in masks]
    wide = GROUP * DH

    def head(m):
        return lax.rem(lax.axis_index("blk"), KVH) ^ m

    keys_spec = pl.BlockSpec((q_rows, DH), lambda m: (0, head(m)))
    values_spec = pl.BlockSpec((q_rows, DH), lambda m: (0, KVH + head(m)))
    return pl.pallas_call(
        functools.partial(span_kernel, masks, parts, rows),
        grid=(KVH,),
        in_specs=[SMEM, pl.BlockSpec((q_rows, wide), lambda m: (0, head(m)))]
        + [keys_spec] * len(masks)
        + [values_spec] * len(masks),
        out_specs=[
            pl.BlockSpec((1, q_rows, wide), lambda m: (m, 0, 0)),
            pl.BlockSpec((1, q_rows, DH), lambda m: (m, 0, 0)),
            pl.BlockSpec((1, q_rows, wide), lambda m: (m, 0, 0)),
            pl.BlockSpec((8, length), lambda m: (0, 0)),
        ],
        out_shape=[
            pltpu.VMEM((KVH, q_rows, wide), jnp.bfloat16),
            pltpu.VMEM((KVH, q_rows, DH), jnp.float32),
            pltpu.VMEM((KVH, q_rows, wide), jnp.bfloat16),
            pltpu.VMEM((8, length), jnp.float32),
        ],
        cost_estimate=pl.CostEstimate(
            flops=4 * q_rows * KVH * wide * q_rows * len(masks),
            bytes_accessed=8 * 2**20,
            transcendentals=0,
        ),
        compiler_params=pltpu.CompilerParams(vmem_limit_bytes=48 * 2**20),
        name="attend_span",
    )(limit, in_hbm(queries), *blocks, *blocks)


def prefix_kernel(mask, at, parts, count_in, offset, mode, waiting, *refs):
    pieces = refs[:count_in]
    query_ref, mean_ref, level_ref, bias_ref, *refs = refs[count_in:]
    q_rows = query_ref.shape[1]
    count = ROWS // q_rows
    pages, rows, _ = pieces[0].shape
    length = count_in // parts * pages * rows
    both = [piece[...].reshape(pages * rows, 2 * DH) for piece in pieces]
    both = both[0] if count_in == 1 else jnp.concatenate(both, axis=0)
    keys = both[:, :DH]
    values = with_ones(both[:, DH:])
    own_head = lax.rem(lax.axis_index("blk"), KVH)
    copies = []
    if mode == "write":
        *_, out_ref, done_ref, sems = refs
    else:
        new_mean_ref = refs[0]
    whole = bias_ref.shape[1] // parts
    safe = min(max(whole * 5 // 8 // DH * DH - offset, 0), length)
    lanes = lax.broadcasted_iota(jnp.int32, (q_rows, DH), 1)
    levels = jnp.zeros((q_rows, DH), jnp.float32)
    for first in range(0, GROUP, count):
        raw = scores_of(query_ref.at[mask], first, count, keys)
        scores = []
        for step in range(parts):
            scores.append(raw[:, step * length : step * length + safe])
            if safe < length:
                bias = bias_ref[:1, step * whole + offset + safe : step * whole + offset + length]
                scores.append(raw[:, step * length + safe : (step + 1) * length] + bias)
        scores = jnp.concatenate([part for part in scores if part.shape[1]], axis=1)
        heads = [slice((first + j) * DH, (first + j + 1) * DH) for j in range(count)]
        level = jnp.concatenate(
            [
                jnp.broadcast_to(level_ref[at, :, first + j : first + j + 1], (q_rows, DH))
                for j in range(count)
            ],
            axis=0,
        )
        mean = jnp.concatenate([mean_ref[at, :, columns] for columns in heads], axis=0)
        top = jnp.maximum(jnp.max(scores, axis=1, keepdims=True) * COEF, level)
        tops = jnp.concatenate([top] * (parts * length // DH), axis=1)
        weights = jnp.exp2(scores * COEF - tops)
        old = jnp.exp2(level - top)
        summed = jnp.dot(
            weights.astype(jnp.bfloat16), values, preferred_element_type=jnp.float32
        )
        total = summed[:, DH:] + old
        result = (summed[:, :DH] + mean.astype(jnp.float32) * old) / total
        for j, columns in enumerate(heads):
            part = slice(j * q_rows, (j + 1) * q_rows)
            rounded = result[part].astype(jnp.bfloat16)
            if mode == "write":
                done_ref[0, :, columns] = rounded
            else:
                new_mean_ref[0, :, columns] = rounded
            if mode == "state":
                levels = jnp.where(lanes == first + j, (top + jnp.log2(total))[part], levels)
        if mode == "write":
            head = jnp.bitwise_xor(own_head, mask)
            copies.append(
                pltpu.make_async_copy(
                    done_ref.at[0, :, first * DH : (first + count) * DH],
                    out_ref.at[:, columns_from(head * GROUP + first, count)],
                    sems.at[first // count],
                )
            )
            copies[-1].start()
        if mode == "write" and first == 0:
            for place, other in enumerate(waiting):
                done_ref[1 + place] = refs[place][0]
                head = jnp.bitwise_xor(own_head, other)
                copies.append(
                    pltpu.make_async_copy(
                        done_ref.at[1 + place],
                        out_ref.at[:, columns_from(head * GROUP, GROUP)],
                        sems.at[GROUP * q_rows // ROWS + place],
                    )
                )
                copies[-1].start()
    for copy in copies:
        copy.wait()
    if mode == "state":
        refs[1][0] = levels


def attend_prefix(held, query, state, bias, mask, mode, offset=0, waiting=()):
    _, q_rows, wide = query.shape
    groups = [held[at] for at in sorted(held) if at % KVH == mask]
    parts = len(groups)
    pieces = [piece for group in groups for piece in group]
    length = len(pieces) * pieces[0].shape[0] * pieces[0].shape[1]
    at = mask if state[0].shape[0] == KVH else 0
    mean_shape = pltpu.VMEM((1, q_rows, wide), jnp.bfloat16)
    scratch = []
    if mode == "write":
        out_specs = ANY
        out_shape = jax.ShapeDtypeStruct((q_rows, KVH * wide), jnp.bfloat16)
        scratch = [
            pltpu.VMEM((1 + len(waiting), q_rows, wide), jnp.bfloat16),
            pltpu.SemaphoreType.DMA((GROUP * q_rows // ROWS + len(waiting),)),
        ]
    elif mode == "mean":
        out_specs, out_shape = VMEM, mean_shape
    else:
        out_specs = [VMEM, VMEM]
        out_shape = [mean_shape, pltpu.VMEM((1, q_rows, DH), jnp.float32)]
    operands = [query, *state, bias, *[result for _, result in waiting]]
    operands = [*pieces, *[in_vmem(array) for array in operands]]
    masks = [other for other, _ in waiting]
    return pl.pallas_call(
        functools.partial(prefix_kernel, mask, at, parts, len(pieces), offset, mode, masks),
        in_specs=[VMEM] * len(operands),
        out_specs=out_specs,
        out_shape=out_shape,
        scratch_shapes=scratch,
        cost_estimate=pl.CostEstimate(
            flops=64 * q_rows * wide * length, bytes_accessed=2**20, transcendentals=0
        ),
        compiler_params=pltpu.CompilerParams(vmem_limit_bytes=48 * 2**20),
        name="attend_prefix",
    )(*operands)


def swap(array, blks, mask):
    return lax.ppermute(array, "blk", [(i, i ^ mask) for i in range(blks)])


def per_device(queries, span_kv, kv_store, page_ids, page_owner, prefix_len):
    pools = lax.axis_size("pool")
    blks = lax.axis_size("blk")
    stored, page, _ = kv_store.shape
    parts = blks // KVH
    rows = page // parts

    owner = lax.broadcasted_iota(jnp.int32, (pools, 1, page_ids.shape[1]), 0)
    wanted = jnp.where(page_owner[None] == owner, page_ids[None], -1)
    tables = lax.all_to_all(wanted, "pool", split_axis=0, concat_axis=0, tiled=True)
    picked = pick_pages(tables, kv_store, rows)
    picked, span_kv = lax.optimization_barrier((picked, span_kv))
    fetched = lax.all_to_all(picked, "pool", split_axis=0, concat_axis=0, tiled=True)
    span = {0: span_kv}
    bit = blks // 2
    while bit:
        span.update({mask ^ bit: swap(rows_of, blks, bit) for mask, rows_of in list(span.items())})
        bit //= 2
    length = page_ids.shape[1] * page
    state = attend_span(prefix_len, queries, span, length, parts, rows)
    fetched, *state = lax.optimization_barrier((fetched, *state))
    mean, level, query, bias = state
    state = (mean, level)
    first, second = order_pages(page_owner, fetched)

    def across(piece):
        held = {0: [piece]}
        bit = blks // 2
        while bit > 1:
            held.update(
                {mask ^ bit: [swap(part[0], blks, bit)] for mask, part in list(held.items())}
            )
            bit //= 2
        return {mask: part for mask, part in held.items() if mask % KVH == 2}

    def relayed(held):
        return {mask ^ 1: [swap(part, blks, 1) for part in parts] for mask, parts in held.items()}

    near = {0: [first, second]}
    for mask in range(KVH, blks, KVH):
        near[mask] = [swap(first, blks, mask), swap(second, blks, mask)]
    near.update(relayed(near))
    attend = functools.partial(attend_prefix, query=query, bias=bias)
    far = across(first)
    own = attend(near, state=state, mask=0, mode="mean")
    second, own = lax.optimization_barrier((second, own))
    rest = across(second)
    other = attend(near, state=state, mask=1, mode="mean")
    own, other, far = lax.optimization_barrier((own, other, far))
    far.update(relayed(far))
    states = [attend(far, state=state, mask=mask, mode="state") for mask in (2, 3)]
    states, rest = lax.optimization_barrier((states, rest))
    rest.update(relayed(rest))
    offset = first.shape[0] * first.shape[1]
    done = attend(rest, state=states[0], mask=2, mode="mean", offset=offset)
    return attend(
        rest,
        state=states[1],
        mask=3,
        mode="write",
        offset=offset,
        waiting=((0, own), (1, other), (2, done)),
    )


def solution(mesh):
    in_specs = (
        P(("pool", "blk"), None),
        P(("pool", "blk"), None),
        P("pool", None, None),
        P("pool", None),
        P("pool", None),
        P("pool"),
    )
    out_specs = P(("pool", "blk"), None)
    return jax.shard_map(
        per_device, mesh=mesh, in_specs=in_specs, out_specs=out_specs, check_vma=False
    )
```

```python
import functools
import math

import jax
import jax.numpy as jnp
from jax import lax
from jax.experimental import pallas as pl
from jax.experimental.pallas import tpu as pltpu
from jax.sharding import PartitionSpec as P

KVH = 4
DH = 128
GROUP = 8
CAP = 2
COEF = math.log2(math.e) / math.sqrt(DH)
LOW = -1e30
ROWS = 256
LOADS = 8


SMEM = pl.BlockSpec(memory_space=pltpu.SMEM)
VMEM = pl.BlockSpec(memory_space=pltpu.VMEM)
ANY = pl.BlockSpec(memory_space=pl.ANY)


def columns_from(first, count):
    return pl.ds(pl.multiple_of(first * DH, DH), count * DH)


def pick_kernel(tables_ref, store_ref, out_ref, table, own, load_sems, sems):
    pools, _, listed = tables_ref.shape
    stored, rows, _ = own.shape
    blk = lax.axis_index("blk")
    head = lax.rem(blk, KVH)
    at_rows = pl.ds(pl.multiple_of(lax.div(blk, KVH) * rows, rows), rows)
    loads = [pltpu.make_async_copy(tables_ref, table, load_sems.at[0])]
    for kind in range(2):
        for first in range(0, stored, stored // LOADS):
            pages = slice(first, first + stored // LOADS)
            loads.append(
                pltpu.make_async_copy(
                    store_ref.at[pages, at_rows, columns_from(kind * KVH + head, 1)],
                    own.at[pages, :, kind * DH : (kind + 1) * DH],
                    load_sems.at[len(loads)],
                )
            )
    for load in loads:
        load.start()
    for load in loads:
        load.wait()

    def page_copy(request, slot, page):
        return pltpu.make_async_copy(
            own.at[page], out_ref.at[request, slot], sems.at[request, slot]
        )

    def serve(request, carry):
        def visit(entry, state):
            rank, pages = state
            page = table[request, 0, entry]
            hit = page >= 0
            pages = [jnp.where(hit & (rank == slot), page, pages[slot]) for slot in range(CAP)]
            return rank + hit.astype(jnp.int32), pages

        state = (jnp.int32(0), [jnp.int32(0)] * CAP)
        _, pages = lax.fori_loop(0, listed, visit, state, unroll=listed <= 8)
        for slot in range(CAP):
            page_copy(request, slot, pages[slot]).start()
        return carry

    lax.fori_loop(0, pools, serve, 0)

    def finish(request, carry):
        for slot in range(CAP):
            page_copy(request, slot, 0).wait()
        return carry

    lax.fori_loop(0, pools, finish, 0)


def pick_pages(tables, kv_store, rows):
    pools = tables.shape[0]
    return pl.pallas_call(
        pick_kernel,
        in_specs=[ANY, ANY],
        out_specs=ANY,
        out_shape=pltpu.HBM((pools, CAP, rows, 2 * DH), kv_store.dtype),
        scratch_shapes=[
            pltpu.SMEM(tables.shape, jnp.int32),
            pltpu.VMEM((kv_store.shape[0], rows, 2 * DH), kv_store.dtype),
            pltpu.SemaphoreType.DMA((1 + 2 * LOADS,)),
            pltpu.SemaphoreType.DMA((pools, CAP)),
        ],
        name="pick_pages",
    )(in_vmem(tables), in_hbm(kv_store))


def in_hbm(array):
    return pltpu.with_memory_space_constraint(array, pltpu.HBM)


def in_vmem(array):
    return pltpu.with_memory_space_constraint(array, pltpu.VMEM)


def order_kernel(owners_ref, fetched_ref, first_ref, second_ref):
    cut = first_ref.shape[0]
    for entry in range(cut + second_ref.shape[0]):
        owner = owners_ref[0, entry]
        rank = jnp.int32(0)
        for earlier in range(entry):
            rank += (owners_ref[0, earlier] == owner).astype(jnp.int32)
        page = fetched_ref[owner, jnp.minimum(rank, CAP - 1)]
        if entry < cut:
            first_ref[entry] = page
        else:
            second_ref[entry - cut] = page


def order_pages(owners, fetched):
    listed = owners.shape[1]
    cut = listed * 3 // 4
    shape = (fetched.shape[2], 2 * DH)
    return pl.pallas_call(
        order_kernel,
        in_specs=[SMEM, VMEM],
        out_specs=[VMEM] * 2,
        out_shape=[
            pltpu.VMEM((cut, *shape), fetched.dtype),
            pltpu.VMEM((listed - cut, *shape), fetched.dtype),
        ],
        name="order_pages",
    )(owners, in_vmem(fetched))


def scores_of(query_ref, first, count, keys):
    heads = [query_ref[:, (first + j) * DH : (first + j + 1) * DH] for j in range(count)]
    stacked = heads[0] if count == 1 else jnp.concatenate(heads, axis=0)
    return lax.dot_general(
        stacked, keys, (((1,), (1,)), ((), ())), preferred_element_type=jnp.float32
    )


def with_ones(values):
    return jnp.concatenate([values, jnp.ones((values.shape[0], DH), values.dtype)], axis=1)


def span_kernel(masks, parts, rows, limit_ref, query_ref, *refs):
    blocks = len(masks)
    keys_refs, values_refs = refs[:blocks], refs[blocks : 2 * blocks]
    mean_ref, level_ref, copy_ref, bias_ref = refs[2 * blocks :]
    q_rows = query_ref.shape[0]
    count = ROWS // q_rows
    copy_ref[0] = query_ref[...]
    own = lax.axis_index("blk")
    shape = (bias_ref.shape[0], bias_ref.shape[1] // parts)
    index = lax.broadcasted_iota(jnp.int32, shape, 1)
    at_page = lax.div(index, rows) * (parts * rows) + lax.rem(index, rows)
    for step in range(parts):
        position = at_page + lax.rem(lax.div(own, KVH) + step, parts) * rows
        bias_ref[:, step * shape[1] : (step + 1) * shape[1]] = jnp.where(
            position < limit_ref[0], 0.0, LOW
        )
    keys = jnp.concatenate([ref[...] for ref in keys_refs], axis=0)
    values = with_ones(jnp.concatenate([ref[...] for ref in values_refs], axis=0))
    ahead = lax.broadcasted_iota(jnp.int32, (q_rows, q_rows), 0) - lax.broadcasted_iota(
        jnp.int32, (q_rows, q_rows), 1
    )
    bias = [
        jnp.where(ahead >= (jnp.bitwise_xor(own, mask) - own) * q_rows, 0.0, LOW) for mask in masks
    ]
    bias = jnp.concatenate(bias, axis=1)
    bias = jnp.concatenate([bias] * count, axis=0)
    lanes = lax.broadcasted_iota(jnp.int32, (q_rows, DH), 1)
    levels = jnp.zeros((q_rows, DH), jnp.float32)
    for first in range(0, GROUP, count):
        scores = scores_of(query_ref, first, count, keys) + bias
        top = jnp.max(scores, axis=1, keepdims=True)
        weights = jnp.exp2((scores - top) * COEF)
        summed = jnp.dot(
            weights.astype(jnp.bfloat16), values, preferred_element_type=jnp.float32
        )
        total = summed[:, DH:]
        level = top * COEF + jnp.log2(total)
        mean = summed[:, :DH] / total
        for j in range(count):
            at = slice(j * q_rows, (j + 1) * q_rows)
            columns = slice((first + j) * DH, (first + j + 1) * DH)
            mean_ref[0, :, columns] = mean[at].astype(jnp.bfloat16)
            levels = jnp.where(lanes == first + j, level[at], levels)
    level_ref[0] = levels


def attend_span(limit, queries, span, length, parts, rows):
    q_rows = queries.shape[0]
    masks = sorted(span)
    blocks = [span[mask] for mask in masks]
    wide = GROUP * DH

    def head(m):
        return lax.rem(lax.axis_index("blk"), KVH) ^ m

    keys_spec = pl.BlockSpec((q_rows, DH), lambda m: (0, head(m)))
    values_spec = pl.BlockSpec((q_rows, DH), lambda m: (0, KVH + head(m)))
    return pl.pallas_call(
        functools.partial(span_kernel, masks, parts, rows),
        grid=(KVH,),
        in_specs=[SMEM, pl.BlockSpec((q_rows, wide), lambda m: (0, head(m)))]
        + [keys_spec] * len(masks)
        + [values_spec] * len(masks),
        out_specs=[
            pl.BlockSpec((1, q_rows, wide), lambda m: (m, 0, 0)),
            pl.BlockSpec((1, q_rows, DH), lambda m: (m, 0, 0)),
            pl.BlockSpec((1, q_rows, wide), lambda m: (m, 0, 0)),
            pl.BlockSpec((8, length), lambda m: (0, 0)),
        ],
        out_shape=[
            pltpu.VMEM((KVH, q_rows, wide), jnp.bfloat16),
            pltpu.VMEM((KVH, q_rows, DH), jnp.float32),
            pltpu.VMEM((KVH, q_rows, wide), jnp.bfloat16),
            pltpu.VMEM((8, length), jnp.float32),
        ],
        cost_estimate=pl.CostEstimate(
            flops=4 * q_rows * KVH * wide * q_rows * len(masks),
            bytes_accessed=8 * 2**20,
            transcendentals=0,
        ),
        compiler_params=pltpu.CompilerParams(vmem_limit_bytes=48 * 2**20),
        name="attend_span",
    )(limit, in_hbm(queries), *blocks, *blocks)


def prefix_kernel(mask, at, parts, count_in, offset, mode, waiting, *refs):
    pieces = refs[:count_in]
    query_ref, mean_ref, level_ref, bias_ref, *refs = refs[count_in:]
    q_rows = query_ref.shape[1]
    count = ROWS // q_rows
    both = [piece[...].reshape(-1, 2 * DH) for piece in pieces]
    length = sum(piece.shape[0] for piece in both) // parts
    both = both[0] if count_in == 1 else jnp.concatenate(both, axis=0)
    keys = both[:, :DH]
    values = with_ones(both[:, DH:])
    own_head = lax.rem(lax.axis_index("blk"), KVH)
    copies = []
    if mode == "write":
        *_, out_ref, done_ref, sems = refs
    else:
        new_mean_ref = refs[0]
    whole = bias_ref.shape[1] // parts
    safe = min(max(whole * 5 // 8 // DH * DH - offset, 0), length)
    lanes = lax.broadcasted_iota(jnp.int32, (q_rows, DH), 1)
    levels = jnp.zeros((q_rows, DH), jnp.float32)
    for first in range(0, GROUP, count):
        raw = scores_of(query_ref.at[mask], first, count, keys)
        scores = []
        for step in range(parts):
            scores.append(raw[:, step * length : step * length + safe])
            if safe < length:
                bias = bias_ref[:1, step * whole + offset + safe : step * whole + offset + length]
                scores.append(raw[:, step * length + safe : (step + 1) * length] + bias)
        scores = jnp.concatenate([part for part in scores if part.shape[1]], axis=1)
        heads = [slice((first + j) * DH, (first + j + 1) * DH) for j in range(count)]
        level = jnp.concatenate(
            [
                jnp.broadcast_to(level_ref[at, :, first + j : first + j + 1], (q_rows, DH))
                for j in range(count)
            ],
            axis=0,
        )
        mean = jnp.concatenate([mean_ref[at, :, columns] for columns in heads], axis=0)
        top = jnp.maximum(jnp.max(scores, axis=1, keepdims=True) * COEF, level)
        tops = jnp.concatenate([top] * (parts * length // DH), axis=1)
        weights = jnp.exp2(scores * COEF - tops)
        old = jnp.exp2(level - top)
        summed = jnp.dot(
            weights.astype(jnp.bfloat16), values, preferred_element_type=jnp.float32
        )
        total = summed[:, DH:] + old
        result = (summed[:, :DH] + mean.astype(jnp.float32) * old) / total
        for j, columns in enumerate(heads):
            part = slice(j * q_rows, (j + 1) * q_rows)
            rounded = result[part].astype(jnp.bfloat16)
            if mode == "write":
                done_ref[0, :, columns] = rounded
            else:
                new_mean_ref[0, :, columns] = rounded
            if mode == "state":
                levels = jnp.where(lanes == first + j, (top + jnp.log2(total))[part], levels)
        if mode == "write":
            head = jnp.bitwise_xor(own_head, mask)
            copies.append(
                pltpu.make_async_copy(
                    done_ref.at[0, :, first * DH : (first + count) * DH],
                    out_ref.at[:, columns_from(head * GROUP + first, count)],
                    sems.at[first // count],
                )
            )
            copies[-1].start()
        if mode == "write" and first == 0:
            for place, other in enumerate(waiting):
                done_ref[1 + place] = refs[place][0]
                head = jnp.bitwise_xor(own_head, other)
                copies.append(
                    pltpu.make_async_copy(
                        done_ref.at[1 + place],
                        out_ref.at[:, columns_from(head * GROUP, GROUP)],
                        sems.at[GROUP * q_rows // ROWS + place],
                    )
                )
                copies[-1].start()
    for copy in copies:
        copy.wait()
    if mode == "state":
        refs[1][0] = levels


def attend_prefix(held, query, state, bias, mask, mode, offset=0, waiting=()):
    _, q_rows, wide = query.shape
    groups = [held[at] for at in sorted(held) if at % KVH == mask]
    parts = len(groups)
    pieces = [piece for group in groups for piece in group]
    length = sum(piece.shape[0] * piece.shape[1] for piece in pieces)
    at = mask if state[0].shape[0] == KVH else 0
    mean_shape = pltpu.VMEM((1, q_rows, wide), jnp.bfloat16)
    scratch = []
    if mode == "write":
        out_specs = ANY
        out_shape = jax.ShapeDtypeStruct((q_rows, KVH * wide), jnp.bfloat16)
        scratch = [
            pltpu.VMEM((1 + len(waiting), q_rows, wide), jnp.bfloat16),
            pltpu.SemaphoreType.DMA((GROUP * q_rows // ROWS + len(waiting),)),
        ]
    elif mode == "mean":
        out_specs, out_shape = VMEM, mean_shape
    else:
        out_specs = [VMEM, VMEM]
        out_shape = [mean_shape, pltpu.VMEM((1, q_rows, DH), jnp.float32)]
    operands = [query, *state, bias, *[result for _, result in waiting]]
    operands = [*pieces, *[in_vmem(array) for array in operands]]
    masks = [other for other, _ in waiting]
    return pl.pallas_call(
        functools.partial(prefix_kernel, mask, at, parts, len(pieces), offset, mode, masks),
        in_specs=[VMEM] * len(operands),
        out_specs=out_specs,
        out_shape=out_shape,
        scratch_shapes=scratch,
        cost_estimate=pl.CostEstimate(
            flops=64 * q_rows * wide * length, bytes_accessed=2**20, transcendentals=0
        ),
        compiler_params=pltpu.CompilerParams(vmem_limit_bytes=48 * 2**20),
        name="attend_prefix",
    )(*operands)


def swap(array, blks, mask):
    return lax.ppermute(array, "blk", [(i, i ^ mask) for i in range(blks)])


def per_device(queries, span_kv, kv_store, page_ids, page_owner, prefix_len):
    pools = lax.axis_size("pool")
    blks = lax.axis_size("blk")
    stored, page, _ = kv_store.shape
    parts = blks // KVH
    rows = page // parts

    owner = lax.broadcasted_iota(jnp.int32, (pools, 1, page_ids.shape[1]), 0)
    wanted = jnp.where(page_owner[None] == owner, page_ids[None], -1)
    tables = lax.all_to_all(wanted, "pool", split_axis=0, concat_axis=0, tiled=True)
    picked = pick_pages(tables, kv_store, rows)
    picked, span_kv = lax.optimization_barrier((picked, span_kv))
    fetched = lax.all_to_all(picked, "pool", split_axis=0, concat_axis=0, tiled=True)
    span = {0: span_kv}
    bit = blks // 2
    while bit:
        span.update({mask ^ bit: swap(rows_of, blks, bit) for mask, rows_of in list(span.items())})
        bit //= 2
    length = page_ids.shape[1] * page
    state = attend_span(prefix_len, queries, span, length, parts, rows)
    fetched, *state = lax.optimization_barrier((fetched, *state))
    mean, level, query, bias = state
    state = (mean, level)
    first, second = order_pages(page_owner, fetched)

    def across(piece):
        held = {0: [piece]}
        bit = blks // 2
        while bit > 1:
            held.update(
                {mask ^ bit: [swap(part[0], blks, bit)] for mask, part in list(held.items())}
            )
            bit //= 2
        return {mask: part for mask, part in held.items() if mask % KVH == 2}

    def relayed(held):
        return {mask ^ 1: [swap(part, blks, 1) for part in parts] for mask, parts in held.items()}

    near = {0: [first, second]}
    for mask in range(KVH, blks, KVH):
        near[mask] = [swap(first, blks, mask), swap(second, blks, mask)]
    near.update(relayed(near))
    attend = functools.partial(attend_prefix, query=query, bias=bias)
    far = across(first)
    own = attend(near, state=state, mask=0, mode="mean")
    second, own = lax.optimization_barrier((second, own))
    rest = across(second)
    other = attend(near, state=state, mask=1, mode="mean")
    own, other, far = lax.optimization_barrier((own, other, far))
    far.update(relayed(far))
    states = [attend(far, state=state, mask=mask, mode="state") for mask in (2, 3)]
    states, rest = lax.optimization_barrier((states, rest))
    rest.update(relayed(rest))
    offset = first.shape[0] * first.shape[1]
    done = attend(rest, state=states[0], mask=2, mode="mean", offset=offset)
    return attend(
        rest,
        state=states[1],
        mask=3,
        mode="write",
        offset=offset,
        waiting=((0, own), (1, other), (2, done)),
    )


def solution(mesh):
    in_specs = (
        P(("pool", "blk"), None),
        P(("pool", "blk"), None),
        P("pool", None, None),
        P("pool", None),
        P("pool", None),
        P("pool"),
    )
    out_specs = P(("pool", "blk"), None)
    return jax.shard_map(
        per_device, mesh=mesh, in_specs=in_specs, out_specs=out_specs, check_vma=False
    )
```

```python
import functools
import math

import jax
import jax.numpy as jnp
from jax import lax
from jax.experimental import pallas as pl
from jax.experimental.pallas import tpu as pltpu
from jax.sharding import PartitionSpec as P

KVH = 4
DH = 128
GROUP = 8
CAP = 2
COEF = math.log2(math.e) / math.sqrt(DH)
LOW = -1e30
ROWS = 256
LOADS = 4


SMEM = pl.BlockSpec(memory_space=pltpu.SMEM)
VMEM = pl.BlockSpec(memory_space=pltpu.VMEM)
ANY = pl.BlockSpec(memory_space=pl.ANY)


def columns_from(first, count):
    return pl.ds(pl.multiple_of(first * DH, DH), count * DH)


def pick_kernel(tables_ref, store_ref, out_ref, table, own, load_sems, sems):
    pools, _, listed = tables_ref.shape
    stored, rows, _ = own.shape
    blk = lax.axis_index("blk")
    head = lax.rem(blk, KVH)
    at_rows = pl.ds(pl.multiple_of(lax.div(blk, KVH) * rows, rows), rows)
    loads = [pltpu.make_async_copy(tables_ref, table, load_sems.at[0])]
    for kind in range(2):
        for first in range(0, stored, stored // LOADS):
            pages = slice(first, first + stored // LOADS)
            loads.append(
                pltpu.make_async_copy(
                    store_ref.at[pages, at_rows, columns_from(kind * KVH + head, 1)],
                    own.at[pages, :, kind * DH : (kind + 1) * DH],
                    load_sems.at[len(loads)],
                )
            )
    for load in loads:
        load.start()
    for load in loads:
        load.wait()

    def page_copy(request, slot, page):
        return pltpu.make_async_copy(
            own.at[page], out_ref.at[request, slot], sems.at[request, slot]
        )

    def serve(request, carry):
        def visit(entry, state):
            rank, pages = state
            page = table[request, 0, entry]
            hit = page >= 0
            pages = [jnp.where(hit & (rank == slot), page, pages[slot]) for slot in range(CAP)]
            return rank + hit.astype(jnp.int32), pages

        state = (jnp.int32(0), [jnp.int32(0)] * CAP)
        _, pages = lax.fori_loop(0, listed, visit, state, unroll=listed <= 8)
        for slot in range(CAP):
            page_copy(request, slot, pages[slot]).start()
        return carry

    lax.fori_loop(0, pools, serve, 0)

    def finish(request, carry):
        for slot in range(CAP):
            page_copy(request, slot, 0).wait()
        return carry

    lax.fori_loop(0, pools, finish, 0)


def pick_pages(tables, kv_store, rows):
    pools = tables.shape[0]
    return pl.pallas_call(
        pick_kernel,
        in_specs=[ANY, ANY],
        out_specs=ANY,
        out_shape=pltpu.HBM((pools, CAP, rows, 2 * DH), kv_store.dtype),
        scratch_shapes=[
            pltpu.SMEM(tables.shape, jnp.int32),
            pltpu.VMEM((kv_store.shape[0], rows, 2 * DH), kv_store.dtype),
            pltpu.SemaphoreType.DMA((1 + 2 * LOADS,)),
            pltpu.SemaphoreType.DMA((pools, CAP)),
        ],
        name="pick_pages",
    )(in_vmem(tables), in_hbm(kv_store))


def in_hbm(array):
    return pltpu.with_memory_space_constraint(array, pltpu.HBM)


def in_vmem(array):
    return pltpu.with_memory_space_constraint(array, pltpu.VMEM)


def order_kernel(owners_ref, fetched_ref, first_ref, second_ref):
    half = first_ref.shape[0]
    for entry in range(2 * half):
        owner = owners_ref[0, entry]
        rank = jnp.int32(0)
        for earlier in range(entry):
            rank += (owners_ref[0, earlier] == owner).astype(jnp.int32)
        half_ref = first_ref if entry < half else second_ref
        half_ref[entry % half] = fetched_ref[owner, jnp.minimum(rank, CAP - 1)]


def order_pages(owners, fetched):
    shape = (owners.shape[1] // 2, fetched.shape[2], 2 * DH)
    return pl.pallas_call(
        order_kernel,
        in_specs=[SMEM, VMEM],
        out_specs=[VMEM] * 2,
        out_shape=[pltpu.VMEM(shape, fetched.dtype)] * 2,
        name="order_pages",
    )(owners, in_vmem(fetched))


def scores_of(query_ref, first, count, keys):
    heads = [query_ref[:, (first + j) * DH : (first + j + 1) * DH] for j in range(count)]
    stacked = heads[0] if count == 1 else jnp.concatenate(heads, axis=0)
    return lax.dot_general(
        stacked, keys, (((1,), (1,)), ((), ())), preferred_element_type=jnp.float32
    )


def with_ones(values):
    return jnp.concatenate([values, jnp.ones((values.shape[0], DH), values.dtype)], axis=1)


def span_kernel(masks, parts, rows, opening, *refs):
    blocks = len(masks)
    limit_ref, query_ref, *refs = refs
    keys_refs, values_refs, refs = refs[:blocks], refs[blocks : 2 * blocks], refs[2 * blocks :]
    if opening:
        mean_ref, level_ref, copy_ref, bias_ref = refs
    else:
        old_mean_ref, old_level_ref, mean_ref, level_ref = refs
    q_rows = query_ref.shape[0]
    count = ROWS // q_rows
    own = lax.axis_index("blk")
    if opening:
        copy_ref[0] = query_ref[...]
        shape = (bias_ref.shape[0], bias_ref.shape[1] // parts)
        index = lax.broadcasted_iota(jnp.int32, shape, 1)
        at_page = lax.div(index, rows) * (parts * rows) + lax.rem(index, rows)
        for step in range(parts):
            position = at_page + lax.rem(lax.div(own, KVH) + step, parts) * rows
            bias_ref[:, step * shape[1] : (step + 1) * shape[1]] = jnp.where(
                position < limit_ref[0], 0.0, LOW
            )
    keys = jnp.concatenate([ref[...] for ref in keys_refs], axis=0)
    values = with_ones(jnp.concatenate([ref[...] for ref in values_refs], axis=0))
    ahead = lax.broadcasted_iota(jnp.int32, (q_rows, q_rows), 0) - lax.broadcasted_iota(
        jnp.int32, (q_rows, q_rows), 1
    )
    bias = [
        jnp.where(ahead >= (jnp.bitwise_xor(own, mask) - own) * q_rows, 0.0, LOW) for mask in masks
    ]
    bias = jnp.concatenate(bias, axis=1)
    bias = jnp.concatenate([bias] * count, axis=0)
    lanes = lax.broadcasted_iota(jnp.int32, (q_rows, DH), 1)
    levels = jnp.zeros((q_rows, DH), jnp.float32)
    for first in range(0, GROUP, count):
        heads = [slice((first + j) * DH, (first + j + 1) * DH) for j in range(count)]
        scores = scores_of(query_ref, first, count, keys) + bias
        top = jnp.max(scores, axis=1, keepdims=True) * COEF
        if opening:
            top = jnp.broadcast_to(top, (count * q_rows, DH))
        else:
            old_level = jnp.concatenate(
                [
                    jnp.broadcast_to(old_level_ref[0, :, first + j : first + j + 1], (q_rows, DH))
                    for j in range(count)
                ],
                axis=0,
            )
            top = jnp.maximum(top, old_level)
        tops = jnp.concatenate([top] * (blocks * q_rows // DH), axis=1)
        weights = jnp.exp2(scores * COEF - tops)
        summed = jnp.dot(
            weights.astype(jnp.bfloat16), values, preferred_element_type=jnp.float32
        )
        numer, total = summed[:, :DH], summed[:, DH:]
        if not opening:
            old = jnp.exp2(old_level - top)
            old_mean = jnp.concatenate([old_mean_ref[0, :, columns] for columns in heads], axis=0)
            numer = numer + old_mean.astype(jnp.float32) * old
            total = total + old
        level = top + jnp.log2(total)
        mean = numer / total
        for j, columns in enumerate(heads):
            at = slice(j * q_rows, (j + 1) * q_rows)
            mean_ref[0, :, columns] = mean[at].astype(jnp.bfloat16)
            levels = jnp.where(lanes == first + j, level[at], levels)
    level_ref[0] = levels


def attend_span(limit, queries, span, length, parts, rows, state=None):
    q_rows = queries.shape[0]
    masks = sorted(span)
    blocks = [span[mask] for mask in masks]
    wide = GROUP * DH
    opening = state is None

    def head(m):
        return lax.rem(lax.axis_index("blk"), KVH) ^ m

    keys_spec = pl.BlockSpec((q_rows, DH), lambda m: (0, head(m)))
    values_spec = pl.BlockSpec((q_rows, DH), lambda m: (0, KVH + head(m)))
    mean_spec = pl.BlockSpec((1, q_rows, wide), lambda m: (m, 0, 0))
    level_spec = pl.BlockSpec((1, q_rows, DH), lambda m: (m, 0, 0))
    mean_shape = pltpu.VMEM((KVH, q_rows, wide), jnp.bfloat16)
    out_specs = [mean_spec, level_spec]
    out_shape = [mean_shape, pltpu.VMEM((KVH, q_rows, DH), jnp.float32)]
    if opening:
        out_specs += [mean_spec, pl.BlockSpec((8, length), lambda m: (0, 0))]
        out_shape += [mean_shape, pltpu.VMEM((8, length), jnp.float32)]
    before = [] if opening else [in_vmem(array) for array in state]
    return pl.pallas_call(
        functools.partial(span_kernel, masks, parts, rows, opening),
        grid=(KVH,),
        in_specs=[SMEM, pl.BlockSpec((q_rows, wide), lambda m: (0, head(m)))]
        + [keys_spec] * len(masks)
        + [values_spec] * len(masks)
        + [mean_spec, level_spec][: len(before)],
        out_specs=out_specs,
        out_shape=out_shape,
        cost_estimate=pl.CostEstimate(
            flops=32 * q_rows * KVH * wide * q_rows * len(masks),
            bytes_accessed=2**20,
            transcendentals=0,
        ),
        compiler_params=pltpu.CompilerParams(vmem_limit_bytes=48 * 2**20),
        name="attend_span",
    )(limit, in_hbm(queries), *blocks, *blocks, *before)


def prefix_kernel(mask, at, parts, count_in, offset, mode, waiting, *refs):
    pieces = refs[:count_in]
    query_ref, mean_ref, level_ref, bias_ref, *refs = refs[count_in:]
    q_rows = query_ref.shape[1]
    count = ROWS // q_rows
    pages, rows, _ = pieces[0].shape
    length = count_in // parts * pages * rows
    both = [piece[...].reshape(pages * rows, 2 * DH) for piece in pieces]
    both = both[0] if count_in == 1 else jnp.concatenate(both, axis=0)
    keys = both[:, :DH]
    values = with_ones(both[:, DH:])
    own_head = lax.rem(lax.axis_index("blk"), KVH)
    copies = []
    if mode == "write":
        *_, out_ref, done_ref, sems = refs
    else:
        new_mean_ref = refs[0]
    whole = bias_ref.shape[1] // parts
    safe = min(max(whole * 5 // 8 // DH * DH - offset, 0), length)
    lanes = lax.broadcasted_iota(jnp.int32, (q_rows, DH), 1)
    levels = jnp.zeros((q_rows, DH), jnp.float32)
    for first in range(0, GROUP, count):
        raw = scores_of(query_ref.at[mask], first, count, keys)
        scores = []
        for step in range(parts):
            scores.append(raw[:, step * length : step * length + safe])
            if safe < length:
                bias = bias_ref[:1, step * whole + offset + safe : step * whole + offset + length]
                scores.append(raw[:, step * length + safe : (step + 1) * length] + bias)
        scores = jnp.concatenate([part for part in scores if part.shape[1]], axis=1)
        heads = [slice((first + j) * DH, (first + j + 1) * DH) for j in range(count)]
        level = jnp.concatenate(
            [
                jnp.broadcast_to(level_ref[at, :, first + j : first + j + 1], (q_rows, DH))
                for j in range(count)
            ],
            axis=0,
        )
        mean = jnp.concatenate([mean_ref[at, :, columns] for columns in heads], axis=0)
        top = jnp.maximum(jnp.max(scores, axis=1, keepdims=True) * COEF, level)
        tops = jnp.concatenate([top] * (parts * length // DH), axis=1)
        weights = jnp.exp2(scores * COEF - tops)
        old = jnp.exp2(level - top)
        summed = jnp.dot(
            weights.astype(jnp.bfloat16), values, preferred_element_type=jnp.float32
        )
        total = summed[:, DH:] + old
        result = (summed[:, :DH] + mean.astype(jnp.float32) * old) / total
        for j, columns in enumerate(heads):
            part = slice(j * q_rows, (j + 1) * q_rows)
            rounded = result[part].astype(jnp.bfloat16)
            if mode == "write":
                done_ref[0, :, columns] = rounded
            else:
                new_mean_ref[0, :, columns] = rounded
            if mode == "state":
                levels = jnp.where(lanes == first + j, (top + jnp.log2(total))[part], levels)
        if mode == "write":
            head = jnp.bitwise_xor(own_head, mask)
            copies.append(
                pltpu.make_async_copy(
                    done_ref.at[0, :, first * DH : (first + count) * DH],
                    out_ref.at[:, columns_from(head * GROUP + first, count)],
                    sems.at[first // count],
                )
            )
            copies[-1].start()
        if mode == "write" and first == 0:
            for place, other in enumerate(waiting):
                done_ref[1 + place] = refs[place][0]
                head = jnp.bitwise_xor(own_head, other)
                copies.append(
                    pltpu.make_async_copy(
                        done_ref.at[1 + place],
                        out_ref.at[:, columns_from(head * GROUP, GROUP)],
                        sems.at[GROUP * q_rows // ROWS + place],
                    )
                )
                copies[-1].start()
    for copy in copies:
        copy.wait()
    if mode == "state":
        refs[1][0] = levels


def attend_prefix(held, query, state, bias, mask, mode, offset=0, waiting=()):
    _, q_rows, wide = query.shape
    groups = [held[at] for at in sorted(held) if at % KVH == mask]
    parts = len(groups)
    pieces = [piece for group in groups for piece in group]
    length = len(pieces) * pieces[0].shape[0] * pieces[0].shape[1]
    at = mask if state[0].shape[0] == KVH else 0
    mean_shape = pltpu.VMEM((1, q_rows, wide), jnp.bfloat16)
    scratch = []
    if mode == "write":
        out_specs = ANY
        out_shape = jax.ShapeDtypeStruct((q_rows, KVH * wide), jnp.bfloat16)
        scratch = [
            pltpu.VMEM((1 + len(waiting), q_rows, wide), jnp.bfloat16),
            pltpu.SemaphoreType.DMA((GROUP * q_rows // ROWS + len(waiting),)),
        ]
    elif mode == "mean":
        out_specs, out_shape = VMEM, mean_shape
    else:
        out_specs = [VMEM, VMEM]
        out_shape = [mean_shape, pltpu.VMEM((1, q_rows, DH), jnp.float32)]
    operands = [query, *state, bias, *[result for _, result in waiting]]
    operands = [*pieces, *[in_vmem(array) for array in operands]]
    masks = [other for other, _ in waiting]
    return pl.pallas_call(
        functools.partial(prefix_kernel, mask, at, parts, len(pieces), offset, mode, masks),
        in_specs=[VMEM] * len(operands),
        out_specs=out_specs,
        out_shape=out_shape,
        scratch_shapes=scratch,
        cost_estimate=pl.CostEstimate(
            flops=64 * q_rows * wide * length, bytes_accessed=2**20, transcendentals=0
        ),
        compiler_params=pltpu.CompilerParams(vmem_limit_bytes=48 * 2**20),
        name="attend_prefix",
    )(*operands)


def swap(array, blks, mask):
    return lax.ppermute(array, "blk", [(i, i ^ mask) for i in range(blks)])


def per_device(queries, span_kv, kv_store, page_ids, page_owner, prefix_len):
    pools = lax.axis_size("pool")
    blks = lax.axis_size("blk")
    stored, page, _ = kv_store.shape
    parts = blks // KVH
    rows = page // parts

    owner = lax.broadcasted_iota(jnp.int32, (pools, 1, page_ids.shape[1]), 0)
    wanted = jnp.where(page_owner[None] == owner, page_ids[None], -1)
    tables = lax.all_to_all(wanted, "pool", split_axis=0, concat_axis=0, tiled=True)
    picked = pick_pages(tables, kv_store, rows)
    picked, span_kv = lax.optimization_barrier((picked, span_kv))
    fetched = lax.all_to_all(picked, "pool", split_axis=0, concat_axis=0, tiled=True)
    far_span = {0: span_kv}
    bit = blks // 2
    while bit > 1:
        far_span.update(
            {mask ^ bit: swap(part, blks, bit) for mask, part in list(far_span.items())}
        )
        bit //= 2
    far_span.pop(0)
    near_span = {0: span_kv, 1: swap(span_kv, blks, 1)}
    length = page_ids.shape[1] * page
    attend = functools.partial(
        attend_span, prefix_len, queries, length=length, parts=parts, rows=rows
    )
    mean, level, query, bias = attend(near_span)
    far_span, mean, level = lax.optimization_barrier((far_span, mean, level))
    far_span.update({mask ^ 1: swap(part, blks, 1) for mask, part in list(far_span.items())})
    mean, level = attend(far_span, state=(mean, level))
    fetched, mean, level, query, bias = lax.optimization_barrier(
        (fetched, mean, level, query, bias)
    )
    state = (mean, level)
    first, second = order_pages(page_owner, fetched)

    def across(piece):
        held = {0: [piece]}
        bit = blks // 2
        while bit > 1:
            held.update(
                {mask ^ bit: [swap(part[0], blks, bit)] for mask, part in list(held.items())}
            )
            bit //= 2
        return {mask: part for mask, part in held.items() if mask % KVH == 2}

    def relayed(held):
        return {mask ^ 1: [swap(part, blks, 1) for part in parts] for mask, parts in held.items()}

    near = {0: [first, second]}
    for mask in range(KVH, blks, KVH):
        near[mask] = [swap(first, blks, mask), swap(second, blks, mask)]
    near.update(relayed(near))
    attend = functools.partial(attend_prefix, query=query, bias=bias)
    far = across(first)
    own = attend(near, state=state, mask=0, mode="mean")
    second, own = lax.optimization_barrier((second, own))
    rest = across(second)
    other = attend(near, state=state, mask=1, mode="mean")
    own, other, far = lax.optimization_barrier((own, other, far))
    far.update(relayed(far))
    states = [attend(far, state=state, mask=mask, mode="state") for mask in (2, 3)]
    states, rest = lax.optimization_barrier((states, rest))
    rest.update(relayed(rest))
    offset = first.shape[0] * first.shape[1]
    done = attend(rest, state=states[0], mask=2, mode="mean", offset=offset)
    return attend(
        rest,
        state=states[1],
        mask=3,
        mode="write",
        offset=offset,
        waiting=((0, own), (1, other), (2, done)),
    )


def solution(mesh):
    in_specs = (
        P(("pool", "blk"), None),
        P(("pool", "blk"), None),
        P("pool", None, None),
        P("pool", None),
        P("pool", None),
        P("pool"),
    )
    out_specs = P(("pool", "blk"), None)
    return jax.shard_map(
        per_device, mesh=mesh, in_specs=in_specs, out_specs=out_specs, check_vma=False
    )
```

```python
import functools
import math

import jax
import jax.numpy as jnp
from jax import lax
from jax.experimental import pallas as pl
from jax.experimental.pallas import tpu as pltpu
from jax.sharding import PartitionSpec as P

KVH = 4
DH = 128
GROUP = 8
CAP = 2
COEF = math.log2(math.e) / math.sqrt(DH)
LOW = -1e30
ROWS = 256
LOADS = 4


SMEM = pl.BlockSpec(memory_space=pltpu.SMEM)
VMEM = pl.BlockSpec(memory_space=pltpu.VMEM)
ANY = pl.BlockSpec(memory_space=pl.ANY)


def columns_from(first, count):
    return pl.ds(pl.multiple_of(first * DH, DH), count * DH)


def pick_kernel(tables_ref, store_ref, out_ref, table, chosen, own, load_sems, sems):
    pools, _, listed = tables_ref.shape
    stored, rows, _ = own.shape
    blk = lax.axis_index("blk")
    head = lax.rem(blk, KVH)
    at_rows = pl.ds(pl.multiple_of(lax.div(blk, KVH) * rows, rows), rows)
    loads = [pltpu.make_async_copy(tables_ref, table, load_sems.at[0])]
    for kind in range(2):
        for first in range(0, stored, stored // LOADS):
            pages = slice(first, first + stored // LOADS)
            loads.append(
                pltpu.make_async_copy(
                    store_ref.at[pages, at_rows, columns_from(kind * KVH + head, 1)],
                    own.at[pages, :, kind * DH : (kind + 1) * DH],
                    load_sems.at[len(loads)],
                )
            )
    for load in loads:
        load.start()
    loads[0].wait()

    def page_copy(request, slot, page):
        return pltpu.make_async_copy(
            own.at[page], out_ref.at[request, slot], sems.at[request, slot]
        )

    def serve(request, carry):
        def visit(entry, state):
            rank, pages = state
            page = table[request, 0, entry]
            hit = page >= 0
            pages = [jnp.where(hit & (rank == slot), page, pages[slot]) for slot in range(CAP)]
            return rank + hit.astype(jnp.int32), pages

        state = (jnp.int32(0), [jnp.int32(0)] * CAP)
        _, pages = lax.fori_loop(0, listed, visit, state, unroll=listed <= 8)
        for slot in range(CAP):
            chosen[request, slot] = pages[slot]
        return carry

    lax.fori_loop(0, pools, serve, 0)
    for load in loads[1:]:
        load.wait()

    def send(request, carry):
        for slot in range(CAP):
            page_copy(request, slot, chosen[request, slot]).start()
        return carry

    lax.fori_loop(0, pools, send, 0)

    def finish(request, carry):
        for slot in range(CAP):
            page_copy(request, slot, 0).wait()
        return carry

    lax.fori_loop(0, pools, finish, 0)


def pick_pages(tables, kv_store, rows):
    pools = tables.shape[0]
    return pl.pallas_call(
        pick_kernel,
        in_specs=[ANY, ANY],
        out_specs=ANY,
        out_shape=pltpu.HBM((pools, CAP, rows, 2 * DH), kv_store.dtype),
        scratch_shapes=[
            pltpu.SMEM(tables.shape, jnp.int32),
            pltpu.SMEM((pools, CAP), jnp.int32),
            pltpu.VMEM((kv_store.shape[0], rows, 2 * DH), kv_store.dtype),
            pltpu.SemaphoreType.DMA((1 + 2 * LOADS,)),
            pltpu.SemaphoreType.DMA((pools, CAP)),
        ],
        name="pick_pages",
    )(in_vmem(tables), in_hbm(kv_store))


def in_hbm(array):
    return pltpu.with_memory_space_constraint(array, pltpu.HBM)


def in_vmem(array):
    return pltpu.with_memory_space_constraint(array, pltpu.VMEM)


def order_kernel(owners_ref, fetched_ref, first_ref, second_ref):
    half = first_ref.shape[0]
    for entry in range(2 * half):
        owner = owners_ref[0, entry]
        rank = jnp.int32(0)
        for earlier in range(entry):
            rank += (owners_ref[0, earlier] == owner).astype(jnp.int32)
        half_ref = first_ref if entry < half else second_ref
        half_ref[entry % half] = fetched_ref[owner, jnp.minimum(rank, CAP - 1)]


def order_pages(owners, fetched):
    shape = (owners.shape[1] // 2, fetched.shape[2], 2 * DH)
    return pl.pallas_call(
        order_kernel,
        in_specs=[SMEM, VMEM],
        out_specs=[VMEM] * 2,
        out_shape=[pltpu.VMEM(shape, fetched.dtype)] * 2,
        name="order_pages",
    )(owners, in_vmem(fetched))


def scores_of(query_ref, first, count, keys):
    heads = [query_ref[:, (first + j) * DH : (first + j + 1) * DH] for j in range(count)]
    stacked = heads[0] if count == 1 else jnp.concatenate(heads, axis=0)
    return lax.dot_general(
        stacked, keys, (((1,), (1,)), ((), ())), preferred_element_type=jnp.float32
    )


def with_ones(values):
    return jnp.concatenate([values, jnp.ones((values.shape[0], DH), values.dtype)], axis=1)


def span_kernel(masks, parts, rows, limit_ref, query_ref, *refs):
    blocks = len(masks)
    keys_refs, values_refs = refs[:blocks], refs[blocks : 2 * blocks]
    mean_ref, level_ref, copy_ref, bias_ref = refs[2 * blocks :]
    q_rows = query_ref.shape[0]
    count = ROWS // q_rows
    copy_ref[0] = query_ref[...]
    own = lax.axis_index("blk")
    shape = (bias_ref.shape[0], bias_ref.shape[1] // parts)
    index = lax.broadcasted_iota(jnp.int32, shape, 1)
    at_page = lax.div(index, rows) * (parts * rows) + lax.rem(index, rows)
    for step in range(parts):
        position = at_page + lax.rem(lax.div(own, KVH) + step, parts) * rows
        bias_ref[:, step * shape[1] : (step + 1) * shape[1]] = jnp.where(
            position < limit_ref[0], 0.0, LOW
        )
    keys = jnp.concatenate([ref[...] for ref in keys_refs], axis=0)
    values = with_ones(jnp.concatenate([ref[...] for ref in values_refs], axis=0))
    ahead = lax.broadcasted_iota(jnp.int32, (q_rows, q_rows), 0) - lax.broadcasted_iota(
        jnp.int32, (q_rows, q_rows), 1
    )
    bias = [
        jnp.where(ahead >= (jnp.bitwise_xor(own, mask) - own) * q_rows, 0.0, LOW) for mask in masks
    ]
    bias = jnp.concatenate(bias, axis=1)
    bias = jnp.concatenate([bias] * count, axis=0)
    lanes = lax.broadcasted_iota(jnp.int32, (q_rows, DH), 1)
    levels = jnp.zeros((q_rows, DH), jnp.float32)
    for first in range(0, GROUP, count):
        scores = scores_of(query_ref, first, count, keys) + bias
        top = jnp.max(scores, axis=1, keepdims=True)
        weights = jnp.exp2((scores - top) * COEF)
        summed = jnp.dot(
            weights.astype(jnp.bfloat16), values, preferred_element_type=jnp.float32
        )
        total = summed[:, DH:]
        level = top * COEF + jnp.log2(total)
        mean = summed[:, :DH] / total
        for j in range(count):
            at = slice(j * q_rows, (j + 1) * q_rows)
            columns = slice((first + j) * DH, (first + j + 1) * DH)
            mean_ref[0, :, columns] = mean[at].astype(jnp.bfloat16)
            levels = jnp.where(lanes == first + j, level[at], levels)
    level_ref[0] = levels


def attend_span(limit, queries, span, length, parts, rows):
    q_rows = queries.shape[0]
    masks = sorted(span)
    blocks = [span[mask] for mask in masks]
    wide = GROUP * DH

    def head(m):
        return lax.rem(lax.axis_index("blk"), KVH) ^ m

    keys_spec = pl.BlockSpec((q_rows, DH), lambda m: (0, head(m)))
    values_spec = pl.BlockSpec((q_rows, DH), lambda m: (0, KVH + head(m)))
    return pl.pallas_call(
        functools.partial(span_kernel, masks, parts, rows),
        grid=(KVH,),
        in_specs=[SMEM, pl.BlockSpec((q_rows, wide), lambda m: (0, head(m)))]
        + [keys_spec] * len(masks)
        + [values_spec] * len(masks),
        out_specs=[
            pl.BlockSpec((1, q_rows, wide), lambda m: (m, 0, 0)),
            pl.BlockSpec((1, q_rows, DH), lambda m: (m, 0, 0)),
            pl.BlockSpec((1, q_rows, wide), lambda m: (m, 0, 0)),
            pl.BlockSpec((8, length), lambda m: (0, 0)),
        ],
        out_shape=[
            pltpu.VMEM((KVH, q_rows, wide), jnp.bfloat16),
            pltpu.VMEM((KVH, q_rows, DH), jnp.float32),
            pltpu.VMEM((KVH, q_rows, wide), jnp.bfloat16),
            pltpu.VMEM((8, length), jnp.float32),
        ],
        cost_estimate=pl.CostEstimate(
            flops=4 * q_rows * KVH * wide * q_rows * len(masks),
            bytes_accessed=8 * 2**20,
            transcendentals=0,
        ),
        compiler_params=pltpu.CompilerParams(vmem_limit_bytes=48 * 2**20),
        name="attend_span",
    )(limit, in_hbm(queries), *blocks, *blocks)


def prefix_kernel(mask, at, parts, count_in, offset, mode, waiting, *refs):
    pieces = refs[:count_in]
    query_ref, mean_ref, level_ref, bias_ref, *refs = refs[count_in:]
    q_rows = query_ref.shape[1]
    count = ROWS // q_rows
    pages, rows, _ = pieces[0].shape
    length = count_in // parts * pages * rows
    both = [piece[...].reshape(pages * rows, 2 * DH) for piece in pieces]
    both = both[0] if count_in == 1 else jnp.concatenate(both, axis=0)
    keys = both[:, :DH]
    values = with_ones(both[:, DH:])
    own_head = lax.rem(lax.axis_index("blk"), KVH)
    copies = []
    if mode == "write":
        *_, out_ref, done_ref, sems = refs
    else:
        new_mean_ref = refs[0]
    whole = bias_ref.shape[1] // parts
    safe = min(max(whole * 5 // 8 // DH * DH - offset, 0), length)
    lanes = lax.broadcasted_iota(jnp.int32, (q_rows, DH), 1)
    levels = jnp.zeros((q_rows, DH), jnp.float32)
    for first in range(0, GROUP, count):
        raw = scores_of(query_ref.at[mask], first, count, keys)
        scores = []
        for step in range(parts):
            scores.append(raw[:, step * length : step * length + safe])
            if safe < length:
                bias = bias_ref[:1, step * whole + offset + safe : step * whole + offset + length]
                scores.append(raw[:, step * length + safe : (step + 1) * length] + bias)
        scores = jnp.concatenate([part for part in scores if part.shape[1]], axis=1)
        heads = [slice((first + j) * DH, (first + j + 1) * DH) for j in range(count)]
        level = jnp.concatenate(
            [
                jnp.broadcast_to(level_ref[at, :, first + j : first + j + 1], (q_rows, DH))
                for j in range(count)
            ],
            axis=0,
        )
        mean = jnp.concatenate([mean_ref[at, :, columns] for columns in heads], axis=0)
        top = jnp.maximum(jnp.max(scores, axis=1, keepdims=True) * COEF, level)
        tops = jnp.concatenate([top] * (parts * length // DH), axis=1)
        weights = jnp.exp2(scores * COEF - tops)
        old = jnp.exp2(level - top)
        summed = jnp.dot(
            weights.astype(jnp.bfloat16), values, preferred_element_type=jnp.float32
        )
        total = summed[:, DH:] + old
        result = (summed[:, :DH] + mean.astype(jnp.float32) * old) / total
        for j, columns in enumerate(heads):
            part = slice(j * q_rows, (j + 1) * q_rows)
            rounded = result[part].astype(jnp.bfloat16)
            if mode == "write":
                done_ref[0, :, columns] = rounded
            else:
                new_mean_ref[0, :, columns] = rounded
            if mode == "state":
                levels = jnp.where(lanes == first + j, (top + jnp.log2(total))[part], levels)
        if mode == "write":
            head = jnp.bitwise_xor(own_head, mask)
            copies.append(
                pltpu.make_async_copy(
                    done_ref.at[0, :, first * DH : (first + count) * DH],
                    out_ref.at[:, columns_from(head * GROUP + first, count)],
                    sems.at[first // count],
                )
            )
            copies[-1].start()
        if mode == "write" and first == 0:
            for place, other in enumerate(waiting):
                done_ref[1 + place] = refs[place][0]
                head = jnp.bitwise_xor(own_head, other)
                copies.append(
                    pltpu.make_async_copy(
                        done_ref.at[1 + place],
                        out_ref.at[:, columns_from(head * GROUP, GROUP)],
                        sems.at[GROUP * q_rows // ROWS + place],
                    )
                )
                copies[-1].start()
    for copy in copies:
        copy.wait()
    if mode == "state":
        refs[1][0] = levels


def attend_prefix(held, query, state, bias, mask, mode, offset=0, waiting=()):
    _, q_rows, wide = query.shape
    groups = [held[at] for at in sorted(held) if at % KVH == mask]
    parts = len(groups)
    pieces = [piece for group in groups for piece in group]
    length = len(pieces) * pieces[0].shape[0] * pieces[0].shape[1]
    at = mask if state[0].shape[0] == KVH else 0
    mean_shape = pltpu.VMEM((1, q_rows, wide), jnp.bfloat16)
    scratch = []
    if mode == "write":
        out_specs = ANY
        out_shape = jax.ShapeDtypeStruct((q_rows, KVH * wide), jnp.bfloat16)
        scratch = [
            pltpu.VMEM((1 + len(waiting), q_rows, wide), jnp.bfloat16),
            pltpu.SemaphoreType.DMA((GROUP * q_rows // ROWS + len(waiting),)),
        ]
    elif mode == "mean":
        out_specs, out_shape = VMEM, mean_shape
    else:
        out_specs = [VMEM, VMEM]
        out_shape = [mean_shape, pltpu.VMEM((1, q_rows, DH), jnp.float32)]
    operands = [query, *state, bias, *[result for _, result in waiting]]
    operands = [*pieces, *[in_vmem(array) for array in operands]]
    masks = [other for other, _ in waiting]
    return pl.pallas_call(
        functools.partial(prefix_kernel, mask, at, parts, len(pieces), offset, mode, masks),
        in_specs=[VMEM] * len(operands),
        out_specs=out_specs,
        out_shape=out_shape,
        scratch_shapes=scratch,
        cost_estimate=pl.CostEstimate(
            flops=64 * q_rows * wide * length, bytes_accessed=2**20, transcendentals=0
        ),
        compiler_params=pltpu.CompilerParams(vmem_limit_bytes=48 * 2**20),
        name="attend_prefix",
    )(*operands)


def swap(array, blks, mask):
    return lax.ppermute(array, "blk", [(i, i ^ mask) for i in range(blks)])


def per_device(queries, span_kv, kv_store, page_ids, page_owner, prefix_len):
    pools = lax.axis_size("pool")
    blks = lax.axis_size("blk")
    stored, page, _ = kv_store.shape
    parts = blks // KVH
    rows = page // parts

    owner = lax.broadcasted_iota(jnp.int32, (pools, 1, page_ids.shape[1]), 0)
    wanted = jnp.where(page_owner[None] == owner, page_ids[None], -1)
    tables = lax.all_to_all(wanted, "pool", split_axis=0, concat_axis=0, tiled=True)
    picked = pick_pages(tables, kv_store, rows)
    picked, span_kv = lax.optimization_barrier((picked, span_kv))
    fetched = lax.all_to_all(picked, "pool", split_axis=0, concat_axis=0, tiled=True)
    span = {0: span_kv}
    bit = blks // 2
    while bit:
        span.update({mask ^ bit: swap(rows_of, blks, bit) for mask, rows_of in list(span.items())})
        bit //= 2
    length = page_ids.shape[1] * page
    state = attend_span(prefix_len, queries, span, length, parts, rows)
    fetched, *state = lax.optimization_barrier((fetched, *state))
    mean, level, query, bias = state
    state = (mean, level)
    first, second = order_pages(page_owner, fetched)

    def across(piece):
        held = {0: [piece]}
        bit = blks // 2
        while bit > 1:
            held.update(
                {mask ^ bit: [swap(part[0], blks, bit)] for mask, part in list(held.items())}
            )
            bit //= 2
        return {mask: part for mask, part in held.items() if mask % KVH == 2}

    def relayed(held):
        return {mask ^ 1: [swap(part, blks, 1) for part in parts] for mask, parts in held.items()}

    near = {0: [first, second]}
    for mask in range(KVH, blks, KVH):
        near[mask] = [swap(first, blks, mask), swap(second, blks, mask)]
    near.update(relayed(near))
    attend = functools.partial(attend_prefix, query=query, bias=bias)
    far = across(first)
    own = attend(near, state=state, mask=0, mode="mean")
    second, own = lax.optimization_barrier((second, own))
    rest = across(second)
    other = attend(near, state=state, mask=1, mode="mean")
    own, other, far = lax.optimization_barrier((own, other, far))
    far.update(relayed(far))
    states = [attend(far, state=state, mask=mask, mode="state") for mask in (2, 3)]
    states, rest = lax.optimization_barrier((states, rest))
    rest.update(relayed(rest))
    offset = first.shape[0] * first.shape[1]
    done = attend(rest, state=states[0], mask=2, mode="mean", offset=offset)
    return attend(
        rest,
        state=states[1],
        mask=3,
        mode="write",
        offset=offset,
        waiting=((0, own), (1, other), (2, done)),
    )


def solution(mesh):
    in_specs = (
        P(("pool", "blk"), None),
        P(("pool", "blk"), None),
        P("pool", None, None),
        P("pool", None),
        P("pool", None),
        P("pool"),
    )
    out_specs = P(("pool", "blk"), None)
    return jax.shard_map(
        per_device, mesh=mesh, in_specs=in_specs, out_specs=out_specs, check_vma=False
    )
```

```python
import functools
import math

import jax
import jax.numpy as jnp
from jax import lax
from jax.experimental import pallas as pl
from jax.experimental.pallas import tpu as pltpu
from jax.sharding import PartitionSpec as P

KVH = 4
DH = 128
GROUP = 8
CAP = 2
COEF = math.log2(math.e) / math.sqrt(DH)
LOW = -1e30
ROWS = 256
LOADS = 4


SMEM = pl.BlockSpec(memory_space=pltpu.SMEM)
VMEM = pl.BlockSpec(memory_space=pltpu.VMEM)
ANY = pl.BlockSpec(memory_space=pl.ANY)


def columns_from(first, count):
    return pl.ds(pl.multiple_of(first * DH, DH), count * DH)


def pick_kernel(tables_ref, store_ref, out_ref, table, own, load_sems, sems):
    pools, _, listed = tables_ref.shape
    stored, rows, _ = own.shape
    blk = lax.axis_index("blk")
    head = lax.rem(blk, KVH)
    at_rows = pl.ds(pl.multiple_of(lax.div(blk, KVH) * rows, rows), rows)
    loads = [pltpu.make_async_copy(tables_ref, table, load_sems.at[0])]
    for kind in range(2):
        for first in range(0, stored, stored // LOADS):
            pages = slice(first, first + stored // LOADS)
            loads.append(
                pltpu.make_async_copy(
                    store_ref.at[pages, at_rows, columns_from(kind * KVH + head, 1)],
                    own.at[pages, :, kind * DH : (kind + 1) * DH],
                    load_sems.at[len(loads)],
                )
            )
    for load in loads:
        load.start()
    for load in loads:
        load.wait()

    def page_copy(request, slot, page):
        return pltpu.make_async_copy(
            own.at[page], out_ref.at[request, slot], sems.at[request, slot]
        )

    def serve(request, carry):
        def visit(entry, state):
            rank, pages = state
            page = table[request, 0, entry]
            hit = page >= 0
            pages = [jnp.where(hit & (rank == slot), page, pages[slot]) for slot in range(CAP)]
            return rank + hit.astype(jnp.int32), pages

        state = (jnp.int32(0), [jnp.int32(0)] * CAP)
        _, pages = lax.fori_loop(0, listed, visit, state, unroll=listed <= 8)
        for slot in range(CAP):
            page_copy(request, slot, pages[slot]).start()
        return carry

    lax.fori_loop(0, pools, serve, 0)

    def finish(request, carry):
        for slot in range(CAP):
            page_copy(request, slot, 0).wait()
        return carry

    lax.fori_loop(0, pools, finish, 0)


def pick_pages(tables, kv_store, rows):
    pools = tables.shape[0]
    return pl.pallas_call(
        pick_kernel,
        in_specs=[ANY, ANY],
        out_specs=ANY,
        out_shape=pltpu.HBM((pools, CAP, rows, 2 * DH), kv_store.dtype),
        scratch_shapes=[
            pltpu.SMEM(tables.shape, jnp.int32),
            pltpu.VMEM((kv_store.shape[0], rows, 2 * DH), kv_store.dtype),
            pltpu.SemaphoreType.DMA((1 + 2 * LOADS,)),
            pltpu.SemaphoreType.DMA((pools, CAP)),
        ],
        name="pick_pages",
    )(in_vmem(tables), in_hbm(kv_store))


def in_hbm(array):
    return pltpu.with_memory_space_constraint(array, pltpu.HBM)


def in_vmem(array):
    return pltpu.with_memory_space_constraint(array, pltpu.VMEM)


def order_kernel(owners_ref, fetched_ref, first_ref, second_ref):
    half = first_ref.shape[0]
    for entry in range(2 * half):
        owner = owners_ref[0, entry]
        rank = jnp.int32(0)
        for earlier in range(entry):
            rank += (owners_ref[0, earlier] == owner).astype(jnp.int32)
        half_ref = first_ref if entry < half else second_ref
        half_ref[entry % half] = fetched_ref[owner, jnp.minimum(rank, CAP - 1)]


def order_pages(owners, fetched):
    shape = (owners.shape[1] // 2, fetched.shape[2], 2 * DH)
    return pl.pallas_call(
        order_kernel,
        in_specs=[SMEM, VMEM],
        out_specs=[VMEM] * 2,
        out_shape=[pltpu.VMEM(shape, fetched.dtype)] * 2,
        name="order_pages",
    )(owners, in_vmem(fetched))


def scores_of(query_ref, first, count, keys):
    heads = [query_ref[:, (first + j) * DH : (first + j + 1) * DH] for j in range(count)]
    stacked = heads[0] if count == 1 else jnp.concatenate(heads, axis=0)
    return lax.dot_general(
        stacked, keys, (((1,), (1,)), ((), ())), preferred_element_type=jnp.float32
    )


def with_ones(values):
    return jnp.concatenate([values, jnp.ones((values.shape[0], DH), values.dtype)], axis=1)


def span_kernel(masks, parts, rows, limit_ref, query_ref, *refs):
    blocks = len(masks)
    keys_refs, values_refs = refs[:blocks], refs[blocks : 2 * blocks]
    mean_ref, level_ref, copy_ref, bias_ref = refs[2 * blocks :]
    q_rows = query_ref.shape[0]
    count = ROWS // q_rows
    copy_ref[0] = query_ref[...]
    own = lax.axis_index("blk")
    shape = (bias_ref.shape[0], bias_ref.shape[1] // parts)
    index = lax.broadcasted_iota(jnp.int32, shape, 1)
    at_page = lax.div(index, rows) * (parts * rows) + lax.rem(index, rows)
    for step in range(parts):
        position = at_page + lax.rem(lax.div(own, KVH) + step, parts) * rows
        bias_ref[:, step * shape[1] : (step + 1) * shape[1]] = jnp.where(
            position < limit_ref[0], 0.0, LOW
        )
    keys = jnp.concatenate([ref[...] for ref in keys_refs], axis=0)
    values = with_ones(jnp.concatenate([ref[...] for ref in values_refs], axis=0))
    ahead = lax.broadcasted_iota(jnp.int32, (q_rows, q_rows), 0) - lax.broadcasted_iota(
        jnp.int32, (q_rows, q_rows), 1
    )
    bias = [
        jnp.where(ahead >= (jnp.bitwise_xor(own, mask) - own) * q_rows, 0.0, LOW) for mask in masks
    ]
    bias = jnp.concatenate(bias, axis=1)
    bias = jnp.concatenate([bias] * count, axis=0)
    lanes = lax.broadcasted_iota(jnp.int32, (q_rows, DH), 1)
    levels = jnp.zeros((q_rows, DH), jnp.float32)
    for first in range(0, GROUP, count):
        scores = scores_of(query_ref, first, count, keys) + bias
        top = jnp.max(scores, axis=1, keepdims=True)
        weights = jnp.exp2((scores - top) * COEF)
        summed = jnp.dot(
            weights.astype(jnp.bfloat16), values, preferred_element_type=jnp.float32
        )
        total = summed[:, DH:]
        level = top * COEF + jnp.log2(total)
        mean = summed[:, :DH] / total
        for j in range(count):
            at = slice(j * q_rows, (j + 1) * q_rows)
            columns = slice((first + j) * DH, (first + j + 1) * DH)
            mean_ref[0, :, columns] = mean[at].astype(jnp.bfloat16)
            levels = jnp.where(lanes == first + j, level[at], levels)
    level_ref[0] = levels


def attend_span(limit, queries, span, length, parts, rows):
    q_rows = queries.shape[0]
    masks = sorted(span)
    blocks = [span[mask] for mask in masks]
    wide = GROUP * DH

    def head(m):
        return lax.rem(lax.axis_index("blk"), KVH) ^ m

    keys_spec = pl.BlockSpec((q_rows, DH), lambda m: (0, head(m)))
    values_spec = pl.BlockSpec((q_rows, DH), lambda m: (0, KVH + head(m)))
    return pl.pallas_call(
        functools.partial(span_kernel, masks, parts, rows),
        grid=(KVH,),
        in_specs=[SMEM, pl.BlockSpec((q_rows, wide), lambda m: (0, head(m)))]
        + [keys_spec] * len(masks)
        + [values_spec] * len(masks),
        out_specs=[
            pl.BlockSpec((1, q_rows, wide), lambda m: (m, 0, 0)),
            pl.BlockSpec((1, q_rows, DH), lambda m: (m, 0, 0)),
            pl.BlockSpec((1, q_rows, wide), lambda m: (m, 0, 0)),
            pl.BlockSpec((8, length), lambda m: (0, 0)),
        ],
        out_shape=[
            pltpu.VMEM((KVH, q_rows, wide), jnp.bfloat16),
            pltpu.VMEM((KVH, q_rows, DH), jnp.float32),
            pltpu.VMEM((KVH, q_rows, wide), jnp.bfloat16),
            pltpu.VMEM((8, length), jnp.float32),
        ],
        cost_estimate=pl.CostEstimate(
            flops=4 * q_rows * KVH * wide * q_rows * len(masks),
            bytes_accessed=8 * 2**20,
            transcendentals=0,
        ),
        compiler_params=pltpu.CompilerParams(vmem_limit_bytes=48 * 2**20),
        name="attend_span",
    )(limit, in_hbm(queries), *blocks, *blocks)


def prefix_kernel(mask, at, parts, count_in, offset, mode, waiting, *refs):
    pieces = refs[:count_in]
    query_ref, mean_ref, level_ref, bias_ref, *refs = refs[count_in:]
    q_rows = query_ref.shape[1]
    count = ROWS // q_rows
    pages, rows, _ = pieces[0].shape
    length = count_in // parts * pages * rows
    both = [piece[...].reshape(pages * rows, 2 * DH) for piece in pieces]
    both = both[0] if count_in == 1 else jnp.concatenate(both, axis=0)
    keys = both[:, :DH]
    values = with_ones(both[:, DH:])
    own_head = lax.rem(lax.axis_index("blk"), KVH)
    copies = []
    if mode == "write":
        *_, out_ref, done_ref, sems = refs
    else:
        new_mean_ref = refs[0]
    whole = bias_ref.shape[1] // parts
    safe = min(max(whole * 5 // 8 // DH * DH - offset, 0), length)
    lanes = lax.broadcasted_iota(jnp.int32, (q_rows, DH), 1)
    levels = jnp.zeros((q_rows, DH), jnp.float32)
    for first in range(0, GROUP, count):
        raw = scores_of(query_ref.at[mask], first, count, keys)
        scores = []
        for step in range(parts):
            scores.append(raw[:, step * length : step * length + safe])
            if safe < length:
                bias = bias_ref[:1, step * whole + offset + safe : step * whole + offset + length]
                scores.append(raw[:, step * length + safe : (step + 1) * length] + bias)
        scores = jnp.concatenate([part for part in scores if part.shape[1]], axis=1)
        heads = [slice((first + j) * DH, (first + j + 1) * DH) for j in range(count)]
        level = jnp.concatenate(
            [
                jnp.broadcast_to(level_ref[at, :, first + j : first + j + 1], (q_rows, DH))
                for j in range(count)
            ],
            axis=0,
        )
        mean = jnp.concatenate([mean_ref[at, :, columns] for columns in heads], axis=0)
        top = jnp.maximum(jnp.max(scores, axis=1, keepdims=True) * COEF, level)
        tops = jnp.concatenate([top] * (parts * length // DH), axis=1)
        weights = jnp.exp2(scores * COEF - tops)
        old = jnp.exp2(level - top)
        summed = jnp.dot(
            weights.astype(jnp.bfloat16), values, preferred_element_type=jnp.float32
        )
        total = summed[:, DH:] + old
        result = (summed[:, :DH] + mean.astype(jnp.float32) * old) / total
        for j, columns in enumerate(heads):
            part = slice(j * q_rows, (j + 1) * q_rows)
            rounded = result[part].astype(jnp.bfloat16)
            if mode == "write":
                done_ref[0, :, columns] = rounded
            else:
                new_mean_ref[0, :, columns] = rounded
            if mode == "state":
                levels = jnp.where(lanes == first + j, (top + jnp.log2(total))[part], levels)
        if mode == "write":
            head = jnp.bitwise_xor(own_head, mask)
            copies.append(
                pltpu.make_async_copy(
                    done_ref.at[0, :, first * DH : (first + count) * DH],
                    out_ref.at[:, columns_from(head * GROUP + first, count)],
                    sems.at[first // count],
                )
            )
            copies[-1].start()
        if mode == "write" and first == 0:
            for place, other in enumerate(waiting):
                done_ref[1 + place] = refs[place][0]
                head = jnp.bitwise_xor(own_head, other)
                copies.append(
                    pltpu.make_async_copy(
                        done_ref.at[1 + place],
                        out_ref.at[:, columns_from(head * GROUP, GROUP)],
                        sems.at[GROUP * q_rows // ROWS + place],
                    )
                )
                copies[-1].start()
    for copy in copies:
        copy.wait()
    if mode == "state":
        refs[1][0] = levels


def attend_prefix(held, query, state, bias, mask, mode, offset=0, waiting=(), partial=()):
    _, q_rows, wide = query.shape
    groups = [held[at] for at in sorted(held) if at % KVH == mask]
    parts = len(groups)
    pieces = [piece for group in groups for piece in group]
    length = len(pieces) * pieces[0].shape[0] * pieces[0].shape[1]
    at = mask if state[0].shape[0] == KVH else 0
    mean_shape = pltpu.VMEM((1, q_rows, wide), jnp.bfloat16)
    scratch = []
    if mode == "write":
        out_specs = ANY
        out_shape = jax.ShapeDtypeStruct((q_rows, KVH * wide), jnp.bfloat16)
        scratch = [
            pltpu.VMEM((1 + len(waiting), q_rows, wide), jnp.bfloat16),
            pltpu.SemaphoreType.DMA((GROUP * q_rows // ROWS + len(waiting),)),
        ]
    elif mode == "mean":
        out_specs, out_shape = VMEM, mean_shape
    else:
        out_specs = [VMEM, VMEM]
        out_shape = [mean_shape, pltpu.VMEM((1, q_rows, DH), jnp.float32)]
    operands = [query, *state, bias, *[result for _, result in waiting]]
    operands = [*pieces, *[in_vmem(array) for array in operands]]
    masks = [other for other, _ in waiting]
    return pl.pallas_call(
        functools.partial(prefix_kernel, mask, at, parts, len(pieces), offset, mode, masks),
        in_specs=[VMEM] * len(operands) + [ANY] * len(partial),
        out_specs=out_specs,
        out_shape=out_shape,
        scratch_shapes=scratch,
        input_output_aliases={len(operands): 0} if partial else {},
        cost_estimate=pl.CostEstimate(
            flops=64 * q_rows * wide * length, bytes_accessed=2**20, transcendentals=0
        ),
        compiler_params=pltpu.CompilerParams(vmem_limit_bytes=48 * 2**20),
        name="attend_prefix",
    )(*operands, *partial)


def swap(array, blks, mask):
    return lax.ppermute(array, "blk", [(i, i ^ mask) for i in range(blks)])


def per_device(queries, span_kv, kv_store, page_ids, page_owner, prefix_len):
    pools = lax.axis_size("pool")
    blks = lax.axis_size("blk")
    stored, page, _ = kv_store.shape
    parts = blks // KVH
    rows = page // parts

    owner = lax.broadcasted_iota(jnp.int32, (pools, 1, page_ids.shape[1]), 0)
    wanted = jnp.where(page_owner[None] == owner, page_ids[None], -1)
    tables = lax.all_to_all(wanted, "pool", split_axis=0, concat_axis=0, tiled=True)
    picked = pick_pages(tables, kv_store, rows)
    picked, span_kv = lax.optimization_barrier((picked, span_kv))
    fetched = lax.all_to_all(picked, "pool", split_axis=0, concat_axis=0, tiled=True)
    span = {0: span_kv}
    bit = blks // 2
    while bit:
        span.update({mask ^ bit: swap(rows_of, blks, bit) for mask, rows_of in list(span.items())})
        bit //= 2
    length = page_ids.shape[1] * page
    state = attend_span(prefix_len, queries, span, length, parts, rows)
    fetched, *state = lax.optimization_barrier((fetched, *state))
    mean, level, query, bias = state
    state = (mean, level)
    first, second = order_pages(page_owner, fetched)

    def across(piece):
        held = {0: [piece]}
        bit = blks // 2
        while bit > 1:
            held.update(
                {mask ^ bit: [swap(part[0], blks, bit)] for mask, part in list(held.items())}
            )
            bit //= 2
        return {mask: part for mask, part in held.items() if mask % KVH == 2}

    def relayed(held):
        return {mask ^ 1: [swap(part, blks, 1) for part in parts] for mask, parts in held.items()}

    near = {0: [first, second]}
    for mask in range(KVH, blks, KVH):
        near[mask] = [swap(first, blks, mask), swap(second, blks, mask)]
    near.update(relayed(near))
    attend = functools.partial(attend_prefix, query=query, bias=bias)
    far = across(first)
    own = attend(near, state=state, mask=0, mode="mean")
    second, own = lax.optimization_barrier((second, own))
    rest = across(second)
    out = attend(near, state=state, mask=1, mode="write", waiting=((0, own),))
    out, far = lax.optimization_barrier((out, far))
    far.update(relayed(far))
    states = [attend(far, state=state, mask=mask, mode="state") for mask in (2, 3)]
    states, rest = lax.optimization_barrier((states, rest))
    rest.update(relayed(rest))
    offset = first.shape[0] * first.shape[1]
    done = attend(rest, state=states[0], mask=2, mode="mean", offset=offset)
    return attend(
        rest,
        state=states[1],
        mask=3,
        mode="write",
        offset=offset,
        waiting=((2, done),),
        partial=[out],
    )


def solution(mesh):
    in_specs = (
        P(("pool", "blk"), None),
        P(("pool", "blk"), None),
        P("pool", None, None),
        P("pool", None),
        P("pool", None),
        P("pool"),
    )
    out_specs = P(("pool", "blk"), None)
    return jax.shard_map(
        per_device, mesh=mesh, in_specs=in_specs, out_specs=out_specs, check_vma=False
    )
```

```python
import functools
import math

import jax
import jax.numpy as jnp
from jax import lax
from jax.experimental import pallas as pl
from jax.experimental.pallas import tpu as pltpu
from jax.sharding import PartitionSpec as P

KVH = 4
DH = 128
GROUP = 8
CAP = 2
COEF = math.log2(math.e) / math.sqrt(DH)
LOW = -1e30
ROWS = 256
LOADS = 2


SMEM = pl.BlockSpec(memory_space=pltpu.SMEM)
VMEM = pl.BlockSpec(memory_space=pltpu.VMEM)
ANY = pl.BlockSpec(memory_space=pl.ANY)


def columns_from(first, count):
    return pl.ds(pl.multiple_of(first * DH, DH), count * DH)


def pick_kernel(tables_ref, store_ref, out_ref, table, own, load_sems, sems):
    pools, _, listed = tables_ref.shape
    stored, rows, _ = own.shape
    blk = lax.axis_index("blk")
    head = lax.rem(blk, KVH)
    at_rows = pl.ds(pl.multiple_of(lax.div(blk, KVH) * rows, rows), rows)
    loads = [pltpu.make_async_copy(tables_ref, table, load_sems.at[0])]
    for kind in range(2):
        for first in range(0, stored, stored // LOADS):
            pages = slice(first, first + stored // LOADS)
            loads.append(
                pltpu.make_async_copy(
                    store_ref.at[pages, at_rows, columns_from(kind * KVH + head, 1)],
                    own.at[pages, :, kind * DH : (kind + 1) * DH],
                    load_sems.at[len(loads)],
                )
            )
    for load in loads:
        load.start()
    for load in loads:
        load.wait()

    def page_copy(request, slot, page):
        return pltpu.make_async_copy(
            own.at[page], out_ref.at[request, slot], sems.at[request, slot]
        )

    def serve(request, carry):
        def visit(entry, state):
            rank, pages = state
            page = table[request, 0, entry]
            hit = page >= 0
            pages = [jnp.where(hit & (rank == slot), page, pages[slot]) for slot in range(CAP)]
            return rank + hit.astype(jnp.int32), pages

        state = (jnp.int32(0), [jnp.int32(0)] * CAP)
        _, pages = lax.fori_loop(0, listed, visit, state, unroll=listed <= 8)
        for slot in range(CAP):
            page_copy(request, slot, pages[slot]).start()
        return carry

    lax.fori_loop(0, pools, serve, 0)

    def finish(request, carry):
        for slot in range(CAP):
            page_copy(request, slot, 0).wait()
        return carry

    lax.fori_loop(0, pools, finish, 0)


def pick_pages(tables, kv_store, rows):
    pools = tables.shape[0]
    return pl.pallas_call(
        pick_kernel,
        in_specs=[ANY, ANY],
        out_specs=ANY,
        out_shape=pltpu.HBM((pools, CAP, rows, 2 * DH), kv_store.dtype),
        scratch_shapes=[
            pltpu.SMEM(tables.shape, jnp.int32),
            pltpu.VMEM((kv_store.shape[0], rows, 2 * DH), kv_store.dtype),
            pltpu.SemaphoreType.DMA((1 + 2 * LOADS,)),
            pltpu.SemaphoreType.DMA((pools, CAP)),
        ],
        name="pick_pages",
    )(in_vmem(tables), in_hbm(kv_store))


def in_hbm(array):
    return pltpu.with_memory_space_constraint(array, pltpu.HBM)


def in_vmem(array):
    return pltpu.with_memory_space_constraint(array, pltpu.VMEM)


def order_kernel(owners_ref, fetched_ref, first_ref, second_ref):
    half = first_ref.shape[0]
    for entry in range(2 * half):
        owner = owners_ref[0, entry]
        rank = jnp.int32(0)
        for earlier in range(entry):
            rank += (owners_ref[0, earlier] == owner).astype(jnp.int32)
        half_ref = first_ref if entry < half else second_ref
        half_ref[entry % half] = fetched_ref[owner, jnp.minimum(rank, CAP - 1)]


def order_pages(owners, fetched):
    shape = (owners.shape[1] // 2, fetched.shape[2], 2 * DH)
    return pl.pallas_call(
        order_kernel,
        in_specs=[SMEM, VMEM],
        out_specs=[VMEM] * 2,
        out_shape=[pltpu.VMEM(shape, fetched.dtype)] * 2,
        name="order_pages",
    )(owners, in_vmem(fetched))


def scores_of(query_ref, first, count, keys):
    heads = [query_ref[:, (first + j) * DH : (first + j + 1) * DH] for j in range(count)]
    stacked = heads[0] if count == 1 else jnp.concatenate(heads, axis=0)
    return lax.dot_general(
        stacked, keys, (((1,), (1,)), ((), ())), preferred_element_type=jnp.float32
    )


def with_ones(values):
    return jnp.concatenate([values, jnp.ones((values.shape[0], DH), values.dtype)], axis=1)


def span_kernel(masks, parts, rows, limit_ref, query_ref, *refs):
    blocks = len(masks)
    keys_refs, values_refs = refs[:blocks], refs[blocks : 2 * blocks]
    mean_ref, level_ref, copy_ref, bias_ref = refs[2 * blocks :]
    q_rows = query_ref.shape[0]
    count = ROWS // q_rows
    copy_ref[0] = query_ref[...]
    own = lax.axis_index("blk")
    shape = (bias_ref.shape[0], bias_ref.shape[1] // parts)
    index = lax.broadcasted_iota(jnp.int32, shape, 1)
    at_page = lax.div(index, rows) * (parts * rows) + lax.rem(index, rows)
    for step in range(parts):
        position = at_page + lax.rem(lax.div(own, KVH) + step, parts) * rows
        bias_ref[:, step * shape[1] : (step + 1) * shape[1]] = jnp.where(
            position < limit_ref[0], 0.0, LOW
        )
    keys = jnp.concatenate([ref[...] for ref in keys_refs], axis=0)
    values = with_ones(jnp.concatenate([ref[...] for ref in values_refs], axis=0))
    ahead = lax.broadcasted_iota(jnp.int32, (q_rows, q_rows), 0) - lax.broadcasted_iota(
        jnp.int32, (q_rows, q_rows), 1
    )
    bias = [
        jnp.where(ahead >= (jnp.bitwise_xor(own, mask) - own) * q_rows, 0.0, LOW) for mask in masks
    ]
    bias = jnp.concatenate(bias, axis=1)
    bias = jnp.concatenate([bias] * count, axis=0)
    lanes = lax.broadcasted_iota(jnp.int32, (q_rows, DH), 1)
    levels = jnp.zeros((q_rows, DH), jnp.float32)
    for first in range(0, GROUP, count):
        scores = scores_of(query_ref, first, count, keys) + bias
        top = jnp.max(scores, axis=1, keepdims=True)
        weights = jnp.exp2((scores - top) * COEF)
        summed = jnp.dot(
            weights.astype(jnp.bfloat16), values, preferred_element_type=jnp.float32
        )
        total = summed[:, DH:]
        level = top * COEF + jnp.log2(total)
        mean = summed[:, :DH] / total
        for j in range(count):
            at = slice(j * q_rows, (j + 1) * q_rows)
            columns = slice((first + j) * DH, (first + j + 1) * DH)
            mean_ref[0, :, columns] = mean[at].astype(jnp.bfloat16)
            levels = jnp.where(lanes == first + j, level[at], levels)
    level_ref[0] = levels


def attend_span(limit, queries, span, length, parts, rows):
    q_rows = queries.shape[0]
    masks = sorted(span)
    blocks = [span[mask] for mask in masks]
    wide = GROUP * DH

    def head(m):
        return lax.rem(lax.axis_index("blk"), KVH) ^ m

    keys_spec = pl.BlockSpec((q_rows, DH), lambda m: (0, head(m)))
    values_spec = pl.BlockSpec((q_rows, DH), lambda m: (0, KVH + head(m)))
    return pl.pallas_call(
        functools.partial(span_kernel, masks, parts, rows),
        grid=(KVH,),
        in_specs=[SMEM, pl.BlockSpec((q_rows, wide), lambda m: (0, head(m)))]
        + [keys_spec] * len(masks)
        + [values_spec] * len(masks),
        out_specs=[
            pl.BlockSpec((1, q_rows, wide), lambda m: (m, 0, 0)),
            pl.BlockSpec((1, q_rows, DH), lambda m: (m, 0, 0)),
            pl.BlockSpec((1, q_rows, wide), lambda m: (m, 0, 0)),
            pl.BlockSpec((8, length), lambda m: (0, 0)),
        ],
        out_shape=[
            pltpu.VMEM((KVH, q_rows, wide), jnp.bfloat16),
            pltpu.VMEM((KVH, q_rows, DH), jnp.float32),
            pltpu.VMEM((KVH, q_rows, wide), jnp.bfloat16),
            pltpu.VMEM((8, length), jnp.float32),
        ],
        cost_estimate=pl.CostEstimate(
            flops=4 * q_rows * KVH * wide * q_rows * len(masks),
            bytes_accessed=8 * 2**20,
            transcendentals=0,
        ),
        compiler_params=pltpu.CompilerParams(vmem_limit_bytes=48 * 2**20),
        name="attend_span",
    )(limit, in_hbm(queries), *blocks, *blocks)


def prefix_kernel(mask, at, parts, count_in, offset, mode, waiting, *refs):
    pieces = refs[:count_in]
    query_ref, mean_ref, level_ref, bias_ref, *refs = refs[count_in:]
    q_rows = query_ref.shape[1]
    count = ROWS // q_rows
    pages, rows, _ = pieces[0].shape
    length = count_in // parts * pages * rows
    both = [piece[...].reshape(pages * rows, 2 * DH) for piece in pieces]
    both = both[0] if count_in == 1 else jnp.concatenate(both, axis=0)
    keys = both[:, :DH]
    values = with_ones(both[:, DH:])
    own_head = lax.rem(lax.axis_index("blk"), KVH)
    copies = []
    if mode == "write":
        *_, out_ref, done_ref, sems = refs
    else:
        new_mean_ref = refs[0]
    whole = bias_ref.shape[1] // parts
    safe = min(max(whole * 5 // 8 // DH * DH - offset, 0), length)
    lanes = lax.broadcasted_iota(jnp.int32, (q_rows, DH), 1)
    levels = jnp.zeros((q_rows, DH), jnp.float32)
    for first in range(0, GROUP, count):
        raw = scores_of(query_ref.at[mask], first, count, keys)
        scores = []
        for step in range(parts):
            scores.append(raw[:, step * length : step * length + safe])
            if safe < length:
                bias = bias_ref[:1, step * whole + offset + safe : step * whole + offset + length]
                scores.append(raw[:, step * length + safe : (step + 1) * length] + bias)
        scores = jnp.concatenate([part for part in scores if part.shape[1]], axis=1)
        heads = [slice((first + j) * DH, (first + j + 1) * DH) for j in range(count)]
        level = jnp.concatenate(
            [
                jnp.broadcast_to(level_ref[at, :, first + j : first + j + 1], (q_rows, DH))
                for j in range(count)
            ],
            axis=0,
        )
        mean = jnp.concatenate([mean_ref[at, :, columns] for columns in heads], axis=0)
        top = jnp.maximum(jnp.max(scores, axis=1, keepdims=True) * COEF, level)
        tops = jnp.concatenate([top] * (parts * length // DH), axis=1)
        weights = jnp.exp2(scores * COEF - tops)
        old = jnp.exp2(level - top)
        summed = jnp.dot(
            weights.astype(jnp.bfloat16), values, preferred_element_type=jnp.float32
        )
        total = summed[:, DH:] + old
        result = (summed[:, :DH] + mean.astype(jnp.float32) * old) / total
        for j, columns in enumerate(heads):
            part = slice(j * q_rows, (j + 1) * q_rows)
            rounded = result[part].astype(jnp.bfloat16)
            if mode == "write":
                done_ref[0, :, columns] = rounded
            else:
                new_mean_ref[0, :, columns] = rounded
            if mode == "state":
                levels = jnp.where(lanes == first + j, (top + jnp.log2(total))[part], levels)
        if mode == "write":
            head = jnp.bitwise_xor(own_head, mask)
            copies.append(
                pltpu.make_async_copy(
                    done_ref.at[0, :, first * DH : (first + count) * DH],
                    out_ref.at[:, columns_from(head * GROUP + first, count)],
                    sems.at[first // count],
                )
            )
            copies[-1].start()
        if mode == "write" and first == 0:
            for place, other in enumerate(waiting):
                done_ref[1 + place] = refs[place][0]
                head = jnp.bitwise_xor(own_head, other)
                copies.append(
                    pltpu.make_async_copy(
                        done_ref.at[1 + place],
                        out_ref.at[:, columns_from(head * GROUP, GROUP)],
                        sems.at[GROUP * q_rows // ROWS + place],
                    )
                )
                copies[-1].start()
    for copy in copies:
        copy.wait()
    if mode == "state":
        refs[1][0] = levels


def attend_prefix(held, query, state, bias, mask, mode, offset=0, waiting=(), partial=()):
    _, q_rows, wide = query.shape
    groups = [held[at] for at in sorted(held) if at % KVH == mask]
    parts = len(groups)
    pieces = [piece for group in groups for piece in group]
    length = len(pieces) * pieces[0].shape[0] * pieces[0].shape[1]
    at = mask if state[0].shape[0] == KVH else 0
    mean_shape = pltpu.VMEM((1, q_rows, wide), jnp.bfloat16)
    scratch = []
    if mode == "write":
        out_specs = ANY
        out_shape = jax.ShapeDtypeStruct((q_rows, KVH * wide), jnp.bfloat16)
        scratch = [
            pltpu.VMEM((1 + len(waiting), q_rows, wide), jnp.bfloat16),
            pltpu.SemaphoreType.DMA((GROUP * q_rows // ROWS + len(waiting),)),
        ]
    elif mode == "mean":
        out_specs, out_shape = VMEM, mean_shape
    else:
        out_specs = [VMEM, VMEM]
        out_shape = [mean_shape, pltpu.VMEM((1, q_rows, DH), jnp.float32)]
    operands = [query, *state, bias, *[result for _, result in waiting]]
    operands = [*pieces, *[in_vmem(array) for array in operands]]
    masks = [other for other, _ in waiting]
    return pl.pallas_call(
        functools.partial(prefix_kernel, mask, at, parts, len(pieces), offset, mode, masks),
        in_specs=[VMEM] * len(operands) + [ANY] * len(partial),
        out_specs=out_specs,
        out_shape=out_shape,
        scratch_shapes=scratch,
        input_output_aliases={len(operands): 0} if partial else {},
        cost_estimate=pl.CostEstimate(
            flops=64 * q_rows * wide * length, bytes_accessed=2**20, transcendentals=0
        ),
        compiler_params=pltpu.CompilerParams(vmem_limit_bytes=48 * 2**20),
        name="attend_prefix",
    )(*operands, *partial)


def swap(array, blks, mask):
    return lax.ppermute(array, "blk", [(i, i ^ mask) for i in range(blks)])


def per_device(queries, span_kv, kv_store, page_ids, page_owner, prefix_len):
    pools = lax.axis_size("pool")
    blks = lax.axis_size("blk")
    stored, page, _ = kv_store.shape
    parts = blks // KVH
    rows = page // parts

    owner = lax.broadcasted_iota(jnp.int32, (pools, 1, page_ids.shape[1]), 0)
    wanted = jnp.where(page_owner[None] == owner, page_ids[None], -1)
    tables = lax.all_to_all(wanted, "pool", split_axis=0, concat_axis=0, tiled=True)
    picked = pick_pages(tables, kv_store, rows)
    picked, span_kv = lax.optimization_barrier((picked, span_kv))
    fetched = lax.all_to_all(picked, "pool", split_axis=0, concat_axis=0, tiled=True)
    span = {0: span_kv}
    bit = blks // 2
    while bit:
        span.update({mask ^ bit: swap(rows_of, blks, bit) for mask, rows_of in list(span.items())})
        bit //= 2
    length = page_ids.shape[1] * page
    state = attend_span(prefix_len, queries, span, length, parts, rows)
    fetched, *state = lax.optimization_barrier((fetched, *state))
    mean, level, query, bias = state
    state = (mean, level)
    first, second = order_pages(page_owner, fetched)

    def across(piece):
        held = {0: [piece]}
        bit = blks // 2
        while bit > 1:
            held.update(
                {mask ^ bit: [swap(part[0], blks, bit)] for mask, part in list(held.items())}
            )
            bit //= 2
        return {mask: part for mask, part in held.items() if mask % KVH == 2}

    def relayed(held):
        return {mask ^ 1: [swap(part, blks, 1) for part in parts] for mask, parts in held.items()}

    near = {0: [first, second]}
    for mask in range(KVH, blks, KVH):
        near[mask] = [swap(first, blks, mask), swap(second, blks, mask)]
    near.update(relayed(near))
    attend = functools.partial(attend_prefix, query=query, bias=bias)
    far = across(first)
    own = attend(near, state=state, mask=0, mode="mean")
    second, own = lax.optimization_barrier((second, own))
    rest = across(second)
    out = attend(near, state=state, mask=1, mode="write", waiting=((0, own),))
    out, far = lax.optimization_barrier((out, far))
    far.update(relayed(far))
    states = [attend(far, state=state, mask=mask, mode="state") for mask in (2, 3)]
    states, rest = lax.optimization_barrier((states, rest))
    rest.update(relayed(rest))
    offset = first.shape[0] * first.shape[1]
    done = attend(rest, state=states[0], mask=2, mode="mean", offset=offset)
    return attend(
        rest,
        state=states[1],
        mask=3,
        mode="write",
        offset=offset,
        waiting=((2, done),),
        partial=[out],
    )


def solution(mesh):
    in_specs = (
        P(("pool", "blk"), None),
        P(("pool", "blk"), None),
        P("pool", None, None),
        P("pool", None),
        P("pool", None),
        P("pool"),
    )
    out_specs = P(("pool", "blk"), None)
    return jax.shard_map(
        per_device, mesh=mesh, in_specs=in_specs, out_specs=out_specs, check_vma=False
    )
```
